32 devices in a mesh: dp: 4 (over z), mp: 8 (over y, x, core).
Axes of the slice: x: 2, y: 2, z: 4, core: 2. Of those that a mesh axis runs over, the one named last changes fastest.
Arguments:
- inputs: bfloat16 [8, 1536, 2048], P('dp', 'mp'), may hold values from -6 to 6
- cotangent: bfloat16 [8, 1536, 2048], P('dp', 'mp'), may hold values from -12 to 12
- lengths: int32 [8, 8], P('dp'), may hold values from 1 to 1024, 1536 in all within a row
- w_query: float32 [2048, 2048], P('dp', 'mp'), may hold values from -0.125 to 0.125
- w_keyval: float32 [2048, 256], P('dp'), may hold values from -0.125 to 0.125
- w_out: float32 [2048, 2048], P('dp', 'mp'), may hold values from -0.5 to 0.5
- w_gate_up: float32 [2048, 2, 5632], P('dp', None, 'mp'), may hold values from -0.125 to 0.125
- w_down: float32 [2048, 5632], P('dp', 'mp'), may hold values from -0.078125 to 0.078125
- gains: float32 [2, 2048], replicated, may hold values from 0.35 to 3.3
- m_query: float32 [2048, 2048], P('dp', 'mp'), may hold values from -1330.215 to 1330.215
- m_keyval: float32 [2048, 256], P('dp'), may hold values from -5320.86 to 5320.86
- m_out: float32 [2048, 2048], P('dp', 'mp'), may hold values from -199.53226 to 199.53226
- m_gate_up: float32 [2048, 2, 5632], P('dp', None, 'mp'), may hold values from -199.53226 to 199.53226
- m_down: float32 [2048, 5632], P('dp', 'mp'), may hold values from -332.55374 to 332.55374
- m_gains: float32 [2, 2048], replicated, may hold values from -665.1075 to 665.1075
Outputs:
- output: bfloat16 [8, 1536, 2048], P('dp', 'mp')
- input_grad: bfloat16 [8, 1536, 2048], P('dp', 'mp')
- grad_query: float32 [2048, 2048], P('dp', 'mp')
- grad_keyval: float32 [2048, 256], P('dp')
- grad_out: float32 [2048, 2048], P('dp', 'mp')
- grad_gate_up: float32 [2048, 2, 5632], P('dp', None, 'mp')
- grad_down: float32 [2048, 5632], P('dp', 'mp')
- grad_gains: float32 [2, 2048], replicated
- moment_query: float32 [2048, 2048], P('dp', 'mp')
- moment_keyval: float32 [2048, 256], P('dp')
- moment_out: float32 [2048, 2048], P('dp', 'mp')
- moment_gate_up: float32 [2048, 2, 5632], P('dp', None, 'mp')
- moment_down: float32 [2048, 5632], P('dp', 'mp')
- moment_gains: float32 [2, 2048], replicated
- new_query: float32 [2048, 2048], P('dp', 'mp')
- new_keyval: float32 [2048, 256], P('dp')
- new_out: float32 [2048, 2048], P('dp', 'mp')
- new_gate_up: float32 [2048, 2, 5632], P('dp', None, 'mp')
- new_down: float32 [2048, 5632], P('dp', 'mp')
- new_gains: float32 [2, 2048], replicated
The draws below stay inside these ranges and needn't reach their ends.
Inputs may be any that keep to these rules, and one draw needn't show every extreme that they name: Each row holds 8 lengths that add up to 1536, the largest exactly 1024.
All inputs are finite; a program needn't handle non-finite values.
Results may differ from the reference program's by a relative error of at most 0.025.
Values may be sent and summed in bfloat16 or wider, within the bound.
No kernel may reach another device: no remote copies, remote signals or barrier semaphores. Data moves between devices by JAX's collectives and lax.ppermute only.
A program may use at most 384 MiB of HBM per device.

```python
import math
import jax
import jax.numpy as jnp
import numpy as np
from jax import lax

D = 2048
HEADS = 16
HD = 128
FF = 5632
FF_BLOCK = 352
SEQ = 1536
LONGEST = 1024
NDOC = 8
NS_ITERS = 5
BATCH = 8
TOKENS = 12288
N_MP = 8


def draw_cotangent(key, part):
    key = jax.random.fold_in(key, 7)
    batch_pos = jnp.arange(BATCH, dtype=jnp.float32)[:, None, None] / BATCH
    seq_pos = jnp.arange(SEQ, dtype=jnp.float32)[None, :, None] / SEQ
    width_pos = jnp.arange(D, dtype=jnp.float32)[None, None, :] / D
    rise = 3.0
    noise = jnp.clip(jax.random.normal(key, (BATCH, SEQ, D), jnp.float32), -4.0, 4.0)
    row_factor = jnp.power(rise, 0.5 * batch_pos + 0.5 * seq_pos - 0.5)
    col_factor = jnp.power(rise, width_pos - 0.5)
    return (noise * row_factor * col_factor).astype(jnp.bfloat16)


def draw_gains(key, part):
    key = jax.random.fold_in(key, 11)
    width_pos = jnp.arange(D, dtype=jnp.float32) / D
    base = 0.6 * jnp.power(3.0, width_pos)
    jitter = jax.random.uniform(key, (2, D), jnp.float32, 0.8, 1.2)
    return base[None, :] * jitter


def levels(own_key, extent, shards, smallest, top_value):
    def one(dim, blocks):
        heights = jax.random.uniform(jax.random.fold_in(jax.random.fold_in(own_key, 6), dim), (blocks,), jnp.float32, smallest / len(shards), top_value / len(shards))
        return jnp.repeat(jnp.exp(heights), extent[dim] // blocks).reshape((-1,) + (1,) * (len(extent) - dim - 1))

    gain = one(*shards[0])
    for cut in shards[1:]:
        gain = gain * one(*cut)
    return gain


def profile(amount, total, limit, skew):
    loads = [(1 << 20) // math.isqrt(rank ** skew) + 1 for rank in range(2, amount + 1)]
    rest, holding = total - limit - (amount - 1), [1] * (amount - 1)
    while rest > 0:
        candidates = [i for i in range(amount - 1) if holding[i] < limit]
        whole, left = sum([loads[i] for i in candidates]), rest
        for i in candidates:
            more = min(limit - holding[i], max(1, left * loads[i] // whole), rest)
            holding[i] = holding[i] + more
            rest = rest - more
    return np.array([limit] + holding)


def ragged_sizes(stream_key, amount, total, most, lean):
    if amount == 2:
        one = jax.random.randint(stream_key, (), max(1, total - most), min(most, total - 1) + 1)
        return jnp.stack([one, total - one])
    tallies = jnp.asarray(profile(amount, total, most, lean), jnp.int32)
    pairs = (amount - 1) // 2
    giver, taker = tallies[1:1 + 2 * pairs:2], tallies[2:2 + 2 * pairs:2]
    room = jnp.minimum(giver - 1, most - taker)
    moved = jax.random.randint(jax.random.fold_in(stream_key, 1), (pairs,), 0, 1 << 20) % (room + 1)
    tallies = tallies.at[1:1 + 2 * pairs:2].set(giver - moved).at[2:2 + 2 * pairs:2].set(taker + moved)
    return tallies[jax.random.permutation(jax.random.fold_in(stream_key, 2), amount)]


def centred(rng, dims, scale, most, shards=(), held_as=jnp.bfloat16):
    drawn = jax.random.normal(rng, dims, jnp.float32) * scale
    if len(shards) > 0:
        drawn = levels(rng, dims, shards, -0.22, 0.18) * drawn
    return jnp.clip(drawn, min=-most, max=most).astype(held_as)


def setup_inputs(seed: int = 0) -> dict:
    seeds = jax.random.split(jax.random.key(seed), 16)
    inputs = centred(seeds[0], (BATCH, SEQ, D), 1.0, 6.0, ((0, 4), (1, 8)))
    cotangent = draw_cotangent(jax.random.fold_in(seeds[15], 71), 0)
    lengths = jax.vmap(lambda own: ragged_sizes(own, NDOC, SEQ, LONGEST, 2))(jax.random.split(seeds[2], BATCH)).reshape((BATCH, NDOC)).astype(jnp.int32)
    w_query = centred(seeds[3], (D, HEADS * HD), D ** -0.5, 0.125, ((0, 4), (1, 8)), jnp.float32)
    w_keyval = centred(seeds[4], (D, 2 * HD), D ** -0.5, 0.125, ((0, 4),), jnp.float32)
    w_out = centred(seeds[5], (D, HEADS * HD), (HEADS * HD // 16) ** -0.5, 0.5, ((0, 4), (1, 8)), jnp.float32)
    w_gate_up = centred(seeds[6], (D, 2, FF), D ** -0.5, 0.125, ((0, 4), (2, 8)), jnp.float32)
    w_down = centred(seeds[7], (D, FF), FF ** -0.5, 0.078125, ((0, 4), (1, 8)), jnp.float32)
    gains = draw_gains(jax.random.fold_in(seeds[15], 71), 0)
    m_query = centred(seeds[9], (D, HEADS * HD), (2.0 * TOKENS ** 0.5), 1330.215, ((0, 4), (1, 8)), jnp.float32)
    m_keyval = centred(seeds[10], (D, 2 * HD), (8.0 * TOKENS ** 0.5), 5320.86, ((0, 4),), jnp.float32)
    m_out = centred(seeds[11], (D, HEADS * HD), (0.3 * TOKENS ** 0.5), 199.53226, ((0, 4), (1, 8)), jnp.float32)
    m_gate_up = centred(seeds[12], (D, 2, FF), (0.3 * TOKENS ** 0.5), 199.53226, ((0, 4), (2, 8)), jnp.float32)
    m_down = centred(seeds[13], (D, FF), (0.5 * TOKENS ** 0.5), 332.55374, ((0, 4), (1, 8)), jnp.float32)
    m_gains = centred(seeds[14], (2, D), (TOKENS ** 0.5), 665.1075, (), jnp.float32)
    return {"inputs": inputs, "cotangent": cotangent, "lengths": lengths, "w_query": w_query, "w_keyval": w_keyval, "w_out": w_out, "w_gate_up": w_gate_up, "w_down": w_down, "gains": gains, "m_query": m_query, "m_keyval": m_keyval, "m_out": m_out, "m_gate_up": m_gate_up, "m_down": m_down, "m_gains": m_gains}


@jax.custom_vjp
def low(v):
    return lax.optimization_barrier(v.astype(jnp.bfloat16)).astype(jnp.float32)

@jax.custom_vjp
def low_back(v):
    return v

def low_keep(v):
    return (low(v), None)

def low_pass(kept, grad):
    return (grad,)

def back_keep(v):
    return (v, None)

def back_low(kept, grad):
    return (low(grad),)
low.defvjp(low_keep, low_pass)
low_back.defvjp(back_keep, back_low)
EPS = 1e-05
THETA = 10000.0
NS_A = 3.4445
NS_B = -4.775
NS_C = 2.0315
MUON_RATE = 0.8
GAIN_RATE = 0.002
DECAY = 0.5
HIGH = lax.Precision.HIGHEST
MASKED = -1e+30

def doc_layout(doc_lengths, seq_len):
    ends = jnp.cumsum(doc_lengths).astype(jnp.int32)
    starts = (ends - doc_lengths).astype(jnp.int32)
    positions = jnp.arange(seq_len, dtype=jnp.int32)
    segment = lax.optimization_barrier(jnp.sum((positions[:, None] >= ends[None, :]).astype(jnp.int32), axis=1))
    member = (segment[:, None] == jnp.arange(doc_lengths.shape[0], dtype=jnp.int32)[None, :]).astype(jnp.int32)
    offset = positions - lax.optimization_barrier(jnp.sum(member * starts[None, :], axis=1))
    return (segment, offset)

def rotary_tables(offset, half_dim):
    freqs = jnp.power(THETA, -jnp.arange(half_dim, dtype=jnp.float32) / half_dim)
    angle = offset.astype(jnp.float32)[:, None] * freqs[None, :]
    return (jnp.cos(angle), jnp.sin(angle))

def rotate(vector, cosine, sine):
    half_dim = vector.shape[-1] // 2
    first_half = vector[..., :half_dim]
    second_half = vector[..., half_dim:]
    return jnp.concatenate([first_half * cosine - second_half * sine, second_half * cosine + first_half * sine], axis=-1)

def inverse_scale(vector):
    return lax.rsqrt(lax.optimization_barrier(jnp.mean(vector * vector, axis=-1, keepdims=True)) + EPS)

def matmul(left, right):
    return jnp.dot(left, right, precision=HIGH, preferred_element_type=jnp.float32)

def head_group(normed, w_query_g, w_out_g, key_rows, value_rows, cosine, sine, allowed):
    seq_len = normed.shape[0]
    shared = low_back(normed)
    queries = low_back(matmul(shared, w_query_g)).reshape(seq_len, -1, HD)
    queries = low(rotate(queries, cosine[:, None, :], sine[:, None, :]))
    scores = low_back(jnp.einsum('qhd,kd->hqk', queries, key_rows, precision=HIGH) * HD ** (-0.5))
    scores = jnp.where(allowed[None], scores, MASKED)
    attn_probs = low(jax.nn.softmax(scores, axis=-1))
    context = jnp.einsum('hqk,kd->qhd', attn_probs, value_rows, precision=HIGH)
    context = low(low_back(context)).reshape(seq_len, -1)
    return low(jnp.einsum('sf,df->sd', context, w_out_g, precision=HIGH))

def hidden_group(normed_mid, w_gate_g, w_up_g, w_down_g):
    shared = low_back(normed_mid)
    gate = low_back(matmul(shared, w_gate_g))
    upward = low_back(matmul(shared, w_up_g))
    hidden = low(jax.nn.silu(gate) * upward)
    return low(jnp.einsum('sf,df->sd', hidden, w_down_g, precision=HIGH))

def layer(weights, inputs, doc_lengths):
    w_query, w_keyval, w_out, w_gate_up, w_down, gains = weights
    seq_len = inputs.shape[0]
    segment, offset = doc_layout(doc_lengths, seq_len)
    cosine, sine = rotary_tables(offset, HD // 2)
    positions = jnp.arange(seq_len, dtype=jnp.int32)
    allowed = (segment[:, None] == segment[None, :]) & (positions[:, None] >= positions[None, :])
    normed = low(inputs * inverse_scale(inputs) * gains[0])
    keyval = low_back(matmul(normed, w_keyval))
    key_rows = low(rotate(keyval[:, :HD], cosine, sine))
    value_rows = low(keyval[:, HD:])
    group_cols = HEADS // N_MP * HD
    attn = jnp.zeros(inputs.shape, jnp.float32)
    for group in range(N_MP):
        cols = slice(group * group_cols, (group + 1) * group_cols)
        attn = attn + jax.checkpoint(head_group)(normed, w_query[:, cols], w_out[:, cols], key_rows, value_rows, cosine, sine, allowed)
    mid = inputs + low_back(attn)
    normed_mid = low(mid * inverse_scale(mid) * gains[1])
    group_units = FF // N_MP
    mlp = jnp.zeros(inputs.shape, jnp.float32)
    for group in range(N_MP):
        units = slice(group * group_units, (group + 1) * group_units)
        mlp = mlp + jax.checkpoint(hidden_group)(normed_mid, w_gate_up[:, 0, units], w_gate_up[:, 1, units], w_down[:, units])
    return mid + low_back(mlp)

def orthogonalize(moment, block_width):
    row_count = moment.shape[0]
    blocks = moment.reshape(row_count, -1, block_width)
    norms = jnp.sqrt(lax.optimization_barrier(jnp.sum(blocks * blocks, axis=(0, 2)))) + 1e-07
    current = blocks / norms[None, :, None]
    for iteration in range(NS_ITERS):
        gram = jnp.einsum('rnb,rnc->nbc', current, current, precision=HIGH)
        poly = NS_B * gram + NS_C * jnp.einsum('nab,nbc->nac', gram, gram, precision=HIGH)
        current = NS_A * current + jnp.einsum('rnb,nbc->rnc', current, poly, precision=HIGH)
    return current.reshape(moment.shape)

def reference(inputs, cotangent, lengths, w_query, w_keyval, w_out, w_gate_up, w_down, gains, m_query, m_keyval, m_out, m_gate_up, m_down, m_gains):
    params = (w_query, w_keyval, w_out, w_gate_up, w_down, gains)

    def forward(weights, activations):
        rounded = (low(weights[0]), low(weights[1]), low(weights[2]), low(weights[3]), low(weights[4]), weights[5])

        def one_batch(carry, item):
            return (carry, layer(rounded, item[0], item[1]))
        unused, result = lax.scan(one_batch, jnp.zeros((), jnp.float32), (activations, lengths))
        return result
    activations = inputs.astype(jnp.float32)
    result, pull = jax.vjp(forward, params, activations)
    grads, input_grad = pull(cotangent.astype(jnp.float32))
    olds = (m_query, m_keyval, m_out, m_gate_up, m_down)
    widths_list = (HD, 2 * HD, HD, FF_BLOCK, FF_BLOCK)
    moments = [DECAY * old + grad_item for old, grad_item in zip(olds, grads[:5])]
    news = [weight - MUON_RATE * orthogonalize(moment, block_width) for weight, moment, block_width in zip(params[:5], moments, widths_list)]
    moment_gains = DECAY * m_gains + grads[5]
    new_gains = gains - GAIN_RATE * moment_gains
    return (result.astype(jnp.bfloat16), input_grad.astype(jnp.bfloat16), grads[0], grads[1], grads[2], grads[3], grads[4], grads[5], moments[0], moments[1], moments[2], moments[3], moments[4], moment_gains, news[0], news[1], news[2], news[3], news[4], new_gains)
```

```python
import functools

import jax
import jax.numpy as jnp
from jax import lax
from jax.experimental import pallas as pl
from jax.experimental.pallas import tpu as pltpu
from jax.sharding import PartitionSpec as P

FF_BLOCK = 352
NS_ITERS = 5
HEADS_PER_STEP = 4

EPS = 1e-05
THETA = 10000.0
NS_A = 3.4445
NS_B = -4.775
NS_C = 2.0315
MUON_RATE = 0.8
GAIN_RATE = 0.002
DECAY = 0.5
HIGH = lax.Precision.HIGHEST
MASKED = -1e30
VMEM_LIMIT = 40 * 1024 * 1024
LOW = jnp.bfloat16


def doc_layout(doc_lengths, positions):
    ends = jnp.cumsum(doc_lengths)
    starts = ends - doc_lengths
    segment = jnp.sum((positions[:, None] >= ends[None, :]).astype(jnp.int32), axis=1)
    member = (
        segment[:, None] == jnp.arange(doc_lengths.shape[0], dtype=jnp.int32)[None, :]
    ).astype(jnp.int32)
    offset = positions - jnp.sum(member * starts[None, :], axis=1)
    return (segment, offset)


def rotary_tables(offset, half_dim):
    freqs = jnp.power(THETA, -jnp.arange(half_dim, dtype=jnp.float32) / half_dim)
    angle = offset.astype(jnp.float32)[..., None] * freqs
    return (jnp.cos(angle), jnp.sin(angle))


def rotate(vector, cosine, sine):
    half_dim = vector.shape[-1] // 2
    first_half = vector[..., :half_dim]
    second_half = vector[..., half_dim:]
    return jnp.concatenate(
        [first_half * cosine - second_half * sine, second_half * cosine + first_half * sine],
        axis=-1,
    )


def inverse_scale(vector):
    return lax.rsqrt(jnp.mean(vector * vector, axis=-1, keepdims=True) + EPS)


def norm_back(grad_rows, value_rows, scale_rows, gain_row):
    weighted = grad_rows * gain_row
    cubed = scale_rows * scale_rows * scale_rows
    return scale_rows * weighted - value_rows * cubed * jnp.mean(
        weighted * value_rows, axis=-1, keepdims=True
    )


def contract(left, right, left_dim, right_dim):
    return lax.dot_general(
        left,
        right,
        (((left_dim,), (right_dim,)), ((), ())),
        preferred_element_type=jnp.float32,
    )


def plain_dot(left, right):
    return contract(left, right, 1, 0)


def rows_dot(left, right):
    return contract(left, right, 1, 1)


def outer_sum(left, right):
    return contract(left, right, 0, 0)


def swap(value, flip, size):
    return lax.ppermute(value, "mp", [(i, i ^ flip) for i in range(size)])


def tie(*values):
    return lax.optimization_barrier(values)


class Gather:
    def __init__(self, value, size):
        self.size = size
        self.half = value.shape[0] // 2
        self.parts = {"own": value}

    def swap(self, name, flip):
        return swap(self.parts[name], flip, self.size)

    def first(self):
        parts = self.parts
        if self.size != 8:
            for s in range(1, self.size):
                parts[str(s)] = self.swap("own", s)
            return
        parts["one"] = self.swap("own", 1)
        parts["two"] = self.swap("own", 2)
        parts["four"] = self.swap("own", 4)

    def second(self):
        parts = self.parts
        if self.size != 8:
            return
        parts["six_top"] = swap(parts["two"][: self.half], 4, self.size)
        parts["six_low"] = swap(parts["four"][self.half :], 2, self.size)
        parts["three"] = self.swap("two", 1)
        parts["five"] = self.swap("four", 1)

    def third(self):
        parts = self.parts
        if self.size != 8:
            return
        parts["seven_top"] = self.swap("six_top", 1)
        parts["seven_low"] = self.swap("six_low", 1)

    def pieces(self):
        parts = self.parts
        if self.size != 8:
            return [[(0, parts["own"])]] + [[(0, parts[str(s)])] for s in range(1, self.size)]
        names = ("own", "one", "two", "three", "four", "five", "six", "seven")
        return [
            [(0, parts[name])]
            if name in parts
            else [(0, parts[name + "_top"]), (self.half, parts[name + "_low"])]
            for name in names
        ]


def flips_of(size):
    flips = [1 << bit for bit in range(size.bit_length() - 1)]
    return flips[1:] + flips[:1]


def gather_order(size):
    order = [0]
    for flip in flips_of(size):
        order = order + [s ^ flip for s in order]
    return order


def gather_small(value, size):
    value = value[None]
    for flip in flips_of(size):
        value = jnp.concatenate([value, swap(value, flip, size)], axis=0)
    return value


def scatter_small(parts, size):
    for flip in flips_of(size)[::-1]:
        half = parts.shape[0] // 2
        parts = wide(parts[:half]) + wide(swap(parts[half:].astype(LOW), flip, size))
    return parts[0]


def wide(value):
    return value.astype(jnp.float32)


def step_order(size):
    if size == 8:
        return [(3, 0), (1, 0), (3, 1), (2, 1)], [(1, 1), (2, 0), (0, 0), (0, 1)]
    steps = [(pair, half) for pair in range(size // 2) for half in range(2)]
    return steps[: len(steps) // 2], steps[len(steps) // 2 :]


class Scatter:
    def __init__(self, size):
        self.size = size
        self.runs = []
        self.parts = {}

    def first(self, evens, odds):
        self.runs.append((evens, odds))
        if self.size == 8:
            self.parts["core" + str(len(self.runs))] = swap(odds, 1, self.size)

    def second(self):
        if self.size != 8:
            steps = step_order(self.size)
            place = {step: (run, n) for run in (0, 1) for n, step in enumerate(steps[run])}
            total = 0.0
            for s in range(self.size):
                halves = []
                for half in (0, 1):
                    run, n = place[(s // 2, half)]
                    halves.append(self.runs[run][s % 2][n])
                part = jnp.concatenate(halves, axis=0)
                total = total + wide(swap(part, s, self.size) if s else part)
            self.parts["total"] = total
            return
        pair = wide(self.runs[0][0]) + wide(self.parts.pop("core1"))
        self.parts["two"] = swap(pair[:2].astype(LOW), 2, self.size)
        self.parts["four"] = swap(pair[2:].astype(LOW), 4, self.size)

    def third(self):
        if self.size != 8:
            return
        evens, core = self.runs[1][0], self.parts["core2"]
        low = wide(evens[0]) + wide(core[0]) + wide(self.parts["four"][0])
        top = wide(evens[1]) + wide(core[1]) + wide(self.parts["two"][0])
        self.parts["low"] = swap(low.astype(LOW), 2, self.size)
        self.parts["top"] = swap(top.astype(LOW), 4, self.size)

    def total(self):
        parts = self.parts
        if self.size != 8:
            return parts["total"]
        evens, core = self.runs[1][0], parts["core2"]
        top = wide(evens[2]) + wide(core[2]) + wide(parts["two"][1]) + wide(parts["top"])
        low = wide(evens[3]) + wide(core[3]) + wide(parts["four"][1]) + wide(parts["low"])
        return jnp.concatenate([top, low], axis=0)


def add_all(value, axis):
    size = lax.axis_size(axis)
    if size & (size - 1):
        return lax.psum(value, axis)
    flip = 1
    while flip < size:
        value = value + lax.ppermute(value, axis, [(i, i ^ flip) for i in range(size)])
        flip = 2 * flip
    return value


def masked_bias(qid_ref, kid_ref):
    rows = qid_ref[0]
    keys = kid_ref[0]
    allowed = (rows[:, 0:1] == keys[0:1, :]) & (rows[:, 1:2] >= keys[1:2, :])
    return jnp.where(allowed, 0.0, MASKED)


def forward_kernel(heads, head_dim, q_ref, kv_ref, qid_ref, kid_ref, ctx_ref, log_ref, bias_ref):
    @pl.when(pl.program_id(1) == 0)
    def _():
        bias_ref[...] = masked_bias(qid_ref, kid_ref)

    keys = kv_ref[0, :, :head_dim]
    values = kv_ref[0, :, head_dim:]
    for head in range(heads):
        cols = slice(head * head_dim, (head + 1) * head_dim)
        scores = contract(q_ref[0, :, cols], keys, 1, 1) * head_dim ** (-0.5) + bias_ref[...]
        top = jnp.max(scores, axis=-1, keepdims=True)
        powers = jnp.exp(scores - top)
        total = jnp.sum(powers, axis=-1, keepdims=True)
        log_ref[0, :, cols] = jnp.broadcast_to(top + jnp.log(total), (scores.shape[0], head_dim))
        probs = (powers * (1.0 / total)).astype(LOW)
        ctx_ref[0, :, cols] = contract(probs, values, 1, 0).astype(LOW)


def attention_forward(batch, queries, keyval, qid, kid, head_dim):
    unused, rows, width = queries.shape
    batches = 1
    seq_len = keyval.shape[1]
    heads = min(HEADS_PER_STEP, width // head_dim)
    block = pl.BlockSpec((1, rows, heads * head_dim), lambda b, h: (batch, 0, h))
    own = pl.BlockSpec((1, rows, heads * head_dim), lambda b, h: (0, 0, h))
    work = batches * rows * width * seq_len
    return pl.pallas_call(
        functools.partial(forward_kernel, heads, head_dim),
        grid=(batches, width // (heads * head_dim)),
        in_specs=[
            block,
            pl.BlockSpec((1, seq_len, 2 * head_dim), lambda b, h: (batch, 0, 0)),
            pl.BlockSpec((1, rows, 2), lambda b, h: (batch, 0, 0)),
            pl.BlockSpec((1, 2, seq_len), lambda b, h: (batch, 0, 0)),
        ],
        out_specs=[own, own],
        out_shape=[
            jax.ShapeDtypeStruct((batches, rows, width), LOW),
            jax.ShapeDtypeStruct((batches, rows, width), jnp.float32),
        ],
        scratch_shapes=[pltpu.VMEM((rows, seq_len), jnp.float32)],
        compiler_params=pltpu.CompilerParams(vmem_limit_bytes=VMEM_LIMIT),
        cost_estimate=pl.CostEstimate(
            flops=8 * work, bytes_accessed=8 * batches * rows * width, transcendentals=work // head_dim
        ),
        name="attention_forward",
    )(queries, keyval, qid, kid)


def backward_kernel(
    heads,
    head_dim,
    q_ref,
    dctx_ref,
    log_ref,
    kv_ref,
    qid_ref,
    kid_ref,
    cos_ref,
    sin_ref,
    dq_ref,
    dkv_ref,
    bias_ref,
):
    @pl.when(pl.program_id(1) == 0)
    def _():
        bias_ref[...] = masked_bias(qid_ref, kid_ref)
        dkv_ref[...] = jnp.zeros_like(dkv_ref)

    scale = head_dim ** (-0.5)
    half = head_dim // 2
    keys = kv_ref[0, :, :head_dim]
    values = kv_ref[0, :, head_dim:]
    cosine = cos_ref[0]
    sine = sin_ref[0]
    d_keys = 0.0
    d_values = 0.0
    for head in range(heads):
        cols = slice(head * head_dim, (head + 1) * head_dim)
        queries = q_ref[0, :, cols]
        d_context = dctx_ref[0, :, cols]
        scores = contract(queries, keys, 1, 1) * scale + bias_ref[...]
        probs = jnp.exp(scores - log_ref[0, :, head * head_dim : head * head_dim + 1])
        d_probs = contract(d_context, values, 1, 1)
        centre = jnp.sum(d_probs * probs, axis=-1, keepdims=True)
        d_scores = (probs * (d_probs - centre)).astype(LOW)
        d_keys = d_keys + contract(d_scores, queries, 0, 0)
        d_values = d_values + contract(probs.astype(LOW), d_context, 0, 0)
        d_query = contract(d_scores, keys, 1, 0) * scale
        first = d_query[:, :half]
        second = d_query[:, half:]
        dq_ref[0, :, cols] = jnp.concatenate(
            [first * cosine + second * sine, second * cosine - first * sine], axis=1
        ).astype(LOW)
    dkv_ref[0, :, :head_dim] += d_keys * scale
    dkv_ref[0, :, head_dim:] += d_values


def attention_backward(batch, queries, d_context, logs, keyval, qid, kid, cosine, sine, head_dim):
    unused, rows, width = queries.shape
    batches = 1
    seq_len = keyval.shape[1]
    heads = min(HEADS_PER_STEP, width // head_dim)
    block = pl.BlockSpec((1, rows, heads * head_dim), lambda b, h: (batch, 0, h))
    own = pl.BlockSpec((1, rows, heads * head_dim), lambda b, h: (0, 0, h))
    work = batches * rows * width * seq_len

    def whole(*shape):
        return pl.BlockSpec((1,) + shape, lambda b, h: (batch, 0, 0))

    return pl.pallas_call(
        functools.partial(backward_kernel, heads, head_dim),
        grid=(batches, width // (heads * head_dim)),
        in_specs=[
            block,
            block,
            own,
            whole(seq_len, 2 * head_dim),
            whole(rows, 2),
            whole(2, seq_len),
            whole(rows, head_dim // 2),
            whole(rows, head_dim // 2),
        ],
        out_specs=[own, pl.BlockSpec((1, seq_len, 2 * head_dim), lambda b, h: (0, 0, 0))],
        out_shape=[
            jax.ShapeDtypeStruct((batches, rows, width), LOW),
            jax.ShapeDtypeStruct((batches, seq_len, 2 * head_dim), jnp.float32),
        ],
        scratch_shapes=[pltpu.VMEM((rows, seq_len), jnp.float32)],
        compiler_params=pltpu.CompilerParams(vmem_limit_bytes=VMEM_LIMIT),
        cost_estimate=pl.CostEstimate(
            flops=20 * work,
            bytes_accessed=12 * batches * rows * width,
            transcendentals=work // head_dim,
        ),
        name="attention_backward",
    )(queries, d_context, logs, keyval, qid, kid, cosine, sine)


def flat_pieces(blocks):
    places = []
    arrays = []
    for number, pieces in enumerate(blocks):
        for first, rows in pieces:
            places.append((number, first, rows.shape[0]))
            arrays.append(rows)
    return places, arrays


def fetch_all(places, piece_refs, weight_ref, sem_ref):
    copies = []
    for number, (block, first, rows) in enumerate(places):
        copies.append(
            pltpu.make_async_copy(
                piece_refs[number],
                weight_ref.at[block, pl.ds(first, rows)],
                sem_ref.at[number],
            )
        )
    for copy in copies:
        copy.start()
    return copies


def project_kernel(places, head_dim, turned, *refs):
    count = len(places)
    piece_refs, refs = refs[:count], refs[count:]
    if turned:
        rows_ref, cos_ref, sin_ref, out_ref, weight_ref, sem_ref = refs
    else:
        rows_ref, out_ref, weight_ref, sem_ref = refs
    copies = fetch_all(places, piece_refs, weight_ref, sem_ref)
    depth = rows_ref.shape[1]
    width = weight_ref.shape[2]
    half = head_dim // 2
    for block in range(weight_ref.shape[0]):
        for number, place in enumerate(places):
            if place[0] == block:
                copies[number].wait()
        product = contract(rows_ref[...], weight_ref[block, :depth], 1, 0)
        if turned:
            for head in range(width // head_dim):
                first = product[:, head * head_dim : head * head_dim + half]
                second = product[:, head * head_dim + half : (head + 1) * head_dim]
                cosine = cos_ref[...]
                sine = sin_ref[...]
                place = block * width + head * head_dim
                out_ref[:, place : place + head_dim] = jnp.concatenate(
                    [first * cosine - second * sine, second * cosine + first * sine], axis=1
                ).astype(LOW)
        else:
            out_ref[:, block * width : (block + 1) * width] = product.astype(LOW)


def project(rows, blocks, head_dim, tables=None):
    places, arrays = flat_pieces(blocks)
    size = len(blocks)
    depth = max(first + count for _, first, count in places)
    width = arrays[0].shape[1]
    vmem = pl.BlockSpec(memory_space=pltpu.VMEM)
    turned = tables is not None
    return pl.pallas_call(
        functools.partial(project_kernel, places, head_dim, turned),
        in_specs=[pl.BlockSpec(memory_space=pl.ANY)] * len(arrays) + [vmem] * (3 if turned else 1),
        out_specs=vmem,
        out_shape=jax.ShapeDtypeStruct((rows.shape[0], size * width), LOW),
        scratch_shapes=[
            pltpu.VMEM((size, depth, width), LOW),
            pltpu.SemaphoreType.DMA((len(arrays),)),
        ],
        compiler_params=pltpu.CompilerParams(vmem_limit_bytes=VMEM_LIMIT),
        cost_estimate=pl.CostEstimate(
            flops=2 * rows.size * size * width,
            bytes_accessed=2 * (size * depth * width + 2 * rows.size),
            transcendentals=0,
        ),
        name="project",
    )(*arrays, rows, *(tables if turned else ()))


def project_back_kernel(places, *refs):
    count = len(places)
    piece_refs, (rows_ref, out_ref, weight_ref, sem_ref) = refs[:count], refs[count:]
    copies = fetch_all(places, piece_refs, weight_ref, sem_ref)
    depth = out_ref.shape[1]
    width = weight_ref.shape[2]
    for block in range(weight_ref.shape[0]):
        for number, place in enumerate(places):
            if place[0] == block:
                copies[number].wait()
        product = contract(
            rows_ref[:, block * width : (block + 1) * width], weight_ref[block, :depth], 1, 1
        )
        if block == 0:
            out_ref[...] = product
        else:
            out_ref[...] += product


def project_back(rows, blocks, depth):
    places, arrays = flat_pieces(blocks)
    size = len(blocks)
    height = max(first + count for _, first, count in places)
    width = arrays[0].shape[1]
    vmem = pl.BlockSpec(memory_space=pltpu.VMEM)
    return pl.pallas_call(
        functools.partial(project_back_kernel, places),
        in_specs=[pl.BlockSpec(memory_space=pl.ANY)] * len(arrays) + [vmem],
        out_specs=vmem,
        out_shape=jax.ShapeDtypeStruct((rows.shape[0], depth), jnp.float32),
        scratch_shapes=[
            pltpu.VMEM((size, height, width), LOW),
            pltpu.SemaphoreType.DMA((len(arrays),)),
        ],
        compiler_params=pltpu.CompilerParams(vmem_limit_bytes=VMEM_LIMIT),
        cost_estimate=pl.CostEstimate(
            flops=2 * rows.size * depth,
            bytes_accessed=2 * (size * height * width + 3 * rows.size),
            transcendentals=0,
        ),
        name="project_back",
    )(*arrays, rows)


def hidden_kernel(places, steps_order, turn, *refs):
    count = len(places)
    piece_refs = refs[:count]
    weight_ref, all_ref, gate_ref, up_ref, hidden_ref, turned_ref, slot_ref, sem_ref = refs[count:]
    step = pl.program_id(0)
    steps = pl.num_programs(0)
    half = slot_ref.shape[1] // 2

    def each(number, act):
        slot = lax.rem(number, 2)
        for static, (pair, side) in enumerate(steps_order):

            @pl.when(number == static)
            def _(pair=pair, side=side):
                for parity in range(2):
                    block, start = 2 * pair + parity, side * half
                    for index, (owner, first, rows) in enumerate(places):
                        if owner == block and first <= start < first + rows:
                            act(
                                pltpu.make_async_copy(
                                    piece_refs[index].at[pl.ds(start - first, half)],
                                    slot_ref.at[slot, pl.ds(parity * half, half)],
                                    sem_ref.at[slot, parity],
                                )
                            )

    @pl.when(step == 0)
    def _():
        each(step, lambda copy: copy.start())

    @pl.when(step + 1 < steps)
    def _():
        each(step + 1, lambda copy: copy.start())

    each(step, lambda copy: copy.wait())
    rows = slot_ref[lax.rem(step, 2)]
    all_ref[...] = rows
    groups, _, _, chunk = weight_ref.shape
    gate = 0.0
    upward = 0.0
    for group in range(groups):
        part = rows[:, group * chunk : (group + 1) * chunk]
        gate = gate + contract(part, weight_ref[group, 0], 1, 1)
        upward = upward + contract(part, weight_ref[group, 1], 1, 1)
    gate_ref[...] = gate
    up_ref[...] = upward
    hidden = gate * jax.nn.sigmoid(gate) * upward
    hidden_ref[...] = hidden.astype(LOW)
    turned_ref[...] = (hidden.T if turn else hidden).astype(LOW)


def in_steps(blocks):
    half = sum(piece.shape[0] for _, piece in blocks[0]) // 2
    rows = []
    for pair, side in sum(step_order(len(blocks)), []):
        start = side * half
        for pieces in blocks[2 * pair : 2 * pair + 2]:
            for first, piece in pieces:
                if first <= start < first + piece.shape[0]:
                    rows.append(piece[start - first : start - first + half])
    return jnp.concatenate(rows, axis=0)


def hidden_units(blocks, gate_up):
    places, arrays = flat_pieces(blocks)
    size = len(blocks)
    rows = max(first + count for _, first, count in places)
    depth = arrays[0].shape[1]
    units = gate_up.shape[2]
    turn = rows % 128 == 0

    def block(width):
        return pl.BlockSpec((rows, width), lambda s: (s, 0))

    turned = pl.BlockSpec((units, rows), lambda s: (0, s)) if turn else block(units)
    turned_shape = (units, size * rows) if turn else (size * rows, units)
    return pl.pallas_call(
        functools.partial(hidden_kernel, places, sum(step_order(size), []), turn),
        grid=(size,),
        in_specs=[pl.BlockSpec(memory_space=pl.ANY)] * len(arrays)
        + [pl.BlockSpec(gate_up.shape, lambda s: (0, 0, 0, 0), pipeline_mode=pl.Buffered(1))],
        out_specs=[block(depth), block(units), block(units), block(units), turned],
        out_shape=[
            jax.ShapeDtypeStruct((size * rows, depth), LOW),
            jax.ShapeDtypeStruct((size * rows, units), jnp.float32),
            jax.ShapeDtypeStruct((size * rows, units), jnp.float32),
            jax.ShapeDtypeStruct((size * rows, units), LOW),
            jax.ShapeDtypeStruct(turned_shape, LOW),
        ],
        scratch_shapes=[pltpu.VMEM((2, rows, depth), LOW), pltpu.SemaphoreType.DMA((2, 2))],
        compiler_params=pltpu.CompilerParams(vmem_limit_bytes=VMEM_LIMIT),
        cost_estimate=pl.CostEstimate(
            flops=4 * size * rows * depth * units,
            bytes_accessed=4 * size * rows * depth,
            transcendentals=size * rows * units,
        ),
        name="hidden_units",
    )(*arrays, gate_up)


def hidden_back_kernel(
    turn, cot_ref, gate_ref, up_ref, gate_up_ref, down_ref, dg_ref, du_ref, even_ref, odd_ref
):
    groups, _, chunk = down_ref.shape
    gate = gate_ref[...]
    upward = up_ref[...]
    sigma = jax.nn.sigmoid(gate)
    d_hidden = 0.0
    for group in range(groups):
        cols = slice(group * chunk, (group + 1) * chunk)
        d_hidden = d_hidden + contract(cot_ref[:, cols], down_ref[group], 1, 1)
    d_gate = d_hidden * upward * sigma * (1.0 + gate * (1.0 - sigma))
    d_up = d_hidden * gate * sigma
    dg_ref[...] = (d_gate.T if turn else d_gate).astype(LOW)
    du_ref[...] = (d_up.T if turn else d_up).astype(LOW)
    d_gate = d_gate.astype(LOW)
    d_up = d_up.astype(LOW)
    for group in range(groups):
        part = contract(d_gate, gate_up_ref[group, 0], 1, 0)
        part = (part + contract(d_up, gate_up_ref[group, 1], 1, 0)).astype(LOW)
        cols = slice(group * chunk, (group + 1) * chunk)
        even_ref[0, :, cols] = part[: part.shape[0] // 2]
        odd_ref[0, :, cols] = part[part.shape[0] // 2 :]


def hidden_back(run, cotangent, gate, upward, gate_up, down, size):
    tokens, depth = cotangent.shape
    rows = tokens // size
    units = gate.shape[1]
    steps = len(step_order(size)[run])
    first = run * steps
    turn = rows % 128 == 0

    def block(width):
        return pl.BlockSpec((rows, width), lambda s: (first + s, 0))

    if turn:
        turned = pl.BlockSpec((units, rows), lambda s: (0, s))
        turned_shape = (units, steps * rows)
    else:
        turned = pl.BlockSpec((rows, units), lambda s: (s, 0))
        turned_shape = (steps * rows, units)
    half = pl.BlockSpec((1, rows // 2, depth), lambda s: (s, 0, 0))
    return pl.pallas_call(
        functools.partial(hidden_back_kernel, turn),
        grid=(steps,),
        in_specs=[
            block(depth),
            block(units),
            block(units),
            pl.BlockSpec(gate_up.shape, lambda s: (0, 0, 0, 0), pipeline_mode=pl.Buffered(1)),
            pl.BlockSpec(down.shape, lambda s: (0, 0, 0), pipeline_mode=pl.Buffered(1)),
        ],
        out_specs=[turned, turned, half, half],
        out_shape=[
            jax.ShapeDtypeStruct(turned_shape, LOW),
            jax.ShapeDtypeStruct(turned_shape, LOW),
            jax.ShapeDtypeStruct((steps, rows // 2, depth), LOW),
            jax.ShapeDtypeStruct((steps, rows // 2, depth), LOW),
        ],
        compiler_params=pltpu.CompilerParams(vmem_limit_bytes=VMEM_LIMIT),
        cost_estimate=pl.CostEstimate(
            flops=6 * steps * rows * depth * units,
            bytes_accessed=4 * steps * rows * depth,
            transcendentals=steps * rows * units,
        ),
        name="hidden_back",
    )(cotangent, gate, upward, gate_up, down)


def hidden_out_kernel(hidden_ref, down_ref, even_ref, odd_ref):
    groups, _, chunk = down_ref.shape
    for group in range(groups):
        part = contract(hidden_ref[...], down_ref[group], 1, 0).astype(LOW)
        cols = slice(group * chunk, (group + 1) * chunk)
        even_ref[0, :, cols] = part[: part.shape[0] // 2]
        odd_ref[0, :, cols] = part[part.shape[0] // 2 :]


def hidden_out(run, hidden, down, size):
    tokens, units = hidden.shape
    rows = tokens // size
    steps = len(step_order(size)[run])
    depth = down.shape[0] * down.shape[2]
    return pl.pallas_call(
        hidden_out_kernel,
        grid=(steps,),
        in_specs=[
            pl.BlockSpec((rows, units), lambda s: (run * steps + s, 0)),
            pl.BlockSpec(down.shape, lambda s: (0, 0, 0), pipeline_mode=pl.Buffered(1)),
        ],
        out_specs=[pl.BlockSpec((1, rows // 2, depth), lambda s: (s, 0, 0))] * 2,
        out_shape=[jax.ShapeDtypeStruct((steps, rows // 2, depth), LOW)] * 2,
        compiler_params=pltpu.CompilerParams(vmem_limit_bytes=VMEM_LIMIT),
        cost_estimate=pl.CostEstimate(
            flops=2 * steps * rows * depth * units,
            bytes_accessed=2 * steps * rows * depth,
            transcendentals=0,
        ),
        name="hidden_out",
    )(hidden, down)


def units_sum_kernel(count, turn, *refs):
    unit_refs, row_ref, out_ref = refs[:count], refs[count], refs[count + 1]
    first = 0
    total = 0.0
    for unit_ref in unit_refs:
        tokens = unit_ref.shape[1 if turn else 0]
        rows = row_ref[first : first + tokens, :]
        total = total + contract(unit_ref[...], rows, 1 if turn else 0, 0)
        first = first + tokens
    out_ref[0] = total.astype(LOW)


def units_sum(units, rows, groups):
    tokens, depth = rows.shape
    turn = sum(part.shape[1] for part in units) == tokens
    width = units[0].shape[0 if turn else 1]
    chunk = depth // groups
    cut = 2
    return pl.pallas_call(
        functools.partial(units_sum_kernel, len(units), turn),
        grid=(groups * cut,),
        in_specs=[
            pl.BlockSpec(part.shape, lambda s: (0, 0), pipeline_mode=pl.Buffered(1))
            for part in units
        ]
        + [pl.BlockSpec((tokens, chunk // cut), lambda s: (0, s))],
        out_specs=pl.BlockSpec((1, width, chunk // cut), lambda s: (s // cut, 0, lax.rem(s, cut))),
        out_shape=jax.ShapeDtypeStruct((groups, width, chunk), LOW),
        compiler_params=pltpu.CompilerParams(vmem_limit_bytes=VMEM_LIMIT),
        cost_estimate=pl.CostEstimate(
            flops=2 * tokens * depth * width,
            bytes_accessed=2 * tokens * (depth + width),
            transcendentals=0,
        ),
        name="units_sum",
    )(*units, rows)


def pick(values, index):
    value = values[0]
    for number in range(1, len(values)):
        value = jnp.where(index == number, values[number], value)
    return value


def blocks_sum_kernel(row_ref, col_ref, even_ref, odd_ref):
    part = contract(row_ref[...], col_ref[...], 0, 0).astype(LOW)
    even_ref[0] = part[:, : part.shape[1] // 2]
    odd_ref[0] = part[:, part.shape[1] // 2 :]


def blocks_sum(run, rows, cols, size):
    tokens, depth = rows.shape
    width = cols.shape[1] // size
    order = step_order(size)[run]
    pairs = [pair for pair, _ in order]
    sides = [side for _, side in order]
    return pl.pallas_call(
        blocks_sum_kernel,
        grid=(len(order),),
        in_specs=[
            pl.BlockSpec((tokens, depth // 2), lambda s: (0, pick(sides, s))),
            pl.BlockSpec((tokens, 2 * width), lambda s: (0, pick(pairs, s))),
        ],
        out_specs=[pl.BlockSpec((1, depth // 2, width), lambda s: (s, 0, 0))] * 2,
        out_shape=[jax.ShapeDtypeStruct((len(order), depth // 2, width), LOW)] * 2,
        compiler_params=pltpu.CompilerParams(vmem_limit_bytes=VMEM_LIMIT),
        cost_estimate=pl.CostEstimate(
            flops=tokens * depth * len(order) * 2 * width,
            bytes_accessed=2 * depth * len(order) * width,
            transcendentals=0,
        ),
        name="blocks_sum",
    )(rows, cols)


def fine_dot(left, right, left_dim=1, right_dim=0):
    return lax.dot_general(
        left,
        right,
        (((left_dim,), (right_dim,)), ((), ())),
        precision=HIGH,
        preferred_element_type=jnp.float32,
    )


def gram_kernel(width, by_rows, matrix_ref, *gram_refs):
    for block, gram_ref in enumerate(gram_refs):
        place = slice(block * width, (block + 1) * width)
        if by_rows:
            gram_ref[...] = fine_dot(matrix_ref[place, :], matrix_ref[place, :], 1, 1)
        else:
            gram_ref[...] = fine_dot(matrix_ref[:, place], matrix_ref[:, place], 0, 0)


def block_grams(matrix, width, by_rows):
    count = matrix.shape[0 if by_rows else 1] // width
    return pl.pallas_call(
        functools.partial(gram_kernel, width, by_rows),
        out_shape=[jax.ShapeDtypeStruct((width, width), jnp.float32)] * count,
        compiler_params=pltpu.CompilerParams(vmem_limit_bytes=VMEM_LIMIT),
        cost_estimate=pl.CostEstimate(
            flops=12 * matrix.size * width, bytes_accessed=4 * matrix.size, transcendentals=0
        ),
        name="block_grams",
    )(matrix)


def newton_factor(gram):
    width = gram.shape[0]
    row = lax.broadcasted_iota(jnp.int32, (width, width), 0)
    col = lax.broadcasted_iota(jnp.int32, (width, width), 1)
    eye = jnp.where(row == col, 1.0, 0.0)
    trace = jnp.sum(jnp.sum(gram * eye, axis=1, keepdims=True), axis=0, keepdims=True)
    inverse = 1.0 / (jnp.sqrt(trace) + 1e-07)
    gram = gram * inverse * inverse
    total = None
    for iteration in range(NS_ITERS):
        poly = NS_A * eye + NS_B * gram + NS_C * fine_dot(gram, gram)
        total = poly if total is None else fine_dot(total, poly)
        if iteration < NS_ITERS - 1:
            gram = fine_dot(fine_dot(poly, gram), poly)
    return total * inverse


def factor_kernel(own_ref, *refs):
    part_refs, factor_ref = refs[:-1], refs[-1]

    @pl.when(own_ref[0] != 0)
    def _():
        gram = part_refs[0][...]
        for part_ref in part_refs[1:]:
            gram = gram + part_ref[...]
        factor_ref[...] = newton_factor(gram)

    @pl.when(own_ref[0] == 0)
    def _():
        factor_ref[...] = jnp.zeros_like(factor_ref)


def block_factor(own, parts):
    width = parts[0].shape[0]
    vmem = pl.BlockSpec(memory_space=pltpu.VMEM)
    return pl.pallas_call(
        factor_kernel,
        in_specs=[pl.BlockSpec(memory_space=pltpu.SMEM)] + [vmem] * len(parts),
        out_specs=vmem,
        out_shape=jax.ShapeDtypeStruct((width, width), jnp.float32),
        compiler_params=pltpu.CompilerParams(vmem_limit_bytes=VMEM_LIMIT),
        cost_estimate=pl.CostEstimate(
            flops=200 * width**3, bytes_accessed=20 * width * width, transcendentals=0
        ),
        name="block_factor",
    )(own, *parts)


def apply_kernel(width, count, place_ref, matrix_ref, weight_ref, *refs):
    choice_refs, new_ref, factor_ref = refs[:-2], refs[-2], refs[-1]
    for block in range(count):
        for number, choice_ref in enumerate(choice_refs):

            @pl.when(place_ref[block] == number)
            def _(choice_ref=choice_ref):
                factor_ref[...] = choice_ref[...].astype(jnp.float32)

        rows = slice(block * width, (block + 1) * width)
        new_ref[rows, :] = weight_ref[rows, :] - MUON_RATE * fine_dot(
            factor_ref[...], matrix_ref[rows, :]
        )


def apply_factors(matrix, weight, places, choices):
    width = choices[0].shape[0]
    count = matrix.shape[0] // width
    vmem = pl.BlockSpec(memory_space=pltpu.VMEM)
    return pl.pallas_call(
        functools.partial(apply_kernel, width, count),
        in_specs=[pl.BlockSpec(memory_space=pltpu.SMEM)] + [vmem] * (2 + len(choices)),
        out_specs=vmem,
        out_shape=jax.ShapeDtypeStruct(matrix.shape, jnp.float32),
        scratch_shapes=[pltpu.VMEM((width, width), jnp.float32)],
        compiler_params=pltpu.CompilerParams(vmem_limit_bytes=VMEM_LIMIT),
        cost_estimate=pl.CostEstimate(
            flops=12 * matrix.size * width, bytes_accessed=12 * matrix.size, transcendentals=0
        ),
        name="apply_factors",
    )(places, matrix, weight, *choices)


def update_kernel(width, count, by_rows, matrix_ref, weight_ref, *refs):
    part_refs, new_ref = refs[:-1], refs[-1]
    for block in range(count):
        gram = part_refs[0][block]
        for part_ref in part_refs[1:]:
            gram = gram + part_ref[block]
        factor = newton_factor(gram)
        place = slice(block * width, (block + 1) * width)
        if by_rows:
            new_ref[place, :] = weight_ref[place, :] - MUON_RATE * fine_dot(
                factor, matrix_ref[place, :]
            )
        else:
            new_ref[:, place] = weight_ref[:, place] - MUON_RATE * fine_dot(
                matrix_ref[:, place], factor
            )


def gather_grams(moment, width, by_rows):
    grams = jnp.stack(block_grams(moment, width, by_rows))
    size = lax.axis_size("dp")
    return [grams] + [
        lax.ppermute(grams, "dp", [(i, (i + shift) % size) for i in range(size)])
        for shift in range(1, size)
    ]


def small_update(moment, weight, width, by_rows, parts=None):
    if parts is None:
        parts = gather_grams(moment, width, by_rows)
    size = len(parts)
    grams = parts[0]
    vmem = pl.BlockSpec(memory_space=pltpu.VMEM)
    count = grams.shape[0]
    return pl.pallas_call(
        functools.partial(update_kernel, width, count, by_rows),
        in_specs=[vmem] * (2 + size),
        out_specs=vmem,
        out_shape=jax.ShapeDtypeStruct(moment.shape, jnp.float32),
        compiler_params=pltpu.CompilerParams(vmem_limit_bytes=VMEM_LIMIT),
        cost_estimate=pl.CostEstimate(
            flops=200 * count * width**3, bytes_accessed=12 * moment.size, transcendentals=0
        ),
        name="small_update",
    )(moment, weight, *parts)


def exchange(values, owners):
    size = lax.axis_size("dp")
    me = lax.axis_index("dp")
    parts = []
    for shift in range(size):
        target = (me + shift) % size
        part = values[0]
        for value, owner in zip(values[1:], owners[1:]):
            part = jnp.where(target == owner, value, part)
        if shift:
            pairs = [((o - shift) % size, o) for o in owners]
            part = lax.ppermute(part, "dp", pairs)
        parts.append(part)
    return parts


def share_out(factor, owners):
    size = lax.axis_size("dp")
    return [factor] + [
        lax.ppermute(factor, "dp", [(o, (o + shift) % size) for o in owners])
        for shift in range(1, size)
    ]


def owned_factor(parts, owners):
    me = lax.axis_index("dp")
    own = jnp.zeros((1,), jnp.int32)
    for o in owners:
        own = own + (me == o).astype(jnp.int32)
    return block_factor(own, parts).astype(LOW)


def owned_update(moment, weight, choices, owners):
    size = lax.axis_size("dp")
    me = lax.axis_index("dp")
    places = jnp.stack([(me - o) % size for o in owners]).astype(jnp.int32)
    return apply_factors(moment, weight, places, choices)


def shards(
    inputs,
    cotangent,
    lengths,
    w_query,
    w_keyval,
    w_out,
    w_gate_up,
    w_down,
    gains,
    m_query,
    m_keyval,
    m_out,
    m_gate_up,
    m_down,
    m_gains,
):
    batches, own_rows, model_width = inputs.shape
    head_dim = w_keyval.shape[1] // 2
    half_dim = head_dim // 2
    units_here = w_down.shape[1]
    query_cols = w_query.shape[1]
    size = lax.axis_size("mp")
    me = lax.axis_index("mp")
    tokens = batches * own_rows
    seq_len = size * own_rows

    groups = lax.axis_size("dp")
    share = w_keyval.shape[0] // size

    def rows_of(value):
        return lax.all_gather(value, "dp", axis=0, tiled=False)

    gate_up_t = jnp.transpose(w_gate_up, (1, 2, 0))
    down_t = jnp.transpose(w_down)
    low_keyval = w_keyval.astype(LOW).reshape(-1, query_cols)
    query_block = rows_of(jnp.concatenate([w_query.astype(LOW), low_keyval], axis=0))
    out_block = rows_of(w_out.astype(LOW))
    full_gate_up = rows_of(gate_up_t.astype(LOW))
    out_block, low_down = tie(out_block, down_t.astype(LOW))
    full_down = rows_of(low_down)

    cot_rows = cotangent.reshape(tokens, model_width)
    cot = Gather(cot_rows, size)
    cot.first()
    cot.second()
    full_keyval = query_block[:, w_query.shape[0] :].reshape(model_width, 2 * head_dim)
    query_block = query_block[:, : w_query.shape[0]].reshape(model_width, query_cols)
    cot.parts, query_block = tie(cot.parts, query_block)
    query_gather = Gather(query_block, size)
    query_gather.first()
    cot.third()

    own_positions = me * own_rows + jnp.arange(own_rows, dtype=jnp.int32)
    key_positions = jnp.concatenate(
        [(me ^ s) * own_rows + jnp.arange(own_rows, dtype=jnp.int32) for s in gather_order(size)]
    )
    qid = []
    kid = []
    offsets = []
    for batch_index in range(batches):
        own_segment, own_offset = doc_layout(lengths[batch_index], own_positions)
        key_segment, unused = doc_layout(lengths[batch_index], key_positions)
        qid.append(jnp.stack([own_segment, own_positions], axis=1))
        kid.append(jnp.stack([key_segment, key_positions], axis=0))
        offsets.append(own_offset)
    qid = jnp.stack(qid)
    kid = jnp.stack(kid)
    cosine, sine = rotary_tables(jnp.stack(offsets), half_dim)
    flat_cos = cosine.reshape(tokens, half_dim)
    flat_sin = sine.reshape(tokens, half_dim)

    x_rows = wide(inputs).reshape(tokens, model_width)
    x_scale = inverse_scale(x_rows)
    normed = (x_rows * x_scale * gains[0]).astype(LOW)
    own_keyval = plain_dot(normed, full_keyval)
    own_keyval = jnp.concatenate(
        [rotate(own_keyval[:, :head_dim], flat_cos, flat_sin), own_keyval[:, head_dim:]], axis=1
    ).astype(LOW)
    keyval = gather_small(own_keyval.reshape(batches, own_rows, 2 * head_dim), size)
    keyval = jnp.swapaxes(keyval, 0, 1).reshape(batches, seq_len, 2 * head_dim)
    query_gather.second()
    query_gather.parts, out_block = tie(query_gather.parts, out_block)
    out_gather = Gather(out_block.reshape(model_width, query_cols), size)
    out_gather.first()
    query_gather.third()
    query_pieces = query_gather.pieces()
    queries = project(normed, query_pieces, head_dim, (flat_cos, flat_sin))
    queries = queries.reshape(batches, own_rows, -1)
    contexts = []
    logs = []
    for batch in range(batches):
        context, log_sums = attention_forward(batch, queries, keyval, qid, kid, head_dim)
        contexts.append(context)
        logs.append(log_sums)
        if batch == 0:
            out_gather.parts, queries, contexts = tie(out_gather.parts, queries, contexts)
            out_gather.second()
    out_gather.parts, contexts = tie(out_gather.parts, contexts)
    out_gather.third()
    context = jnp.concatenate(contexts, axis=0).reshape(tokens, -1)
    full_cot = in_steps(cot.pieces())
    out_pieces = out_gather.pieces()
    mid = x_rows + project_back(context, out_pieces, model_width)
    mid_scale = inverse_scale(mid)
    normed_mid_rows = (mid * mid_scale * gains[1]).astype(LOW)
    mid_gather = Gather(normed_mid_rows, size)
    mid_gather.first()
    mid_gather.parts, full_cot = tie(mid_gather.parts, full_cot)
    mid_gather.second()
    mid_gather.third()

    normed_mid, gate, upward, hidden, hidden_t = hidden_units(mid_gather.pieces(), full_gate_up)
    sum_down = units_sum([hidden_t], full_cot, groups)
    sum_down, gate = tie(sum_down, gate)
    d_mid_sum = Scatter(size)
    backs = []
    for run in range(2):
        *turned, evens, odds = hidden_back(
            run, full_cot, gate, upward, full_gate_up, full_down, size
        )
        backs.append(turned)
        if run == 0:
            odds, gate = tie(odds, gate)
        else:
            d_mid_sum.parts, odds = tie(d_mid_sum.parts, odds)
        d_mid_sum.first(evens, odds)
    d_mid_sum.second()
    sum_gate = units_sum([back[0] for back in backs], normed_mid, groups)

    def scatter_rows(value):
        return lax.psum_scatter(value, "dp", scatter_dimension=0, tiled=False)

    old_gate_up = jnp.transpose(m_gate_up, (1, 2, 0))
    old_down = jnp.transpose(m_down)
    grad_down = scatter_rows(sum_down)
    sum_gate, backs = tie(sum_gate, backs)
    grad_gate = scatter_rows(sum_gate)
    sum_up = units_sum([back[1] for back in backs], normed_mid, groups)
    d_mid_sum.parts, sum_up, hidden, grad_down = tie(d_mid_sum.parts, sum_up, hidden, grad_down)
    grad_up = scatter_rows(sum_up)
    d_mid_sum.third()
    mlp_sum = Scatter(size)
    mlp_parts = [hidden_out(run, hidden, full_down, size) for run in range(2)]
    d_mid_sum.parts, mlp_parts = tie(d_mid_sum.parts, mlp_parts)
    for evens, odds in mlp_parts:
        mlp_sum.first(evens, odds)
    d_mid_norm = d_mid_sum.total()
    d_mid = wide(cot_rows) + norm_back(d_mid_norm, mid, mid_scale, gains[1])
    gain_mid = jnp.sum(d_mid_norm * mid * mid_scale, axis=0)

    d_mid_low = d_mid.astype(LOW)
    out_sum = Scatter(size)
    out_parts = [blocks_sum(run, d_mid_low, context, size) for run in range(2)]
    mlp_sum.parts, out_parts, d_mid_low = tie(mlp_sum.parts, out_parts, d_mid_low)
    for evens, odds in out_parts:
        out_sum.first(evens, odds)
    mlp_sum.second()
    d_context = project(d_mid_low, out_pieces, head_dim).reshape(batches, own_rows, -1)
    out_sum.parts, d_context = tie(out_sum.parts, d_context)
    out_sum.second()
    fast = groups == 4 and units_here == 2 * FF_BLOCK
    grad_down = wide(grad_down)
    moment_down = DECAY * old_down + grad_down
    moment_gate = DECAY * old_gate_up[0] + wide(grad_gate)
    first_owners = (0, 1, 2, 3)
    last_owners = (1, 2)
    backs = []
    for batch in range(batches):
        backs.append(
            attention_backward(
                batch, queries, d_context, logs[batch], keyval, qid, kid, cosine, sine, head_dim
            )
        )
        if batch == 0:
            backs, mlp_sum.parts, d_context, moment_down, moment_gate = tie(
                backs, mlp_sum.parts, d_context, moment_down, moment_gate
            )
            mlp_sum.third()
            if fast:
                down_grams = block_grams(moment_down, FF_BLOCK, True)
                gate_grams = block_grams(moment_gate, FF_BLOCK, True)
                first_parts = exchange(
                    (gate_grams[0], down_grams[0], down_grams[1], gate_grams[1]), first_owners
                )
    backs, out_sum.parts, grad_up = tie(backs, out_sum.parts, grad_up)
    out_sum.third()
    d_queries = jnp.concatenate([back[0] for back in backs], axis=0).reshape(tokens, -1)
    d_keyval = jnp.concatenate([back[1] for back in backs], axis=0).astype(LOW)

    def own_rows_of(total, width):
        return scatter_rows(total.astype(LOW).reshape(groups, -1, width))

    query_sum = Scatter(size)
    for run in range(2):
        evens, odds = blocks_sum(run, normed, d_queries, size)
        query_sum.first(evens, odds)
    query_sum.parts, out_sum.parts, d_queries = tie(query_sum.parts, out_sum.parts, d_queries)
    query_sum.second()
    grad_out = own_rows_of(out_sum.total(), query_cols)
    d_keyval = d_keyval.reshape(batches, size, own_rows, 2 * head_dim)
    d_keyval = scatter_small(jnp.swapaxes(d_keyval, 0, 1), size).reshape(tokens, 2 * head_dim)
    output = (mid + mlp_sum.total()).astype(LOW).reshape(inputs.shape)
    d_normed = project_back(d_queries, query_pieces, model_width)
    d_keyval, d_normed = tie(d_keyval, d_normed)
    d_keyval = jnp.concatenate(
        [rotate(d_keyval[:, :head_dim], flat_cos, -flat_sin), d_keyval[:, head_dim:]], axis=1
    ).astype(LOW)
    sum_keyval = outer_sum(normed, d_keyval).astype(LOW)
    sum_keyval = jnp.swapaxes(sum_keyval.reshape(groups, size, share, 2 * head_dim), 0, 1)
    order = jnp.array(gather_order(size), jnp.int32)
    sum_keyval = sum_keyval[me ^ order]
    moment_up = DECAY * old_gate_up[1] + wide(grad_up)
    if fast:
        up_grams = block_grams(moment_up, FF_BLOCK, True)
        up_grams, sum_keyval = tie(up_grams, sum_keyval)
        last_parts = exchange(up_grams, last_owners)
    share_sums = scatter_small(sum_keyval, size).astype(LOW)
    d_normed = d_normed + rows_dot(d_keyval, full_keyval)
    input_grad = (d_mid + norm_back(d_normed, x_rows, x_scale, gains[0])).astype(LOW)
    input_grad = input_grad.reshape(inputs.shape)
    gain_input = jnp.sum(d_normed * x_rows * x_scale, axis=0)
    if fast:
        share_sums, first_parts, input_grad = tie(share_sums, first_parts, input_grad)
        first_factor = owned_factor(first_parts, first_owners)
        query_sum.parts, first_factor = tie(query_sum.parts, first_factor)
    query_sum.third()
    my_group = lax.axis_index("dp")
    share_parts = [share_sums[my_group]]
    for shift in range(1, groups):
        part = share_sums[(my_group + shift) % groups]
        pairs = [(i, (i + shift) % groups) for i in range(groups)]
        share_parts.append(lax.ppermute(part, "dp", pairs))
    if fast:
        first_factor, share_parts = tie(first_factor, share_parts)
        first_choices = share_out(first_factor, first_owners)
    grad_keyval = wide(share_parts[0])
    for part in share_parts[1:]:
        grad_keyval = grad_keyval + wide(part)
    grad_keyval = gather_small(grad_keyval.astype(LOW), size)
    if fast:
        last_factor = owned_factor(last_parts, last_owners)
        query_sum.parts, grad_keyval, last_factor = tie(
            query_sum.parts, grad_keyval, last_factor
        )
        last_choices = share_out(last_factor, last_owners)
    grad_query = own_rows_of(query_sum.total(), query_cols)
    place = jnp.zeros((size,), jnp.int32).at[order].set(jnp.arange(size, dtype=jnp.int32))
    grad_keyval = grad_keyval[place[me ^ jnp.arange(size)]]
    grad_keyval = wide(grad_keyval).reshape(w_keyval.shape)
    moment_keyval = DECAY * m_keyval + grad_keyval
    keyval_grams = gather_grams(moment_keyval, 2 * head_dim, False)
    grad_out = wide(grad_out)
    moment_out = DECAY * m_out + grad_out
    out_grams = gather_grams(moment_out, head_dim, False)
    if fast:
        new_down = owned_update(moment_down, down_t, first_choices, (1, 2))
        new_gate = owned_update(moment_gate, gate_up_t[0], first_choices, (0, 3))
        new_down, new_gate, grad_query = tie(new_down, new_gate, grad_query)
    else:
        new_down = small_update(moment_down, down_t, FF_BLOCK, True)
        new_gate = small_update(moment_gate, gate_up_t[0], FF_BLOCK, True)
    grad_query = wide(grad_query)
    moment_query = DECAY * m_query + grad_query
    query_grams = gather_grams(moment_query, head_dim, False)
    if fast:
        new_up = owned_update(moment_up, gate_up_t[1], last_choices, last_owners)
    else:
        new_up = small_update(moment_up, gate_up_t[1], FF_BLOCK, True)
    new_out = small_update(moment_out, w_out, head_dim, False, out_grams)
    new_keyval = small_update(moment_keyval, w_keyval, 2 * head_dim, False, keyval_grams)
    new_query = small_update(moment_query, w_query, head_dim, False, query_grams)
    grad_gains = add_all(add_all(jnp.stack([gain_input, gain_mid], axis=0), "mp"), "dp")
    grad_gate_up = wide(jnp.stack([grad_gate, grad_up]))
    moment_gate_up = DECAY * old_gate_up + grad_gate_up
    new_gate_up = jnp.stack([new_gate, new_up])

    def back(value):
        return jnp.transpose(value, (2, 0, 1))

    moment_gains = DECAY * m_gains + grad_gains
    new_gains = gains - GAIN_RATE * moment_gains
    return (
        output,
        input_grad,
        grad_query,
        grad_keyval,
        grad_out,
        back(grad_gate_up),
        jnp.transpose(grad_down),
        grad_gains,
        moment_query,
        moment_keyval,
        moment_out,
        back(moment_gate_up),
        jnp.transpose(moment_down),
        moment_gains,
        new_query,
        new_keyval,
        new_out,
        back(new_gate_up),
        jnp.transpose(new_down),
        new_gains,
    )


def solution(mesh):
    rows = P("dp", None)
    both = P("dp", "mp")
    tokens = P("dp", "mp", None)
    gate_up = P("dp", None, "mp")
    weights = (both, rows, both, gate_up, both, P())
    return jax.shard_map(
        shards,
        mesh=mesh,
        in_specs=(tokens, tokens, rows) + weights + weights,
        out_specs=(tokens, tokens) + weights + weights + weights,
        check_vma=False,
    )
```

```python
import functools

import jax
import jax.numpy as jnp
from jax import lax
from jax.experimental import pallas as pl
from jax.experimental.pallas import tpu as pltpu
from jax.sharding import PartitionSpec as P

FF_BLOCK = 352
NS_ITERS = 5
HEADS_PER_STEP = 4

EPS = 1e-05
THETA = 10000.0
NS_A = 3.4445
NS_B = -4.775
NS_C = 2.0315
MUON_RATE = 0.8
GAIN_RATE = 0.002
DECAY = 0.5
MASKED = -1e30
VMEM_LIMIT = 40 * 1024 * 1024
LOW = jnp.bfloat16


def doc_layout(doc_lengths, positions):
    ends = jnp.cumsum(doc_lengths)
    starts = ends - doc_lengths
    segment = jnp.sum((positions[:, None] >= ends[None, :]).astype(jnp.int32), axis=1)
    member = (
        segment[:, None] == jnp.arange(doc_lengths.shape[0], dtype=jnp.int32)[None, :]
    ).astype(jnp.int32)
    offset = positions - jnp.sum(member * starts[None, :], axis=1)
    return (segment, offset)


def rotary_tables(offset, half_dim):
    freqs = jnp.power(THETA, -jnp.arange(half_dim, dtype=jnp.float32) / half_dim)
    angle = offset.astype(jnp.float32)[..., None] * freqs
    return (jnp.cos(angle), jnp.sin(angle))


def rotate(vector, cosine, sine):
    half_dim = vector.shape[-1] // 2
    first_half = vector[..., :half_dim]
    second_half = vector[..., half_dim:]
    return jnp.concatenate(
        [first_half * cosine - second_half * sine, second_half * cosine + first_half * sine],
        axis=-1,
    )


def inverse_scale(vector):
    return lax.rsqrt(jnp.mean(vector * vector, axis=-1, keepdims=True) + EPS)


def norm_back(grad_rows, value_rows, scale_rows, gain_row):
    weighted = grad_rows * gain_row
    cubed = scale_rows * scale_rows * scale_rows
    return scale_rows * weighted - value_rows * cubed * jnp.mean(
        weighted * value_rows, axis=-1, keepdims=True
    )


def contract(left, right, left_dim, right_dim):
    return lax.dot_general(
        left,
        right,
        (((left_dim,), (right_dim,)), ((), ())),
        preferred_element_type=jnp.float32,
    )


def plain_dot(left, right):
    return contract(left, right, 1, 0)


def rows_dot(left, right):
    return contract(left, right, 1, 1)


def outer_sum(left, right):
    return contract(left, right, 0, 0)


def swap(value, flip, size):
    return lax.ppermute(value, "mp", [(i, i ^ flip) for i in range(size)])


def tie(*values):
    return lax.optimization_barrier(values)


class Gather:
    def __init__(self, value, size):
        self.size = size
        self.half = value.shape[0] // 2
        self.parts = {"own": value}

    def swap(self, name, flip):
        return swap(self.parts[name], flip, self.size)

    def first(self):
        parts = self.parts
        if self.size != 8:
            for s in range(1, self.size):
                parts[str(s)] = self.swap("own", s)
            return
        parts["one"] = self.swap("own", 1)
        parts["two"] = self.swap("own", 2)
        parts["four"] = self.swap("own", 4)

    def second(self):
        parts = self.parts
        if self.size != 8:
            return
        parts["six_top"] = swap(parts["two"][: self.half], 4, self.size)
        parts["six_low"] = swap(parts["four"][self.half :], 2, self.size)

    def relay(self):
        parts = self.parts
        if self.size != 8:
            return
        parts["three"] = self.swap("two", 1)
        parts["five"] = self.swap("four", 1)

    def third(self):
        parts = self.parts
        if self.size != 8:
            return
        parts["seven_top"] = self.swap("six_top", 1)
        parts["seven_low"] = self.swap("six_low", 1)

    def pieces(self):
        parts = self.parts
        if self.size != 8:
            return [[(0, parts["own"])]] + [[(0, parts[str(s)])] for s in range(1, self.size)]
        blocks = []
        for name in ("own", "one", "two", "three", "four", "five", "six", "seven"):
            if name in parts:
                blocks.append([(0, parts[name])])
            elif name + "_top" in parts:
                blocks.append([(0, parts[name + "_top"]), (self.half, parts[name + "_low"])])
            else:
                blocks.append([])
        return blocks


def flips_of(size):
    flips = [1 << bit for bit in range(size.bit_length() - 1)]
    return flips[1:] + flips[:1]


def gather_order(size):
    order = [0]
    for flip in flips_of(size):
        order = order + [s ^ flip for s in order]
    return order


def gather_small(value, size):
    value = value[None]
    for flip in flips_of(size):
        value = jnp.concatenate([value, swap(value, flip, size)], axis=0)
    return value


def scatter_small(parts, size):
    for flip in flips_of(size)[::-1]:
        half = parts.shape[0] // 2
        parts = wide(parts[:half]) + wide(swap(parts[half:].astype(LOW), flip, size))
    return parts[0]


def wide(value):
    return value.astype(jnp.float32)


def step_order(size):
    if size == 8:
        return [(3, 0), (1, 0), (3, 1), (2, 1)], [(1, 1), (2, 0), (0, 0), (0, 1)]
    steps = [(pair, half) for pair in range(size // 2) for half in range(2)]
    return steps[: len(steps) // 2], steps[len(steps) // 2 :]


class Scatter:
    def __init__(self, size):
        self.size = size
        self.runs = []
        self.parts = {}

    def first(self, evens, odds):
        self.runs.append((evens, odds))
        if self.size == 8:
            self.parts["core" + str(len(self.runs))] = swap(odds, 1, self.size)

    def second(self, later=None):
        if self.size != 8:
            steps = step_order(self.size)
            place = {step: (run, n) for run in (0, 1) for n, step in enumerate(steps[run])}
            total = 0.0
            for s in range(self.size):
                halves = []
                for half in (0, 1):
                    run, n = place[(s // 2, half)]
                    halves.append(self.runs[run][s % 2][n])
                part = jnp.concatenate(halves, axis=0)
                total = total + wide(swap(part, s, self.size) if s else part)
            self.parts["total"] = total
            return later
        evens, core = self.runs[0][0], self.parts.pop("core1")
        two = (wide(evens[:2]) + wide(core[:2])).astype(LOW)
        four = (wide(evens[2:]) + wide(core[2:])).astype(LOW)
        two, four, later = tie(two, four, later)
        self.parts["two"] = swap(two, 2, self.size)
        self.parts["four"] = swap(four, 4, self.size)
        return later

    def third(self, later=None):
        if self.size != 8:
            return later
        evens, core = self.runs[1][0], self.parts["core2"]
        low = wide(evens[0]) + wide(core[0]) + wide(self.parts["four"][0])
        top = wide(evens[1]) + wide(core[1]) + wide(self.parts["two"][0])
        low, top, later = tie(low.astype(LOW), top.astype(LOW), later)
        self.parts["low"] = swap(low, 2, self.size)
        self.parts["top"] = swap(top, 4, self.size)
        return later

    def total(self):
        parts = self.parts
        if self.size != 8:
            return parts["total"]
        evens, core = self.runs[1][0], parts["core2"]
        top = wide(evens[2]) + wide(core[2]) + wide(parts["two"][1]) + wide(parts["top"])
        low = wide(evens[3]) + wide(core[3]) + wide(parts["four"][1]) + wide(parts["low"])
        return jnp.concatenate([top, low], axis=0)


def add_all(value, axis):
    size = lax.axis_size(axis)
    if size & (size - 1):
        return lax.psum(value, axis)
    flip = 1
    while flip < size:
        value = value + lax.ppermute(value, axis, [(i, i ^ flip) for i in range(size)])
        flip = 2 * flip
    return value


def masked_bias(qid_ref, kid_ref):
    rows = qid_ref[0]
    keys = kid_ref[0]
    allowed = (rows[:, 0:1] == keys[0:1, :]) & (rows[:, 1:2] >= keys[1:2, :])
    return jnp.where(allowed, 0.0, MASKED)


def forward_kernel(heads, head_dim, q_ref, kv_ref, qid_ref, kid_ref, ctx_ref, log_ref, bias_ref):
    @pl.when(pl.program_id(1) == 0)
    def _():
        bias_ref[...] = masked_bias(qid_ref, kid_ref)

    keys = kv_ref[0, :, :head_dim]
    values = kv_ref[0, :, head_dim:]
    for head in range(heads):
        cols = slice(head * head_dim, (head + 1) * head_dim)
        scores = contract(q_ref[0, :, cols], keys, 1, 1) * head_dim ** (-0.5) + bias_ref[...]
        top = jnp.max(scores, axis=-1, keepdims=True)
        powers = jnp.exp(scores - top)
        total = jnp.sum(powers, axis=-1, keepdims=True)
        log_ref[0, :, cols] = jnp.broadcast_to(top + jnp.log(total), (scores.shape[0], head_dim))
        probs = (powers * (1.0 / total)).astype(LOW)
        ctx_ref[0, :, cols] = contract(probs, values, 1, 0).astype(LOW)


def attention_forward(batch, queries, keyval, qid, kid, head_dim):
    unused, rows, width = queries.shape
    batches = 1
    seq_len = keyval.shape[1]
    heads = min(HEADS_PER_STEP, width // head_dim)
    block = pl.BlockSpec((1, rows, heads * head_dim), lambda b, h: (batch, 0, h))
    own = pl.BlockSpec((1, rows, heads * head_dim), lambda b, h: (0, 0, h))
    work = batches * rows * width * seq_len
    return pl.pallas_call(
        functools.partial(forward_kernel, heads, head_dim),
        grid=(batches, width // (heads * head_dim)),
        in_specs=[
            block,
            pl.BlockSpec((1, seq_len, 2 * head_dim), lambda b, h: (batch, 0, 0)),
            pl.BlockSpec((1, rows, 2), lambda b, h: (batch, 0, 0)),
            pl.BlockSpec((1, 2, seq_len), lambda b, h: (batch, 0, 0)),
        ],
        out_specs=[own, own],
        out_shape=[
            jax.ShapeDtypeStruct((batches, rows, width), LOW),
            jax.ShapeDtypeStruct((batches, rows, width), jnp.float32),
        ],
        scratch_shapes=[pltpu.VMEM((rows, seq_len), jnp.float32)],
        compiler_params=pltpu.CompilerParams(vmem_limit_bytes=VMEM_LIMIT),
        cost_estimate=pl.CostEstimate(
            flops=8 * work, bytes_accessed=8 * batches * rows * width, transcendentals=work // head_dim
        ),
        name="attention_forward",
    )(queries, keyval, qid, kid)


def backward_kernel(
    heads,
    head_dim,
    q_ref,
    dctx_ref,
    log_ref,
    kv_ref,
    qid_ref,
    kid_ref,
    cos_ref,
    sin_ref,
    dq_ref,
    dkv_ref,
    bias_ref,
):
    @pl.when(pl.program_id(1) == 0)
    def _():
        bias_ref[...] = masked_bias(qid_ref, kid_ref)
        dkv_ref[...] = jnp.zeros_like(dkv_ref)

    scale = head_dim ** (-0.5)
    half = head_dim // 2
    keys = kv_ref[0, :, :head_dim]
    values = kv_ref[0, :, head_dim:]
    cosine = cos_ref[0]
    sine = sin_ref[0]
    d_keys = 0.0
    d_values = 0.0
    for head in range(heads):
        cols = slice(head * head_dim, (head + 1) * head_dim)
        queries = q_ref[0, :, cols]
        d_context = dctx_ref[0, :, cols]
        scores = contract(queries, keys, 1, 1) * scale + bias_ref[...]
        probs = jnp.exp(scores - log_ref[0, :, head * head_dim : head * head_dim + 1])
        d_probs = contract(d_context, values, 1, 1)
        centre = jnp.sum(d_probs * probs, axis=-1, keepdims=True)
        d_scores = (probs * (d_probs - centre)).astype(LOW)
        d_keys = d_keys + contract(d_scores, queries, 0, 0)
        d_values = d_values + contract(probs.astype(LOW), d_context, 0, 0)
        d_query = contract(d_scores, keys, 1, 0) * scale
        first = d_query[:, :half]
        second = d_query[:, half:]
        dq_ref[0, :, cols] = jnp.concatenate(
            [first * cosine + second * sine, second * cosine - first * sine], axis=1
        ).astype(LOW)
    dkv_ref[0, :, :head_dim] += d_keys * scale
    dkv_ref[0, :, head_dim:] += d_values


def attention_backward(batch, queries, d_context, logs, keyval, qid, kid, cosine, sine, head_dim):
    unused, rows, width = queries.shape
    batches = 1
    seq_len = keyval.shape[1]
    heads = min(HEADS_PER_STEP, width // head_dim)
    block = pl.BlockSpec((1, rows, heads * head_dim), lambda b, h: (batch, 0, h))
    own = pl.BlockSpec((1, rows, heads * head_dim), lambda b, h: (0, 0, h))
    work = batches * rows * width * seq_len

    def whole(*shape):
        return pl.BlockSpec((1,) + shape, lambda b, h: (batch, 0, 0))

    return pl.pallas_call(
        functools.partial(backward_kernel, heads, head_dim),
        grid=(batches, width // (heads * head_dim)),
        in_specs=[
            block,
            block,
            own,
            whole(seq_len, 2 * head_dim),
            whole(rows, 2),
            whole(2, seq_len),
            whole(rows, head_dim // 2),
            whole(rows, head_dim // 2),
        ],
        out_specs=[own, pl.BlockSpec((1, seq_len, 2 * head_dim), lambda b, h: (0, 0, 0))],
        out_shape=[
            jax.ShapeDtypeStruct((batches, rows, width), LOW),
            jax.ShapeDtypeStruct((batches, seq_len, 2 * head_dim), jnp.float32),
        ],
        scratch_shapes=[pltpu.VMEM((rows, seq_len), jnp.float32)],
        compiler_params=pltpu.CompilerParams(vmem_limit_bytes=VMEM_LIMIT),
        cost_estimate=pl.CostEstimate(
            flops=20 * work,
            bytes_accessed=12 * batches * rows * width,
            transcendentals=work // head_dim,
        ),
        name="attention_backward",
    )(queries, d_context, logs, keyval, qid, kid, cosine, sine)


def flat_pieces(blocks):
    places = []
    arrays = []
    for number, pieces in enumerate(blocks):
        for first, rows in pieces:
            places.append((number, first, rows.shape[0]))
            arrays.append(rows)
    return places, arrays


def fetch_all(places, piece_refs, weight_ref, sem_ref):
    copies = []
    for number, (block, first, rows) in enumerate(places):
        copies.append(
            pltpu.make_async_copy(
                piece_refs[number],
                weight_ref.at[block, pl.ds(first, rows)],
                sem_ref.at[number],
            )
        )
    for copy in copies:
        copy.start()
    return copies


def project_kernel(places, head_dim, turned, *refs):
    count = len(places)
    piece_refs, refs = refs[:count], refs[count:]
    if turned:
        rows_ref, cos_ref, sin_ref, out_ref, weight_ref, sem_ref = refs
    else:
        rows_ref, out_ref, weight_ref, sem_ref = refs
    copies = fetch_all(places, piece_refs, weight_ref, sem_ref)
    depth = rows_ref.shape[1]
    width = weight_ref.shape[2]
    half = head_dim // 2
    for block in range(weight_ref.shape[0]):
        for number, place in enumerate(places):
            if place[0] == block:
                copies[number].wait()
        product = contract(rows_ref[...], weight_ref[block, :depth], 1, 0)
        if turned:
            for head in range(width // head_dim):
                first = product[:, head * head_dim : head * head_dim + half]
                second = product[:, head * head_dim + half : (head + 1) * head_dim]
                cosine = cos_ref[...]
                sine = sin_ref[...]
                place = block * width + head * head_dim
                out_ref[:, place : place + head_dim] = jnp.concatenate(
                    [first * cosine - second * sine, second * cosine + first * sine], axis=1
                ).astype(LOW)
        else:
            out_ref[:, block * width : (block + 1) * width] = product.astype(LOW)


def project(rows, blocks, head_dim, tables=None):
    places, arrays = flat_pieces(blocks)
    size = len(blocks)
    depth = max(first + count for _, first, count in places)
    width = arrays[0].shape[1]
    vmem = pl.BlockSpec(memory_space=pltpu.VMEM)
    turned = tables is not None
    return pl.pallas_call(
        functools.partial(project_kernel, places, head_dim, turned),
        in_specs=[pl.BlockSpec(memory_space=pl.ANY)] * len(arrays) + [vmem] * (3 if turned else 1),
        out_specs=vmem,
        out_shape=jax.ShapeDtypeStruct((rows.shape[0], size * width), LOW),
        scratch_shapes=[
            pltpu.VMEM((size, depth, width), LOW),
            pltpu.SemaphoreType.DMA((len(arrays),)),
        ],
        compiler_params=pltpu.CompilerParams(vmem_limit_bytes=VMEM_LIMIT),
        cost_estimate=pl.CostEstimate(
            flops=2 * rows.size * size * width,
            bytes_accessed=2 * (size * depth * width + 2 * rows.size),
            transcendentals=0,
        ),
        name="project",
    )(*arrays, rows, *(tables if turned else ()))


def project_back_kernel(places, *refs):
    count = len(places)
    piece_refs, (rows_ref, out_ref, weight_ref, sem_ref) = refs[:count], refs[count:]
    copies = fetch_all(places, piece_refs, weight_ref, sem_ref)
    project_back_blocks(places, copies, rows_ref, out_ref, weight_ref)


def project_back_blocks(places, copies, rows_ref, out_ref, weight_ref):
    depth = out_ref.shape[1]
    width = weight_ref.shape[2]
    for block in range(weight_ref.shape[0]):
        for number, place in enumerate(places):
            if place[0] == block:
                copies[number].wait()
        product = contract(
            rows_ref[:, block * width : (block + 1) * width], weight_ref[block, :depth], 1, 1
        )
        if block == 0:
            out_ref[...] = product
        else:
            out_ref[...] += product


def project_back(rows, blocks, depth):
    places, arrays = flat_pieces(blocks)
    size = len(blocks)
    height = max(first + count for _, first, count in places)
    width = arrays[0].shape[1]
    vmem = pl.BlockSpec(memory_space=pltpu.VMEM)
    return pl.pallas_call(
        functools.partial(project_back_kernel, places),
        in_specs=[pl.BlockSpec(memory_space=pl.ANY)] * len(arrays) + [vmem],
        out_specs=vmem,
        out_shape=jax.ShapeDtypeStruct((rows.shape[0], depth), jnp.float32),
        scratch_shapes=[
            pltpu.VMEM((size, height, width), LOW),
            pltpu.SemaphoreType.DMA((len(arrays),)),
        ],
        compiler_params=pltpu.CompilerParams(vmem_limit_bytes=VMEM_LIMIT),
        cost_estimate=pl.CostEstimate(
            flops=2 * rows.size * depth,
            bytes_accessed=2 * (size * height * width + 3 * rows.size),
            transcendentals=0,
        ),
        name="project_back",
    )(*arrays, rows)


def hidden_kernel(places, steps_order, turn, *refs):
    count = len(places)
    piece_refs = refs[:count]
    weight_ref, all_ref, gate_ref, up_ref, hidden_ref, turned_ref, slot_ref, sem_ref = refs[count:]
    step = pl.program_id(0)
    steps = pl.num_programs(0)
    half = slot_ref.shape[1] // 2

    def each(number, act):
        slot = lax.rem(number, 2)
        for static, (pair, side) in enumerate(steps_order):

            @pl.when(number == static)
            def _(pair=pair, side=side):
                for parity in range(2):
                    block, start = 2 * pair + parity, side * half
                    for index, (owner, first, rows) in enumerate(places):
                        if owner == block and first <= start < first + rows:
                            act(
                                pltpu.make_async_copy(
                                    piece_refs[index].at[pl.ds(start - first, half)],
                                    slot_ref.at[slot, pl.ds(parity * half, half)],
                                    sem_ref.at[slot, parity],
                                )
                            )

    @pl.when(step == 0)
    def _():
        each(step, lambda copy: copy.start())

    @pl.when(step + 1 < steps)
    def _():
        each(step + 1, lambda copy: copy.start())

    each(step, lambda copy: copy.wait())
    rows = slot_ref[lax.rem(step, 2)]
    all_ref[...] = rows
    groups, _, _, chunk = weight_ref.shape
    gate = 0.0
    upward = 0.0
    for group in range(groups):
        part = rows[:, group * chunk : (group + 1) * chunk]
        gate = gate + contract(part, weight_ref[group, 0], 1, 1)
        upward = upward + contract(part, weight_ref[group, 1], 1, 1)
    gate_ref[...] = gate
    up_ref[...] = upward
    hidden = gate * jax.nn.sigmoid(gate) * upward
    hidden_ref[...] = hidden.astype(LOW)
    turned_ref[...] = (hidden.T if turn else hidden).astype(LOW)


def in_steps(run, blocks):
    half = sum(piece.shape[0] for _, piece in blocks[0]) // 2
    rows = []
    for pair, side in step_order(len(blocks))[run]:
        start = side * half
        for pieces in blocks[2 * pair : 2 * pair + 2]:
            for first, piece in pieces:
                if first <= start < first + piece.shape[0]:
                    rows.append(piece[start - first : start - first + half])
    return jnp.concatenate(rows, axis=0)


def hidden_units(run, blocks, gate_up):
    size = len(blocks)
    steps = step_order(size)[run]
    used = {2 * pair + parity for pair, _ in steps for parity in (0, 1)}
    places, arrays = flat_pieces([part if s in used else [] for s, part in enumerate(blocks)])
    rows = max(first + count for _, first, count in places)
    depth = arrays[0].shape[1]
    units = gate_up.shape[2]
    turn = rows % 128 == 0

    def block(width):
        return pl.BlockSpec((rows, width), lambda s: (s, 0))

    turned = pl.BlockSpec((units, rows), lambda s: (0, s)) if turn else block(units)
    turned_shape = (units, len(steps) * rows) if turn else (len(steps) * rows, units)
    return pl.pallas_call(
        functools.partial(hidden_kernel, places, steps, turn),
        grid=(len(steps),),
        in_specs=[pl.BlockSpec(memory_space=pl.ANY)] * len(arrays)
        + [pl.BlockSpec(gate_up.shape, lambda s: (0, 0, 0, 0), pipeline_mode=pl.Buffered(1))],
        out_specs=[block(depth), block(units), block(units), block(units), turned],
        out_shape=[
            jax.ShapeDtypeStruct((len(steps) * rows, depth), LOW),
            jax.ShapeDtypeStruct((len(steps) * rows, units), jnp.float32),
            jax.ShapeDtypeStruct((len(steps) * rows, units), jnp.float32),
            jax.ShapeDtypeStruct((len(steps) * rows, units), LOW),
            jax.ShapeDtypeStruct(turned_shape, LOW),
        ],
        scratch_shapes=[pltpu.VMEM((2, rows, depth), LOW), pltpu.SemaphoreType.DMA((2, 2))],
        compiler_params=pltpu.CompilerParams(vmem_limit_bytes=VMEM_LIMIT),
        cost_estimate=pl.CostEstimate(
            flops=4 * len(steps) * rows * depth * units,
            bytes_accessed=4 * len(steps) * rows * depth,
            transcendentals=len(steps) * rows * units,
        ),
        name="hidden_units",
    )(*arrays, gate_up)


def hidden_back_kernel(
    turn, cot_ref, gate_ref, up_ref, gate_up_ref, down_ref, dg_ref, du_ref, even_ref, odd_ref
):
    groups, _, chunk = down_ref.shape
    gate = gate_ref[...]
    upward = up_ref[...]
    sigma = jax.nn.sigmoid(gate)
    d_hidden = 0.0
    for group in range(groups):
        cols = slice(group * chunk, (group + 1) * chunk)
        d_hidden = d_hidden + contract(cot_ref[:, cols], down_ref[group], 1, 1)
    d_gate = d_hidden * upward * sigma * (1.0 + gate * (1.0 - sigma))
    d_up = d_hidden * gate * sigma
    dg_ref[...] = (d_gate.T if turn else d_gate).astype(LOW)
    du_ref[...] = (d_up.T if turn else d_up).astype(LOW)
    d_gate = d_gate.astype(LOW)
    d_up = d_up.astype(LOW)
    for group in range(groups):
        part = contract(d_gate, gate_up_ref[group, 0], 1, 0)
        part = (part + contract(d_up, gate_up_ref[group, 1], 1, 0)).astype(LOW)
        cols = slice(group * chunk, (group + 1) * chunk)
        even_ref[0, :, cols] = part[: part.shape[0] // 2]
        odd_ref[0, :, cols] = part[part.shape[0] // 2 :]


def hidden_back(cotangent, gate, upward, gate_up, down, steps):
    tokens, depth = cotangent.shape
    rows = tokens // steps
    units = gate.shape[1]
    turn = rows % 128 == 0

    def block(width):
        return pl.BlockSpec((rows, width), lambda s: (s, 0))

    if turn:
        turned = pl.BlockSpec((units, rows), lambda s: (0, s))
        turned_shape = (units, steps * rows)
    else:
        turned = pl.BlockSpec((rows, units), lambda s: (s, 0))
        turned_shape = (steps * rows, units)
    half = pl.BlockSpec((1, rows // 2, depth), lambda s: (s, 0, 0))
    return pl.pallas_call(
        functools.partial(hidden_back_kernel, turn),
        grid=(steps,),
        in_specs=[
            block(depth),
            block(units),
            block(units),
            pl.BlockSpec(gate_up.shape, lambda s: (0, 0, 0, 0), pipeline_mode=pl.Buffered(1)),
            pl.BlockSpec(down.shape, lambda s: (0, 0, 0), pipeline_mode=pl.Buffered(1)),
        ],
        out_specs=[turned, turned, half, half],
        out_shape=[
            jax.ShapeDtypeStruct(turned_shape, LOW),
            jax.ShapeDtypeStruct(turned_shape, LOW),
            jax.ShapeDtypeStruct((steps, rows // 2, depth), LOW),
            jax.ShapeDtypeStruct((steps, rows // 2, depth), LOW),
        ],
        compiler_params=pltpu.CompilerParams(vmem_limit_bytes=VMEM_LIMIT),
        cost_estimate=pl.CostEstimate(
            flops=6 * steps * rows * depth * units,
            bytes_accessed=4 * steps * rows * depth,
            transcendentals=steps * rows * units,
        ),
        name="hidden_back",
    )(cotangent, gate, upward, gate_up, down)


def hidden_out_kernel(hidden_ref, down_ref, even_ref, odd_ref):
    groups, _, chunk = down_ref.shape
    for group in range(groups):
        part = contract(hidden_ref[...], down_ref[group], 1, 0).astype(LOW)
        cols = slice(group * chunk, (group + 1) * chunk)
        even_ref[0, :, cols] = part[: part.shape[0] // 2]
        odd_ref[0, :, cols] = part[part.shape[0] // 2 :]


def hidden_out(hidden, down, steps):
    tokens, units = hidden.shape
    rows = tokens // steps
    depth = down.shape[0] * down.shape[2]
    return pl.pallas_call(
        hidden_out_kernel,
        grid=(steps,),
        in_specs=[
            pl.BlockSpec((rows, units), lambda s: (s, 0)),
            pl.BlockSpec(down.shape, lambda s: (0, 0, 0), pipeline_mode=pl.Buffered(1)),
        ],
        out_specs=[pl.BlockSpec((1, rows // 2, depth), lambda s: (s, 0, 0))] * 2,
        out_shape=[jax.ShapeDtypeStruct((steps, rows // 2, depth), LOW)] * 2,
        compiler_params=pltpu.CompilerParams(vmem_limit_bytes=VMEM_LIMIT),
        cost_estimate=pl.CostEstimate(
            flops=2 * steps * rows * depth * units,
            bytes_accessed=2 * steps * rows * depth,
            transcendentals=0,
        ),
        name="hidden_out",
    )(hidden, down)


def units_sum_kernel(runs, turn, *refs):
    row_refs, refs = refs[:runs], refs[runs:]
    sums = len(refs) // (runs + 1)
    unit_refs, out_refs = refs[: runs * sums], refs[runs * sums :]
    for number, out_ref in enumerate(out_refs):
        total = 0.0
        for run, row_ref in enumerate(row_refs):
            unit_ref = unit_refs[number * runs + run]
            total = total + contract(unit_ref[...], row_ref[...], 1 if turn else 0, 0)
        out_ref[0] = total.astype(LOW)


def units_sum(units, rows, groups):
    tokens, depth = rows[0].shape
    turn = units[0][0].shape[1] == tokens
    width = units[0][0].shape[0 if turn else 1]
    chunk = depth // groups
    cut = 2
    flat = [part for parts in units for part in parts]
    out = pl.BlockSpec((1, width, chunk // cut), lambda s: (s // cut, 0, lax.rem(s, cut)))
    return pl.pallas_call(
        functools.partial(units_sum_kernel, len(rows), turn),
        grid=(groups * cut,),
        in_specs=[pl.BlockSpec((tokens, chunk // cut), lambda s: (0, s))] * len(rows)
        + [
            pl.BlockSpec(part.shape, lambda s: (0, 0), pipeline_mode=pl.Buffered(1))
            for part in flat
        ],
        out_specs=[out] * len(units),
        out_shape=[jax.ShapeDtypeStruct((groups, width, chunk), LOW)] * len(units),
        compiler_params=pltpu.CompilerParams(vmem_limit_bytes=VMEM_LIMIT),
        cost_estimate=pl.CostEstimate(
            flops=2 * len(flat) * tokens * depth * width,
            bytes_accessed=2 * len(flat) * tokens * (depth + width),
            transcendentals=0,
        ),
        name="units_sum",
    )(*rows, *flat)


def pick(values, index):
    value = values[0]
    for number in range(1, len(values)):
        value = jnp.where(index == number, values[number], value)
    return value


def blocks_sum_kernel(row_ref, col_ref, even_ref, odd_ref):
    part = contract(row_ref[...], col_ref[...], 0, 0).astype(LOW)
    even_ref[0] = part[:, : part.shape[1] // 2]
    odd_ref[0] = part[:, part.shape[1] // 2 :]


def blocks_sum(run, rows, cols, size):
    tokens, depth = rows.shape
    width = cols.shape[1] // size
    order = step_order(size)[run]
    pairs = [pair for pair, _ in order]
    sides = [side for _, side in order]
    return pl.pallas_call(
        blocks_sum_kernel,
        grid=(len(order),),
        in_specs=[
            pl.BlockSpec((tokens, depth // 2), lambda s: (0, pick(sides, s))),
            pl.BlockSpec((tokens, 2 * width), lambda s: (0, pick(pairs, s))),
        ],
        out_specs=[pl.BlockSpec((1, depth // 2, width), lambda s: (s, 0, 0))] * 2,
        out_shape=[jax.ShapeDtypeStruct((len(order), depth // 2, width), LOW)] * 2,
        compiler_params=pltpu.CompilerParams(vmem_limit_bytes=VMEM_LIMIT),
        cost_estimate=pl.CostEstimate(
            flops=tokens * depth * len(order) * 2 * width,
            bytes_accessed=2 * depth * len(order) * width,
            transcendentals=0,
        ),
        name="blocks_sum",
    )(rows, cols)


def split(value):
    high = value.astype(LOW)
    return high, (value - wide(high)).astype(LOW)


def fine_dot(left, right, left_dim=1, right_dim=0):
    left_high, left_low = split(left)
    right_high, right_low = split(right)
    small = contract(left_high, right_low, left_dim, right_dim)
    small = small + contract(left_low, right_high, left_dim, right_dim)
    return contract(left_high, right_high, left_dim, right_dim) + small


def eye_of(width):
    row = lax.broadcasted_iota(jnp.int32, (width, width), 0)
    col = lax.broadcasted_iota(jnp.int32, (width, width), 1)
    return row, col, jnp.where(row == col, 1.0, 0.0)


def packed_kernel(width, matrix_ref, *gram_refs):
    row, col, eye = eye_of(width)
    for block, gram_ref in enumerate(gram_refs):
        part = matrix_ref[block * width : (block + 1) * width, :]
        gram = fine_dot(part, part, 1, 1)
        high = wide(gram.astype(LOW))
        low = gram - high
        gram_ref[:width, :] = jnp.where(col >= row, high, low).astype(LOW)
        last = jnp.sum(low * eye, axis=0, keepdims=True)
        gram_ref[width:, :] = jnp.broadcast_to(
            last, (gram_ref.shape[0] - width, width)
        ).astype(LOW)


def packed_grams(matrix, width):
    count = matrix.shape[0] // width
    return pl.pallas_call(
        functools.partial(packed_kernel, width),
        out_shape=[jax.ShapeDtypeStruct((width + 16, width), LOW)] * count,
        compiler_params=pltpu.CompilerParams(vmem_limit_bytes=VMEM_LIMIT),
        cost_estimate=pl.CostEstimate(
            flops=6 * matrix.size * width, bytes_accessed=4 * matrix.size, transcendentals=0
        ),
        name="packed_grams",
    )(matrix)


def gram_kernel(width, by_rows, matrix_ref, *gram_refs):
    for block, gram_ref in enumerate(gram_refs):
        place = slice(block * width, (block + 1) * width)
        if by_rows:
            gram_ref[...] = fine_dot(matrix_ref[place, :], matrix_ref[place, :], 1, 1)
        else:
            gram_ref[...] = fine_dot(matrix_ref[:, place], matrix_ref[:, place], 0, 0)


def block_grams(matrix, width, by_rows):
    count = matrix.shape[0 if by_rows else 1] // width
    return pl.pallas_call(
        functools.partial(gram_kernel, width, by_rows),
        out_shape=[jax.ShapeDtypeStruct((width, width), jnp.float32)] * count,
        compiler_params=pltpu.CompilerParams(vmem_limit_bytes=VMEM_LIMIT),
        cost_estimate=pl.CostEstimate(
            flops=12 * matrix.size * width, bytes_accessed=4 * matrix.size, transcendentals=0
        ),
        name="block_grams",
    )(matrix)


def newton_factor(gram):
    _, _, eye = eye_of(gram.shape[0])
    trace = jnp.sum(jnp.sum(gram * eye, axis=1, keepdims=True), axis=0, keepdims=True)
    inverse = 1.0 / (jnp.sqrt(trace) + 1e-07)
    gram = gram * inverse * inverse
    total = None
    for iteration in range(NS_ITERS):
        poly = NS_A * eye + NS_B * gram + NS_C * fine_dot(gram, gram)
        total = poly if total is None else fine_dot(total, poly)
        if iteration < NS_ITERS - 1:
            gram = fine_dot(fine_dot(poly, gram), poly)
    return total * inverse


def factor_kernel(own_ref, *refs):
    part_refs, factor_ref = refs[:-1], refs[-1]
    width = factor_ref.shape[0]

    @pl.when(own_ref[0] != 0)
    def _():
        total = wide(part_refs[0][...])
        for part_ref in part_refs[1:]:
            total = total + wide(part_ref[...])
        _, _, eye = eye_of(width)
        packed = total[:width]
        gram = packed + packed.T + eye * (total[width : width + 1] - packed)
        factor_ref[...] = newton_factor(gram).astype(LOW)

    @pl.when(own_ref[0] == 0)
    def _():
        factor_ref[...] = jnp.zeros_like(factor_ref)


def block_factor(own, parts):
    width = parts[0].shape[1]
    vmem = pl.BlockSpec(memory_space=pltpu.VMEM)
    return pl.pallas_call(
        factor_kernel,
        in_specs=[pl.BlockSpec(memory_space=pltpu.SMEM)] + [vmem] * len(parts),
        out_specs=vmem,
        out_shape=jax.ShapeDtypeStruct((width, width), LOW),
        compiler_params=pltpu.CompilerParams(vmem_limit_bytes=VMEM_LIMIT),
        cost_estimate=pl.CostEstimate(
            flops=100 * width**3, bytes_accessed=20 * width * width, transcendentals=0
        ),
        name="block_factor",
    )(own, *parts)


def apply_kernel(width, count, place_ref, matrix_ref, weight_ref, *refs):
    choice_refs, new_ref, factor_ref = refs[:-2], refs[-2], refs[-1]
    for block in range(count):
        for number, choice_ref in enumerate(choice_refs):

            @pl.when(place_ref[block] == number)
            def _(choice_ref=choice_ref):
                factor_ref[...] = choice_ref[...]

        rows = slice(block * width, (block + 1) * width)
        high, low = split(matrix_ref[rows, :])
        product = contract(factor_ref[...], high, 1, 0) + contract(factor_ref[...], low, 1, 0)
        new_ref[rows, :] = weight_ref[rows, :] - MUON_RATE * product


def apply_factors(matrix, weight, places, choices):
    width = choices[0].shape[0]
    count = matrix.shape[0] // width
    vmem = pl.BlockSpec(memory_space=pltpu.VMEM)
    return pl.pallas_call(
        functools.partial(apply_kernel, width, count),
        in_specs=[pl.BlockSpec(memory_space=pltpu.SMEM)] + [vmem] * (2 + len(choices)),
        out_specs=vmem,
        out_shape=jax.ShapeDtypeStruct(matrix.shape, jnp.float32),
        scratch_shapes=[pltpu.VMEM((width, width), LOW)],
        compiler_params=pltpu.CompilerParams(vmem_limit_bytes=VMEM_LIMIT),
        cost_estimate=pl.CostEstimate(
            flops=4 * matrix.size * width, bytes_accessed=12 * matrix.size, transcendentals=0
        ),
        name="apply_factors",
    )(places, matrix, weight, *choices)


def update_kernel(width, count, by_rows, matrix_ref, weight_ref, *refs):
    part_refs, new_ref = refs[:-1], refs[-1]
    for block in range(count):
        gram = part_refs[0][block]
        for part_ref in part_refs[1:]:
            gram = gram + part_ref[block]
        factor = newton_factor(gram)
        place = slice(block * width, (block + 1) * width)
        if by_rows:
            new_ref[place, :] = weight_ref[place, :] - MUON_RATE * fine_dot(
                factor, matrix_ref[place, :]
            )
        else:
            new_ref[:, place] = weight_ref[:, place] - MUON_RATE * fine_dot(
                matrix_ref[:, place], factor
            )


def gather_grams(moment, width, by_rows):
    grams = jnp.stack(block_grams(moment, width, by_rows))
    size = lax.axis_size("dp")
    return [grams] + [
        lax.ppermute(grams, "dp", [(i, (i + shift) % size) for i in range(size)])
        for shift in range(1, size)
    ]


def small_update(moment, weight, width, by_rows, parts=None):
    if parts is None:
        parts = gather_grams(moment, width, by_rows)
    size = len(parts)
    grams = parts[0]
    vmem = pl.BlockSpec(memory_space=pltpu.VMEM)
    count = grams.shape[0]
    return pl.pallas_call(
        functools.partial(update_kernel, width, count, by_rows),
        in_specs=[vmem] * (2 + size),
        out_specs=vmem,
        out_shape=jax.ShapeDtypeStruct(moment.shape, jnp.float32),
        compiler_params=pltpu.CompilerParams(vmem_limit_bytes=VMEM_LIMIT),
        cost_estimate=pl.CostEstimate(
            flops=200 * count * width**3, bytes_accessed=12 * moment.size, transcendentals=0
        ),
        name="small_update",
    )(moment, weight, *parts)


def exchange(values, owners):
    size = lax.axis_size("dp")
    me = lax.axis_index("dp")
    if owners == tuple(range(size)):
        parts = lax.all_to_all(jnp.stack(values), "dp", 0, 0, tiled=True)
        return [parts[number] for number in range(size)]
    parts = []
    for shift in range(size):
        target = (me + shift) % size
        part = values[0]
        for value, owner in zip(values[1:], owners[1:]):
            part = jnp.where(target == owner, value, part)
        if shift:
            pairs = [((o - shift) % size, o) for o in owners]
            part = lax.ppermute(part, "dp", pairs)
        parts.append(part)
    return parts


def share_out(factor, owners):
    size = lax.axis_size("dp")
    return [factor] + [
        lax.ppermute(factor, "dp", [(o, (o + shift) % size) for o in owners])
        for shift in range(1, size)
    ]


def back_factor_kernel(places, parts, *refs):
    own_ref, refs = refs[0], refs[1:]
    count = len(places)
    piece_refs, refs = refs[:count], refs[count:]
    rows_ref, part_refs = refs[0], refs[1 : 1 + parts]
    out_ref, factor_ref, weight_ref, sem_ref = refs[1 + parts :]
    copies = fetch_all(places, piece_refs, weight_ref, sem_ref)
    factor_kernel(own_ref, *part_refs, factor_ref)
    project_back_blocks(places, copies, rows_ref, out_ref, weight_ref)


def back_and_factor(rows, blocks, depth, own, parts):
    places, arrays = flat_pieces(blocks)
    size = len(blocks)
    height = max(first + count for _, first, count in places)
    width = arrays[0].shape[1]
    gram_width = parts[0].shape[1]
    vmem = pl.BlockSpec(memory_space=pltpu.VMEM)
    return pl.pallas_call(
        functools.partial(back_factor_kernel, places, len(parts)),
        in_specs=[pl.BlockSpec(memory_space=pltpu.SMEM)]
        + [pl.BlockSpec(memory_space=pl.ANY)] * len(arrays)
        + [vmem] * (1 + len(parts)),
        out_specs=[vmem, vmem],
        out_shape=[
            jax.ShapeDtypeStruct((rows.shape[0], depth), jnp.float32),
            jax.ShapeDtypeStruct((gram_width, gram_width), LOW),
        ],
        scratch_shapes=[
            pltpu.VMEM((size, height, width), LOW),
            pltpu.SemaphoreType.DMA((len(arrays),)),
        ],
        compiler_params=pltpu.CompilerParams(vmem_limit_bytes=VMEM_LIMIT),
        cost_estimate=pl.CostEstimate(
            flops=2 * rows.size * depth + 100 * gram_width**3,
            bytes_accessed=2 * (size * height * width + 3 * rows.size),
            transcendentals=0,
        ),
        name="back_and_factor",
    )(own, *arrays, rows, *parts)


def is_owner(owners):
    me = lax.axis_index("dp")
    own = jnp.zeros((1,), jnp.int32)
    for o in owners:
        own = own + (me == o).astype(jnp.int32)
    return own


def owned_factor(parts, owners):
    return block_factor(is_owner(owners), parts)


def owned_update(moment, weight, choices, owners):
    size = lax.axis_size("dp")
    me = lax.axis_index("dp")
    places = jnp.stack([(me - o) % size for o in owners]).astype(jnp.int32)
    return apply_factors(moment, weight, places, choices)


def shards(
    inputs,
    cotangent,
    lengths,
    w_query,
    w_keyval,
    w_out,
    w_gate_up,
    w_down,
    gains,
    m_query,
    m_keyval,
    m_out,
    m_gate_up,
    m_down,
    m_gains,
):
    batches, own_rows, model_width = inputs.shape
    head_dim = w_keyval.shape[1] // 2
    half_dim = head_dim // 2
    units_here = w_down.shape[1]
    query_cols = w_query.shape[1]
    size = lax.axis_size("mp")
    me = lax.axis_index("mp")
    tokens = batches * own_rows
    seq_len = size * own_rows

    groups = lax.axis_size("dp")
    share = w_keyval.shape[0] // size

    def rows_of(value):
        return lax.all_gather(value, "dp", axis=0, tiled=False)

    gate_up_t = jnp.transpose(w_gate_up, (1, 2, 0))
    down_t = jnp.transpose(w_down)
    low_keyval = w_keyval.astype(LOW).reshape(-1, query_cols)
    query_block = rows_of(jnp.concatenate([w_query.astype(LOW), low_keyval], axis=0))
    out_block = rows_of(w_out.astype(LOW))
    full_gate_up = rows_of(gate_up_t.astype(LOW))
    out_block, low_down = tie(out_block, down_t.astype(LOW))
    full_down = rows_of(low_down)
    order = jnp.array(gather_order(size), jnp.int32)
    place = jnp.zeros((size,), jnp.int32).at[order].set(jnp.arange(size, dtype=jnp.int32))
    place = place[me ^ jnp.arange(size)]

    cot_rows = cotangent.reshape(tokens, model_width)
    cot = Gather(cot_rows, size)
    cot.first()
    full_keyval = query_block[:, w_query.shape[0] :].reshape(model_width, 2 * head_dim)
    query_block = query_block[:, : w_query.shape[0]].reshape(model_width, query_cols)
    cot.parts, query_block = tie(cot.parts, query_block)
    query_gather = Gather(query_block, size)
    query_gather.first()
    cot.relay()

    own_positions = me * own_rows + jnp.arange(own_rows, dtype=jnp.int32)
    key_positions = jnp.concatenate(
        [(me ^ s) * own_rows + jnp.arange(own_rows, dtype=jnp.int32) for s in gather_order(size)]
    )
    qid = []
    kid = []
    offsets = []
    for batch_index in range(batches):
        own_segment, own_offset = doc_layout(lengths[batch_index], own_positions)
        key_segment, unused = doc_layout(lengths[batch_index], key_positions)
        qid.append(jnp.stack([own_segment, own_positions], axis=1))
        kid.append(jnp.stack([key_segment, key_positions], axis=0))
        offsets.append(own_offset)
    qid = jnp.stack(qid)
    kid = jnp.stack(kid)
    cosine, sine = rotary_tables(jnp.stack(offsets), half_dim)
    flat_cos = cosine.reshape(tokens, half_dim)
    flat_sin = sine.reshape(tokens, half_dim)

    x_rows = wide(inputs).reshape(tokens, model_width)
    x_scale = inverse_scale(x_rows)
    normed = (x_rows * x_scale * gains[0]).astype(LOW)
    own_keyval = plain_dot(normed, full_keyval)
    own_keyval = jnp.concatenate(
        [rotate(own_keyval[:, :head_dim], flat_cos, flat_sin), own_keyval[:, head_dim:]], axis=1
    ).astype(LOW)
    keyval = gather_small(own_keyval.reshape(batches, own_rows, 2 * head_dim), size)
    keyval = jnp.swapaxes(keyval, 0, 1).reshape(batches, seq_len, 2 * head_dim)
    query_gather.parts, cot.parts, keyval = tie(query_gather.parts, cot.parts, keyval)
    query_gather.second()
    query_gather.relay()
    query_gather.parts, out_block = tie(query_gather.parts, out_block)
    out_gather = Gather(out_block.reshape(model_width, query_cols), size)
    out_gather.first()
    query_gather.third()
    query_pieces = query_gather.pieces()
    queries = project(normed, query_pieces, head_dim, (flat_cos, flat_sin))
    queries = queries.reshape(batches, own_rows, -1)
    contexts = []
    logs = []
    for batch in range(batches):
        context, log_sums = attention_forward(batch, queries, keyval, qid, kid, head_dim)
        contexts.append(context)
        logs.append(log_sums)
        if batch == 0:
            out_gather.parts, queries, contexts = tie(out_gather.parts, queries, contexts)
            out_gather.second()
            out_gather.relay()
    out_gather.parts, contexts, cot.parts = tie(out_gather.parts, contexts, cot.parts)
    out_gather.third()
    cot.second()
    context = jnp.concatenate(contexts, axis=0).reshape(tokens, -1)
    out_pieces = out_gather.pieces()
    mid = x_rows + project_back(context, out_pieces, model_width)
    mid_scale = inverse_scale(mid)
    normed_mid_rows = (mid * mid_scale * gains[1]).astype(LOW)
    mid_gather = Gather(normed_mid_rows, size)
    mid_gather.first()
    cot.third()
    full_cot = [in_steps(run, cot.pieces()) for run in range(2)]
    mid_gather.parts, full_cot = tie(mid_gather.parts, full_cot)
    mid_gather.second()
    mid_gather.relay()
    units = [None, None]
    units[1] = hidden_units(1, mid_gather.pieces(), full_gate_up)
    mid_gather.parts, units[1] = tie(mid_gather.parts, units[1])
    mid_gather.third()
    units[0] = hidden_units(0, mid_gather.pieces(), full_gate_up)
    normed_mid = [unit[0] for unit in units]
    (sum_down,) = units_sum([[unit[4] for unit in units]], full_cot, groups)
    sum_down, units = tie(sum_down, units)
    d_mid_sum = Scatter(size)
    steps = size // 2
    turned = []
    for run in range(2):
        _, gate, upward, _, _ = units[run]
        *grads, evens, odds = hidden_back(
            full_cot[run], gate, upward, full_gate_up, full_down, steps
        )
        turned.append(grads)
        if run == 0:
            odds, units = tie(odds, units)
        else:
            d_mid_sum.parts, odds = tie(d_mid_sum.parts, odds)
        d_mid_sum.first(evens, odds)
    turned = d_mid_sum.second(turned)

    def scatter_rows(value):
        return lax.psum_scatter(value, "dp", scatter_dimension=0, tiled=False)

    old_gate_up = jnp.transpose(m_gate_up, (1, 2, 0))
    old_down = jnp.transpose(m_down)
    grad_down = scatter_rows(sum_down)
    sum_gate, sum_up = units_sum(
        [[grads[0] for grads in turned], [grads[1] for grads in turned]], normed_mid, groups
    )
    d_mid_sum.parts, sum_gate, sum_up, grad_down = tie(
        d_mid_sum.parts, sum_gate, sum_up, grad_down
    )
    grad_gate = scatter_rows(sum_gate)
    grad_up = scatter_rows(sum_up)
    hidden = d_mid_sum.third([unit[3] for unit in units])
    mlp_sum = Scatter(size)
    mlp_parts = [hidden_out(part, full_down, steps) for part in hidden]
    d_mid_sum.parts, mlp_parts = tie(d_mid_sum.parts, mlp_parts)
    for evens, odds in mlp_parts:
        mlp_sum.first(evens, odds)
    d_mid_norm = d_mid_sum.total()
    d_mid = wide(cot_rows) + norm_back(d_mid_norm, mid, mid_scale, gains[1])
    gain_mid = jnp.sum(d_mid_norm * mid * mid_scale, axis=0)

    d_mid_low = d_mid.astype(LOW)
    out_sum = Scatter(size)
    out_parts = [blocks_sum(run, d_mid_low, context, size) for run in range(2)]
    mlp_sum.parts, out_parts, d_mid_low = tie(mlp_sum.parts, out_parts, d_mid_low)
    for evens, odds in out_parts:
        out_sum.first(evens, odds)
    d_mid_low = mlp_sum.second(d_mid_low)
    d_context = project(d_mid_low, out_pieces, head_dim).reshape(batches, own_rows, -1)
    out_sum.parts, d_context, grad_gate = tie(out_sum.parts, d_context, grad_gate)
    d_context = out_sum.second(d_context)
    fast = groups == 4 and units_here == 2 * FF_BLOCK
    grad_down = wide(grad_down)
    moment_down = DECAY * old_down + grad_down
    moment_gate = DECAY * old_gate_up[0] + wide(grad_gate)
    first_owners = (0, 1, 2, 3)
    last_owners = (1, 2)
    if fast:
        moment_down, moment_gate, d_context = tie(moment_down, moment_gate, d_context)
        down_grams = packed_grams(moment_down, FF_BLOCK)
        gate_grams = packed_grams(moment_gate, FF_BLOCK)
        down_grams, gate_grams, d_context = tie(down_grams, gate_grams, d_context)
        first_parts = exchange(
            (gate_grams[0], down_grams[0], down_grams[1], gate_grams[1]), first_owners
        )
    backs = []
    for batch in range(batches):
        backs.append(
            attention_backward(
                batch, queries, d_context, logs[batch], keyval, qid, kid, cosine, sine, head_dim
            )
        )
        if batch == 0:
            backs, mlp_sum.parts, d_context = tie(backs, mlp_sum.parts, d_context)
            d_context = mlp_sum.third(d_context)
    if fast:
        backs, first_parts = tie(backs, first_parts)
    backs, out_sum.parts, grad_up = tie(backs, out_sum.parts, grad_up)
    backs = out_sum.third(backs)
    d_queries = jnp.concatenate([back[0] for back in backs], axis=0).reshape(tokens, -1)
    d_keyval = jnp.concatenate([back[1] for back in backs], axis=0).astype(LOW)

    def own_rows_of(total, width):
        return scatter_rows(total.astype(LOW).reshape(groups, -1, width))

    query_sum = Scatter(size)
    query_parts = [blocks_sum(run, normed, d_queries, size) for run in range(2)]
    for evens, odds in query_parts:
        query_sum.first(evens, odds)
    d_keyval = d_keyval.reshape(batches, size, own_rows, 2 * head_dim)
    d_keyval = jnp.swapaxes(d_keyval, 0, 1)[place]
    d_keyval = lax.all_to_all(d_keyval, "mp", 0, 0, tiled=True)
    output = (mid + mlp_sum.total()).astype(LOW).reshape(inputs.shape)
    moment_up = DECAY * old_gate_up[1] + wide(grad_up)
    query_parts, d_queries, moment_up = tie(query_parts, d_queries, moment_up)
    if fast:
        up_grams = packed_grams(moment_up, FF_BLOCK)
        query_sum.parts, up_grams, d_queries = tie(query_sum.parts, up_grams, d_queries)
        last_parts = exchange(up_grams, last_owners)
    out_sum.parts, d_queries = tie(out_sum.parts, d_queries)
    grad_out = own_rows_of(out_sum.total(), query_cols)
    d_queries = query_sum.second(d_queries)
    if fast:
        d_normed, first_factor = back_and_factor(
            d_queries, query_pieces, model_width, is_owner(first_owners), first_parts
        )
    else:
        d_normed = project_back(d_queries, query_pieces, model_width)
    d_keyval, d_normed, query_sum.parts = tie(d_keyval, d_normed, query_sum.parts)
    d_normed = query_sum.third(d_normed)
    d_keyval = jnp.sum(wide(d_keyval), axis=0).reshape(tokens, 2 * head_dim)
    d_keyval = jnp.concatenate(
        [rotate(d_keyval[:, :head_dim], flat_cos, -flat_sin), d_keyval[:, head_dim:]], axis=1
    ).astype(LOW)
    sum_keyval = outer_sum(normed, d_keyval).astype(LOW)
    sum_keyval = jnp.swapaxes(sum_keyval.reshape(groups, size, share, 2 * head_dim), 0, 1)
    sum_keyval = lax.all_to_all(sum_keyval, "mp", 0, 0, tiled=True)
    if fast:
        last_parts, d_keyval = tie(last_parts, d_keyval)
        last_factor = owned_factor(last_parts, last_owners)
        query_sum.parts, last_factor, d_normed = tie(query_sum.parts, last_factor, d_normed)
        first_choices = share_out(first_factor, first_owners)
        last_choices = share_out(last_factor, last_owners)
    grad_query = own_rows_of(query_sum.total(), query_cols)
    d_normed = d_normed + rows_dot(d_keyval, full_keyval)
    input_grad = (d_mid + norm_back(d_normed, x_rows, x_scale, gains[0])).astype(LOW)
    input_grad = input_grad.reshape(inputs.shape)
    gain_input = jnp.sum(d_normed * x_rows * x_scale, axis=0)
    share_sums = jnp.sum(wide(sum_keyval), axis=0).astype(LOW)
    share_sums, input_grad = tie(share_sums, input_grad)
    share_parts = lax.all_to_all(share_sums, "dp", 0, 0, tiled=True)
    grad_out = wide(grad_out)
    moment_out = DECAY * m_out + grad_out
    out_grams = gather_grams(moment_out, head_dim, False)
    if fast:
        new_down = owned_update(moment_down, down_t, first_choices, (1, 2))
        new_gate = owned_update(moment_gate, gate_up_t[0], first_choices, (0, 3))
    else:
        new_down = small_update(moment_down, down_t, FF_BLOCK, True)
        new_gate = small_update(moment_gate, gate_up_t[0], FF_BLOCK, True)
    share_parts, new_gate = tie(share_parts, new_gate)
    grad_keyval = jnp.sum(wide(share_parts), axis=0)
    grad_keyval = gather_small(grad_keyval.astype(LOW), size)
    if fast:
        new_up = owned_update(moment_up, gate_up_t[1], last_choices, last_owners)
    else:
        new_up = small_update(moment_up, gate_up_t[1], FF_BLOCK, True)
    new_out = small_update(moment_out, w_out, head_dim, False, out_grams)
    grad_keyval, new_out, new_up = tie(grad_keyval, new_out, new_up)
    grad_keyval = wide(grad_keyval[place]).reshape(w_keyval.shape)
    moment_keyval = DECAY * m_keyval + grad_keyval
    keyval_grams = gather_grams(moment_keyval, 2 * head_dim, False)
    grad_query = wide(grad_query)
    moment_query = DECAY * m_query + grad_query
    query_grams = gather_grams(moment_query, head_dim, False)
    new_keyval = small_update(moment_keyval, w_keyval, 2 * head_dim, False, keyval_grams)
    new_query = small_update(moment_query, w_query, head_dim, False, query_grams)
    grad_gains = add_all(add_all(jnp.stack([gain_input, gain_mid], axis=0), "mp"), "dp")
    grad_gate_up = wide(jnp.stack([grad_gate, grad_up]))
    moment_gate_up = DECAY * old_gate_up + grad_gate_up
    new_gate_up = jnp.stack([new_gate, new_up])

    def back(value):
        return jnp.transpose(value, (2, 0, 1))

    moment_gains = DECAY * m_gains + grad_gains
    new_gains = gains - GAIN_RATE * moment_gains
    return (
        output,
        input_grad,
        grad_query,
        grad_keyval,
        grad_out,
        back(grad_gate_up),
        jnp.transpose(grad_down),
        grad_gains,
        moment_query,
        moment_keyval,
        moment_out,
        back(moment_gate_up),
        jnp.transpose(moment_down),
        moment_gains,
        new_query,
        new_keyval,
        new_out,
        back(new_gate_up),
        jnp.transpose(new_down),
        new_gains,
    )


def solution(mesh):
    rows = P("dp", None)
    both = P("dp", "mp")
    tokens = P("dp", "mp", None)
    gate_up = P("dp", None, "mp")
    weights = (both, rows, both, gate_up, both, P())
    return jax.shard_map(
        shards,
        mesh=mesh,
        in_specs=(tokens, tokens, rows) + weights + weights,
        out_specs=(tokens, tokens) + weights + weights + weights,
        check_vma=False,
    )
```

```python
import functools

import jax
import jax.numpy as jnp
from jax import lax
from jax.experimental import pallas as pl
from jax.experimental.pallas import tpu as pltpu
from jax.sharding import PartitionSpec as P

FF_BLOCK = 352
NS_ITERS = 5
FORWARD_HEADS = 8
BACKWARD_HEADS = 4

EPS = 1e-05
THETA = 10000.0
NS_A = 3.4445
NS_B = -4.775
NS_C = 2.0315
MUON_RATE = 0.8
GAIN_RATE = 0.002
DECAY = 0.5
MASKED = -1e30
VMEM_LIMIT = 40 * 1024 * 1024
VMEM_MOST = 58 * 1024 * 1024
LOW = jnp.bfloat16


def doc_layout(doc_lengths, positions):
    ends = jnp.cumsum(doc_lengths)
    starts = ends - doc_lengths
    segment = jnp.sum((positions[:, None] >= ends[None, :]).astype(jnp.int32), axis=1)
    member = (
        segment[:, None] == jnp.arange(doc_lengths.shape[0], dtype=jnp.int32)[None, :]
    ).astype(jnp.int32)
    offset = positions - jnp.sum(member * starts[None, :], axis=1)
    return (segment, offset)


def rotary_tables(offset, half_dim):
    freqs = jnp.power(THETA, -jnp.arange(half_dim, dtype=jnp.float32) / half_dim)
    angle = offset.astype(jnp.float32)[..., None] * freqs
    return (jnp.cos(angle), jnp.sin(angle))


def rotate(vector, cosine, sine):
    half_dim = vector.shape[-1] // 2
    first_half = vector[..., :half_dim]
    second_half = vector[..., half_dim:]
    return jnp.concatenate(
        [first_half * cosine - second_half * sine, second_half * cosine + first_half * sine],
        axis=-1,
    )


def inverse_scale(vector):
    return lax.rsqrt(jnp.mean(vector * vector, axis=-1, keepdims=True) + EPS)


def norm_back(grad_rows, value_rows, scale_rows, gain_row):
    weighted = grad_rows * gain_row
    cubed = scale_rows * scale_rows * scale_rows
    return scale_rows * weighted - value_rows * cubed * jnp.mean(
        weighted * value_rows, axis=-1, keepdims=True
    )


def contract(left, right, left_dim, right_dim):
    return lax.dot_general(
        left,
        right,
        (((left_dim,), (right_dim,)), ((), ())),
        preferred_element_type=jnp.float32,
    )


def plain_dot(left, right):
    return contract(left, right, 1, 0)


def rows_dot(left, right):
    return contract(left, right, 1, 1)


def outer_sum(left, right):
    return contract(left, right, 0, 0)


def swap(value, flip, size):
    return lax.ppermute(value, "mp", [(i, i ^ flip) for i in range(size)])


def tie(*values):
    return lax.optimization_barrier(values)


class Gather:
    def __init__(self, value, size):
        self.size = size
        self.half = value.shape[0] // 2
        self.parts = {"own": value}
        self.cuts = []

    def swap(self, name, flip):
        return swap(self.parts[name], flip, self.size)

    def first(self):
        parts = self.parts
        if self.size != 8:
            for s in range(1, self.size):
                parts[str(s)] = self.swap("own", s)
            return
        parts["one"] = self.swap("own", 1)
        parts["two"] = self.swap("own", 2)
        parts["four"] = self.swap("own", 4)

    def cut(self, value):
        parts = self.parts
        if self.size != 8:
            return value
        top, low = parts["two"][: self.half], parts["four"][self.half :]
        self.cuts = list(tie(top, low, value))
        return self.cuts.pop()

    def second(self):
        parts = self.parts
        if self.size != 8:
            return
        if not self.cuts:
            self.cut(jnp.zeros((), jnp.float32))
        parts["six_top"] = swap(self.cuts[0], 4, self.size)
        parts["six_low"] = swap(self.cuts[1], 2, self.size)

    def relay(self):
        parts = self.parts
        if self.size != 8:
            return
        parts["three"] = self.swap("two", 1)
        parts["five"] = self.swap("four", 1)

    def third(self):
        parts = self.parts
        if self.size != 8:
            return
        parts["seven_top"] = self.swap("six_top", 1)
        parts["seven_low"] = self.swap("six_low", 1)

    def pieces(self):
        parts = self.parts
        if self.size != 8:
            return [[(0, parts["own"])]] + [[(0, parts[str(s)])] for s in range(1, self.size)]
        blocks = []
        for name in ("own", "one", "two", "three", "four", "five", "six", "seven"):
            if name in parts:
                blocks.append([(0, parts[name])])
            elif name + "_top" in parts:
                blocks.append([(0, parts[name + "_top"]), (self.half, parts[name + "_low"])])
            else:
                blocks.append([])
        return blocks


def flips_of(size):
    flips = [1 << bit for bit in range(size.bit_length() - 1)]
    return flips[1:] + flips[:1]


def gather_order(size):
    order = [0]
    for flip in flips_of(size):
        order = order + [s ^ flip for s in order]
    return order


def gather_small(value, size):
    value = value[None]
    for flip in flips_of(size):
        value = jnp.concatenate([value, swap(value, flip, size)], axis=0)
    return value


def scatter_small(parts, size):
    for flip in flips_of(size)[::-1]:
        half = parts.shape[0] // 2
        parts = wide(parts[:half]) + wide(swap(parts[half:].astype(LOW), flip, size))
    return parts[0]


def wide(value):
    return value.astype(jnp.float32)


def step_order(size):
    if size == 8:
        return [(3, 0), (1, 0), (3, 1), (2, 1)], [(1, 1), (2, 0), (0, 0), (0, 1)]
    steps = [(pair, half) for pair in range(size // 2) for half in range(2)]
    return steps[: len(steps) // 2], steps[len(steps) // 2 :]


class Scatter:
    def __init__(self, size):
        self.size = size
        self.runs = []
        self.parts = {}

    def first(self, evens, odds):
        self.runs.append((evens, odds))
        if self.size == 8:
            self.parts["core" + str(len(self.runs))] = swap(odds, 1, self.size)

    def second(self, later=None):
        if self.size != 8:
            steps = step_order(self.size)
            place = {step: (run, n) for run in (0, 1) for n, step in enumerate(steps[run])}
            total = 0.0
            for s in range(self.size):
                halves = []
                for half in (0, 1):
                    run, n = place[(s // 2, half)]
                    halves.append(self.runs[run][s % 2][n])
                part = jnp.concatenate(halves, axis=0)
                total = total + wide(swap(part, s, self.size) if s else part)
            self.parts["total"] = total
            return later
        evens, core = self.runs[0][0], self.parts.pop("core1")
        two = (wide(evens[:2]) + wide(core[:2])).astype(LOW)
        four = (wide(evens[2:]) + wide(core[2:])).astype(LOW)
        two, four, later = tie(two, four, later)
        self.parts["two"] = swap(two, 2, self.size)
        self.parts["four"] = swap(four, 4, self.size)
        return later

    def third(self, later=None):
        if self.size != 8:
            return later
        evens, core = self.runs[1][0], self.parts["core2"]
        low = wide(evens[0]) + wide(core[0]) + wide(self.parts["four"][0])
        top = wide(evens[1]) + wide(core[1]) + wide(self.parts["two"][0])
        low, top, later = tie(low.astype(LOW), top.astype(LOW), later)
        self.parts["low"] = swap(low, 2, self.size)
        self.parts["top"] = swap(top, 4, self.size)
        return later

    def total(self):
        parts = self.parts
        if self.size != 8:
            return parts["total"]
        evens, core = self.runs[1][0], parts["core2"]
        top = wide(evens[2]) + wide(core[2]) + wide(parts["two"][1]) + wide(parts["top"])
        low = wide(evens[3]) + wide(core[3]) + wide(parts["four"][1]) + wide(parts["low"])
        return jnp.concatenate([top, low], axis=0)


def add_all(value, axis):
    size = lax.axis_size(axis)
    if size & (size - 1):
        return lax.psum(value, axis)
    flip = 1
    while flip < size:
        value = value + lax.ppermute(value, axis, [(i, i ^ flip) for i in range(size)])
        flip = 2 * flip
    return value


def masked_bias(qid_ref, kid_ref):
    rows = qid_ref[0]
    keys = kid_ref[0]
    allowed = (rows[:, 0:1] == keys[0:1, :]) & (rows[:, 1:2] >= keys[1:2, :])
    return jnp.where(allowed, 0.0, MASKED)


def forward_kernel(heads, head_dim, q_ref, kv_ref, qid_ref, kid_ref, *refs):
    ctx_ref, log_ref, bias_ref, probs_ref = refs[-4:]

    @pl.when(pl.program_id(1) == 0)
    def _():
        bias_ref[...] = masked_bias(qid_ref, kid_ref)

    keys = kv_ref[0, :, :head_dim]
    values = kv_ref[0, :, head_dim:]
    rows = q_ref.shape[1]
    for head in range(heads):
        cols = slice(head * head_dim, (head + 1) * head_dim)
        scores = contract(q_ref[0, :, cols], keys, 1, 1) * head_dim ** (-0.5) + bias_ref[...]
        top = jnp.max(scores, axis=-1, keepdims=True)
        powers = jnp.exp(scores - top)
        total = jnp.sum(powers, axis=-1, keepdims=True)
        log_ref[0, :, cols] = jnp.broadcast_to(top + jnp.log(total), (rows, head_dim))
        probs_ref[head * rows : (head + 1) * rows] = (powers * (1.0 / total)).astype(LOW)
    context = contract(probs_ref[...], values, 1, 0).astype(LOW)
    for head in range(heads):
        cols = slice(head * head_dim, (head + 1) * head_dim)
        ctx_ref[0, :, cols] = context[head * rows : (head + 1) * rows]


def attention_forward(batch, queries, keyval, qid, kid, head_dim, earlier=()):
    all_batches, rows, width = queries.shape
    batches = 1
    seq_len = keyval.shape[1]
    heads = min(FORWARD_HEADS, width // head_dim)
    block = pl.BlockSpec((1, rows, heads * head_dim), lambda b, h: (batch, 0, h))
    work = batches * rows * width * seq_len
    return pl.pallas_call(
        functools.partial(forward_kernel, heads, head_dim),
        grid=(batches, width // (heads * head_dim)),
        in_specs=[
            block,
            pl.BlockSpec((1, seq_len, 2 * head_dim), lambda b, h: (batch, 0, 0)),
            pl.BlockSpec((1, rows, 2), lambda b, h: (batch, 0, 0)),
            pl.BlockSpec((1, 2, seq_len), lambda b, h: (batch, 0, 0)),
        ]
        + [pl.BlockSpec(memory_space=pltpu.HBM)] * len(earlier),
        out_specs=[block, block],
        out_shape=[
            jax.ShapeDtypeStruct((all_batches, rows, width), LOW),
            jax.ShapeDtypeStruct((all_batches, rows, width), jnp.float32),
        ],
        input_output_aliases={4 + n: n for n in range(len(earlier))},
        scratch_shapes=[
            pltpu.VMEM((rows, seq_len), jnp.float32),
            pltpu.VMEM((heads * rows, seq_len), LOW),
        ],
        compiler_params=pltpu.CompilerParams(vmem_limit_bytes=VMEM_LIMIT),
        cost_estimate=pl.CostEstimate(
            flops=8 * work, bytes_accessed=8 * batches * rows * width, transcendentals=work // head_dim
        ),
        name="attention_forward",
    )(queries, keyval, qid, kid, *earlier)


def backward_kernel(
    heads,
    head_dim,
    q_ref,
    dctx_ref,
    log_ref,
    kv_ref,
    qid_ref,
    kid_ref,
    cos_ref,
    sin_ref,
    *refs,
):
    dq_ref, out_ref, dkv_ref, bias_ref, probs_ref, ds_ref = refs[-6:]

    @pl.when(pl.program_id(1) == 0)
    def _():
        bias_ref[...] = masked_bias(qid_ref, kid_ref)
        dkv_ref[...] = jnp.zeros_like(dkv_ref)

    scale = head_dim ** (-0.5)
    half = head_dim // 2
    keys = kv_ref[0, :, :head_dim]
    values = kv_ref[0, :, head_dim:]
    cosine = cos_ref[0]
    sine = sin_ref[0]
    rows = q_ref.shape[1]
    for head in range(heads):
        cols = slice(head * head_dim, (head + 1) * head_dim)
        place = slice(head * rows, (head + 1) * rows)
        scores = contract(q_ref[0, :, cols], keys, 1, 1) * scale + bias_ref[...]
        probs = jnp.exp(scores - log_ref[0, :, head * head_dim : head * head_dim + 1])
        d_probs = contract(dctx_ref[0, :, cols], values, 1, 1)
        centre = jnp.sum(d_probs * probs, axis=-1, keepdims=True)
        ds_ref[place] = (probs * (d_probs - centre)).astype(LOW)
        probs_ref[place] = probs.astype(LOW)
    queries = jnp.concatenate(
        [q_ref[0, :, head * head_dim : (head + 1) * head_dim] for head in range(heads)], axis=0
    )
    d_context = jnp.concatenate(
        [dctx_ref[0, :, head * head_dim : (head + 1) * head_dim] for head in range(heads)], axis=0
    )
    dkv_ref[:, :head_dim] += contract(queries, ds_ref[...], 0, 0).T * scale
    dkv_ref[:, head_dim:] += contract(d_context, probs_ref[...], 0, 0).T
    d_query = contract(ds_ref[...], keys, 1, 0) * scale
    for head in range(heads):
        first = d_query[head * rows : (head + 1) * rows, :half]
        second = d_query[head * rows : (head + 1) * rows, half:]
        dq_ref[0, :, head * head_dim : (head + 1) * head_dim] = jnp.concatenate(
            [first * cosine + second * sine, second * cosine - first * sine], axis=1
        ).astype(LOW)

    @pl.when(pl.program_id(1) == pl.num_programs(1) - 1)
    def _():
        out_ref[0] = dkv_ref[...].astype(LOW)


def attention_backward(
    batch, queries, d_context, logs, keyval, qid, kid, cosine, sine, head_dim, earlier=()
):
    all_batches, rows, width = queries.shape
    batches = 1
    seq_len = keyval.shape[1]
    heads = min(BACKWARD_HEADS, width // head_dim)
    block = pl.BlockSpec((1, rows, heads * head_dim), lambda b, h: (batch, 0, h))
    work = batches * rows * width * seq_len

    def whole(*shape):
        return pl.BlockSpec((1,) + shape, lambda b, h: (batch, 0, 0))

    return pl.pallas_call(
        functools.partial(backward_kernel, heads, head_dim),
        grid=(batches, width // (heads * head_dim)),
        in_specs=[
            block,
            block,
            block,
            whole(seq_len, 2 * head_dim),
            whole(rows, 2),
            whole(2, seq_len),
            whole(rows, head_dim // 2),
            whole(rows, head_dim // 2),
        ]
        + [pl.BlockSpec(memory_space=pltpu.HBM)] * len(earlier),
        out_specs=[block, whole(seq_len, 2 * head_dim)],
        out_shape=[
            jax.ShapeDtypeStruct((all_batches, rows, width), LOW),
            jax.ShapeDtypeStruct((all_batches, seq_len, 2 * head_dim), LOW),
        ],
        input_output_aliases={8 + n: n for n in range(len(earlier))},
        scratch_shapes=[
            pltpu.VMEM((seq_len, 2 * head_dim), jnp.float32),
            pltpu.VMEM((rows, seq_len), jnp.float32),
            pltpu.VMEM((heads * rows, seq_len), LOW),
            pltpu.VMEM((heads * rows, seq_len), LOW),
        ],
        compiler_params=pltpu.CompilerParams(vmem_limit_bytes=VMEM_LIMIT),
        cost_estimate=pl.CostEstimate(
            flops=20 * work,
            bytes_accessed=12 * batches * rows * width,
            transcendentals=work // head_dim,
        ),
        name="attention_backward",
    )(queries, d_context, logs, keyval, qid, kid, cosine, sine, *earlier)


def flat_pieces(blocks):
    places = []
    arrays = []
    for number, pieces in enumerate(blocks):
        for first, rows in pieces:
            places.append((number, first, rows.shape[0]))
            arrays.append(rows)
    return places, arrays


def fetch_all(places, piece_refs, weight_ref, sem_ref):
    copies = []
    for number, (block, first, rows) in enumerate(places):
        copies.append(
            pltpu.make_async_copy(
                piece_refs[number],
                weight_ref.at[block, pl.ds(first, rows)],
                sem_ref.at[number],
            )
        )
    for copy in copies:
        copy.start()
    return copies


def project_kernel(places, head_dim, turned, *refs):
    count = len(places)
    piece_refs, refs = refs[:count], refs[count:]
    if turned:
        rows_ref, cos_ref, sin_ref, out_ref, weight_ref, sem_ref = refs
    else:
        rows_ref, out_ref, weight_ref, sem_ref = refs
    copies = fetch_all(places, piece_refs, weight_ref, sem_ref)
    depth = rows_ref.shape[1]
    width = weight_ref.shape[2]
    half = head_dim // 2
    for block in range(weight_ref.shape[0]):
        for number, place in enumerate(places):
            if place[0] == block:
                copies[number].wait()
        product = contract(rows_ref[...], weight_ref[block, :depth], 1, 0)
        if turned:
            for head in range(width // head_dim):
                first = product[:, head * head_dim : head * head_dim + half]
                second = product[:, head * head_dim + half : (head + 1) * head_dim]
                cosine = cos_ref[...]
                sine = sin_ref[...]
                place = block * width + head * head_dim
                out_ref[:, place : place + head_dim] = jnp.concatenate(
                    [first * cosine - second * sine, second * cosine + first * sine], axis=1
                ).astype(LOW)
        else:
            out_ref[:, block * width : (block + 1) * width] = product.astype(LOW)


def project(rows, blocks, head_dim, tables=None):
    places, arrays = flat_pieces(blocks)
    size = len(blocks)
    depth = max(first + count for _, first, count in places)
    width = arrays[0].shape[1]
    vmem = pl.BlockSpec(memory_space=pltpu.VMEM)
    turned = tables is not None
    return pl.pallas_call(
        functools.partial(project_kernel, places, head_dim, turned),
        in_specs=[pl.BlockSpec(memory_space=pltpu.HBM)] * len(arrays) + [vmem] * (3 if turned else 1),
        out_specs=vmem,
        out_shape=jax.ShapeDtypeStruct((rows.shape[0], size * width), LOW),
        scratch_shapes=[
            pltpu.VMEM((size, depth, width), LOW),
            pltpu.SemaphoreType.DMA((len(arrays),)),
        ],
        compiler_params=pltpu.CompilerParams(vmem_limit_bytes=VMEM_LIMIT),
        cost_estimate=pl.CostEstimate(
            flops=2 * rows.size * size * width,
            bytes_accessed=2 * (size * depth * width + 2 * rows.size),
            transcendentals=0,
        ),
        name="project",
    )(*arrays, rows, *(tables if turned else ()))


def project_back_kernel(places, *refs):
    count = len(places)
    piece_refs, (rows_ref, out_ref, weight_ref, sem_ref) = refs[:count], refs[count:]
    copies = fetch_all(places, piece_refs, weight_ref, sem_ref)
    project_back_blocks(places, copies, rows_ref, out_ref, weight_ref)


def project_back_blocks(places, copies, rows_ref, out_ref, weight_ref):
    depth = out_ref.shape[1]
    width = weight_ref.shape[2]
    for block in range(weight_ref.shape[0]):
        for number, place in enumerate(places):
            if place[0] == block:
                copies[number].wait()
        product = contract(
            rows_ref[:, block * width : (block + 1) * width], weight_ref[block, :depth], 1, 1
        )
        if block == 0:
            out_ref[...] = product
        else:
            out_ref[...] += product


def project_back(rows, blocks, depth):
    places, arrays = flat_pieces(blocks)
    size = len(blocks)
    height = max(first + count for _, first, count in places)
    width = arrays[0].shape[1]
    vmem = pl.BlockSpec(memory_space=pltpu.VMEM)
    return pl.pallas_call(
        functools.partial(project_back_kernel, places),
        in_specs=[pl.BlockSpec(memory_space=pltpu.HBM)] * len(arrays) + [vmem],
        out_specs=vmem,
        out_shape=jax.ShapeDtypeStruct((rows.shape[0], depth), jnp.float32),
        scratch_shapes=[
            pltpu.VMEM((size, height, width), LOW),
            pltpu.SemaphoreType.DMA((len(arrays),)),
        ],
        compiler_params=pltpu.CompilerParams(vmem_limit_bytes=VMEM_LIMIT),
        cost_estimate=pl.CostEstimate(
            flops=2 * rows.size * depth,
            bytes_accessed=2 * (size * height * width + 3 * rows.size),
            transcendentals=0,
        ),
        name="project_back",
    )(*arrays, rows)


def beside(source_refs, weight_ref, sem_ref, whole=(), whole_ref=None):
    @pl.when(pl.program_id(0) == 0)
    def _():
        copies = []
        for number, source_ref in enumerate(source_refs):
            groups, _, chunk = source_ref.shape
            for group in range(groups):
                cols = pl.ds(group * chunk, chunk)
                copies.append(
                    pltpu.make_async_copy(
                        source_ref.at[group],
                        weight_ref.at[number, :, cols],
                        sem_ref.at[number, group],
                    )
                )
        for ref, number in whole:
            copies.append(
                pltpu.make_async_copy(
                    ref, whole_ref.at[number], sem_ref.at[len(source_refs) + number, 0]
                )
            )
        for copy in copies:
            copy.start()
        for copy in copies:
            copy.wait()


def hidden_kernel(places, steps_order, turn, *refs):
    count = len(places)
    piece_refs = refs[:count]
    source_refs = refs[count : count + 2]
    all_ref, gate_ref, up_ref, hidden_ref, turned_ref = refs[count + 2 : count + 7]
    slot_ref, weight_ref, sem_ref, weight_sem_ref = refs[count + 7 :]
    step = pl.program_id(0)
    steps = pl.num_programs(0)
    half = slot_ref.shape[1] // 2

    def each(number, act):
        slot = lax.rem(number, 2)
        for static, (pair, side) in enumerate(steps_order):

            @pl.when(number == static)
            def _(pair=pair, side=side):
                for parity in range(2):
                    block, start = 2 * pair + parity, side * half
                    for index, (owner, first, rows) in enumerate(places):
                        if owner == block and first <= start < first + rows:
                            act(
                                pltpu.make_async_copy(
                                    piece_refs[index].at[pl.ds(start - first, half)],
                                    slot_ref.at[slot, pl.ds(parity * half, half)],
                                    sem_ref.at[slot, parity],
                                )
                            )

    @pl.when(step == 0)
    def _():
        each(step, lambda copy: copy.start())

    @pl.when(step + 1 < steps)
    def _():
        each(step + 1, lambda copy: copy.start())

    beside(source_refs, weight_ref, weight_sem_ref)
    each(step, lambda copy: copy.wait())
    rows = slot_ref[lax.rem(step, 2)]
    all_ref[...] = rows
    gate = contract(rows, weight_ref[0], 1, 1)
    upward = contract(rows, weight_ref[1], 1, 1)
    gate_ref[...] = gate
    up_ref[...] = upward
    hidden = gate * jax.nn.sigmoid(gate) * upward
    hidden_ref[...] = hidden.astype(LOW)
    turned_ref[...] = (hidden.T if turn else hidden).astype(LOW)


def in_steps(run, blocks):
    half = sum(piece.shape[0] for _, piece in blocks[0]) // 2
    rows = []
    for pair, side in step_order(len(blocks))[run]:
        start = side * half
        for pieces in blocks[2 * pair : 2 * pair + 2]:
            for first, piece in pieces:
                if first <= start < first + piece.shape[0]:
                    rows.append(piece[start - first : start - first + half])
    return jnp.concatenate(rows, axis=0)


def hidden_units(run, blocks, full_gate, full_up):
    size = len(blocks)
    steps = step_order(size)[run]
    used = {2 * pair + parity for pair, _ in steps for parity in (0, 1)}
    places, arrays = flat_pieces([part if s in used else [] for s, part in enumerate(blocks)])
    rows = max(first + count for _, first, count in places)
    depth = arrays[0].shape[1]
    units = full_gate.shape[1]
    turn = rows % 128 == 0

    def block(width):
        return pl.BlockSpec((rows, width), lambda s: (s, 0))

    turned = pl.BlockSpec((units, rows), lambda s: (0, s)) if turn else block(units)
    turned_shape = (units, len(steps) * rows) if turn else (len(steps) * rows, units)
    return pl.pallas_call(
        functools.partial(hidden_kernel, places, steps, turn),
        grid=(len(steps),),
        in_specs=[pl.BlockSpec(memory_space=pltpu.HBM)] * (len(arrays) + 2),
        out_specs=[block(depth), block(units), block(units), block(units), turned],
        out_shape=[
            jax.ShapeDtypeStruct((len(steps) * rows, depth), LOW),
            jax.ShapeDtypeStruct((len(steps) * rows, units), jnp.float32),
            jax.ShapeDtypeStruct((len(steps) * rows, units), jnp.float32),
            jax.ShapeDtypeStruct((len(steps) * rows, units), LOW),
            jax.ShapeDtypeStruct(turned_shape, LOW),
        ],
        scratch_shapes=[
            pltpu.VMEM((2, rows, depth), LOW),
            pltpu.VMEM((2, units, depth), LOW),
            pltpu.SemaphoreType.DMA((2, 2)),
            pltpu.SemaphoreType.DMA((2, full_gate.shape[0])),
        ],
        compiler_params=pltpu.CompilerParams(vmem_limit_bytes=VMEM_LIMIT),
        cost_estimate=pl.CostEstimate(
            flops=4 * len(steps) * rows * depth * units,
            bytes_accessed=4 * len(steps) * rows * depth,
            transcendentals=len(steps) * rows * units,
        ),
        name="hidden_units",
    )(*arrays, full_gate, full_up)


def hidden_back_kernel(
    turn,
    cot_ref,
    gate_ref,
    up_ref,
    full_gate_ref,
    full_up_ref,
    source_ref,
    dg_ref,
    du_ref,
    even_ref,
    odd_ref,
    down_ref,
    both_ref,
    sem_ref,
):
    groups, _, chunk = full_gate_ref.shape
    beside([source_ref], down_ref, sem_ref, [(full_gate_ref, 0), (full_up_ref, 1)], both_ref)
    gate = gate_ref[...]
    upward = up_ref[...]
    sigma = jax.nn.sigmoid(gate)
    d_hidden = contract(cot_ref[...], down_ref[0], 1, 1)
    d_gate = d_hidden * upward * sigma * (1.0 + gate * (1.0 - sigma))
    d_up = d_hidden * gate * sigma
    dg_ref[...] = (d_gate.T if turn else d_gate).astype(LOW)
    du_ref[...] = (d_up.T if turn else d_up).astype(LOW)
    d_gate = d_gate.astype(LOW)
    d_up = d_up.astype(LOW)
    for group in range(groups):
        part = contract(d_gate, both_ref[0, group], 1, 0)
        part = (part + contract(d_up, both_ref[1, group], 1, 0)).astype(LOW)
        cols = slice(group * chunk, (group + 1) * chunk)
        even_ref[0, :, cols] = part[: part.shape[0] // 2]
        odd_ref[0, :, cols] = part[part.shape[0] // 2 :]


def hidden_back(cotangent, gate, upward, full_gate, full_up, down, steps):
    tokens, depth = cotangent.shape
    rows = tokens // steps
    units = gate.shape[1]
    turn = rows % 128 == 0

    def block(width):
        return pl.BlockSpec((rows, width), lambda s: (s, 0))

    if turn:
        turned = pl.BlockSpec((units, rows), lambda s: (0, s))
        turned_shape = (units, steps * rows)
    else:
        turned = pl.BlockSpec((rows, units), lambda s: (s, 0))
        turned_shape = (steps * rows, units)
    half = pl.BlockSpec((1, rows // 2, depth), lambda s: (s, 0, 0))
    return pl.pallas_call(
        functools.partial(hidden_back_kernel, turn),
        grid=(steps,),
        in_specs=[
            block(depth),
            block(units),
            block(units),
            pl.BlockSpec(memory_space=pltpu.HBM),
            pl.BlockSpec(memory_space=pltpu.HBM),
            pl.BlockSpec(memory_space=pltpu.HBM),
        ],
        out_specs=[turned, turned, half, half],
        out_shape=[
            jax.ShapeDtypeStruct(turned_shape, LOW),
            jax.ShapeDtypeStruct(turned_shape, LOW),
            jax.ShapeDtypeStruct((steps, rows // 2, depth), LOW),
            jax.ShapeDtypeStruct((steps, rows // 2, depth), LOW),
        ],
        scratch_shapes=[
            pltpu.VMEM((1, units, depth), LOW),
            pltpu.VMEM((2,) + full_gate.shape, LOW),
            pltpu.SemaphoreType.DMA((3, down.shape[0])),
        ],
        compiler_params=pltpu.CompilerParams(vmem_limit_bytes=VMEM_MOST),
        cost_estimate=pl.CostEstimate(
            flops=6 * steps * rows * depth * units,
            bytes_accessed=4 * steps * rows * depth,
            transcendentals=steps * rows * units,
        ),
        name="hidden_back",
    )(cotangent, gate, upward, full_gate, full_up, down)


def hidden_out_kernel(hidden_ref, down_ref, even_ref, odd_ref):
    groups, _, chunk = down_ref.shape
    for group in range(groups):
        part = contract(hidden_ref[...], down_ref[group], 1, 0).astype(LOW)
        cols = slice(group * chunk, (group + 1) * chunk)
        even_ref[0, :, cols] = part[: part.shape[0] // 2]
        odd_ref[0, :, cols] = part[part.shape[0] // 2 :]


def hidden_out(hidden, down, steps):
    tokens, units = hidden.shape
    rows = tokens // steps
    depth = down.shape[0] * down.shape[2]
    return pl.pallas_call(
        hidden_out_kernel,
        grid=(steps,),
        in_specs=[
            pl.BlockSpec((rows, units), lambda s: (s, 0)),
            pl.BlockSpec(down.shape, lambda s: (0, 0, 0), pipeline_mode=pl.Buffered(1)),
        ],
        out_specs=[pl.BlockSpec((1, rows // 2, depth), lambda s: (s, 0, 0))] * 2,
        out_shape=[jax.ShapeDtypeStruct((steps, rows // 2, depth), LOW)] * 2,
        compiler_params=pltpu.CompilerParams(vmem_limit_bytes=VMEM_LIMIT),
        cost_estimate=pl.CostEstimate(
            flops=2 * steps * rows * depth * units,
            bytes_accessed=2 * steps * rows * depth,
            transcendentals=0,
        ),
        name="hidden_out",
    )(hidden, down)


def units_sum_kernel(runs, turn, *refs):
    row_refs, refs = refs[:runs], refs[runs:]
    sums = len(refs) // (runs + 1)
    unit_refs, out_refs = refs[: runs * sums], refs[runs * sums :]
    for number, out_ref in enumerate(out_refs):
        total = 0.0
        for run, row_ref in enumerate(row_refs):
            unit_ref = unit_refs[number * runs + run]
            total = total + contract(unit_ref[...], row_ref[...], 1 if turn else 0, 0)
        out_ref[0] = total.astype(LOW)


def units_sum(units, rows, groups):
    tokens, depth = rows[0].shape
    turn = units[0][0].shape[1] == tokens
    width = units[0][0].shape[0 if turn else 1]
    chunk = depth // groups
    cut = 2
    flat = [part for parts in units for part in parts]
    out = pl.BlockSpec((1, width, chunk // cut), lambda s: (s // cut, 0, lax.rem(s, cut)))
    return pl.pallas_call(
        functools.partial(units_sum_kernel, len(rows), turn),
        grid=(groups * cut,),
        in_specs=[pl.BlockSpec((tokens, chunk // cut), lambda s: (0, s))] * len(rows)
        + [
            pl.BlockSpec(part.shape, lambda s: (0, 0), pipeline_mode=pl.Buffered(1))
            for part in flat
        ],
        out_specs=[out] * len(units),
        out_shape=[jax.ShapeDtypeStruct((groups, width, chunk), LOW)] * len(units),
        compiler_params=pltpu.CompilerParams(vmem_limit_bytes=VMEM_LIMIT),
        cost_estimate=pl.CostEstimate(
            flops=2 * len(flat) * tokens * depth * width,
            bytes_accessed=2 * len(flat) * tokens * (depth + width),
            transcendentals=0,
        ),
        name="units_sum",
    )(*rows, *flat)


def pick(values, index):
    value = values[0]
    for number in range(1, len(values)):
        value = jnp.where(index == number, values[number], value)
    return value


def blocks_sum_kernel(row_ref, col_ref, even_ref, odd_ref):
    part = contract(row_ref[...], col_ref[...], 0, 0).astype(LOW)
    even_ref[0] = part[:, : part.shape[1] // 2]
    odd_ref[0] = part[:, part.shape[1] // 2 :]


def blocks_sum(run, rows, cols, size):
    tokens, depth = rows.shape
    width = cols.shape[1] // size
    order = step_order(size)[run]
    pairs = [pair for pair, _ in order]
    sides = [side for _, side in order]
    return pl.pallas_call(
        blocks_sum_kernel,
        grid=(len(order),),
        in_specs=[
            pl.BlockSpec((tokens, depth // 2), lambda s: (0, pick(sides, s))),
            pl.BlockSpec((tokens, 2 * width), lambda s: (0, pick(pairs, s))),
        ],
        out_specs=[pl.BlockSpec((1, depth // 2, width), lambda s: (s, 0, 0))] * 2,
        out_shape=[jax.ShapeDtypeStruct((len(order), depth // 2, width), LOW)] * 2,
        compiler_params=pltpu.CompilerParams(vmem_limit_bytes=VMEM_LIMIT),
        cost_estimate=pl.CostEstimate(
            flops=tokens * depth * len(order) * 2 * width,
            bytes_accessed=2 * depth * len(order) * width,
            transcendentals=0,
        ),
        name="blocks_sum",
    )(rows, cols)


def split(value):
    high = value.astype(LOW)
    return high, (value - wide(high)).astype(LOW)


def fine_dot(left, right, left_dim=1, right_dim=0):
    left_high, left_low = split(left)
    right_high, right_low = split(right)
    small = contract(left_high, right_low, left_dim, right_dim)
    small = small + contract(left_low, right_high, left_dim, right_dim)
    return contract(left_high, right_high, left_dim, right_dim) + small


def eye_of(width):
    row = lax.broadcasted_iota(jnp.int32, (width, width), 0)
    col = lax.broadcasted_iota(jnp.int32, (width, width), 1)
    return row, col, jnp.where(row == col, 1.0, 0.0)


def packed_kernel(width, slots, *refs):
    matrix_refs, out_ref = refs[:-1], refs[-1]
    row, col, eye = eye_of(width)
    for slot in range(out_ref.shape[0]):
        if slot not in [used for _, _, used in slots]:
            out_ref[slot] = jnp.zeros_like(out_ref[slot])
    for number, block, slot in slots:
        part = matrix_refs[number][block * width : (block + 1) * width, :]
        gram = fine_dot(part, part, 1, 1)
        high = wide(gram.astype(LOW))
        low = gram - high
        out_ref[slot, :width, :] = jnp.where(col >= row, high, low).astype(LOW)
        last = jnp.sum(low * eye, axis=0, keepdims=True)
        out_ref[slot, width:, :] = jnp.broadcast_to(
            last, (out_ref.shape[1] - width, width)
        ).astype(LOW)


def owners_parts(matrices, width, slots, size):
    packed = pl.pallas_call(
        functools.partial(packed_kernel, width, slots),
        out_shape=jax.ShapeDtypeStruct((size, width + 16, width), LOW),
        compiler_params=pltpu.CompilerParams(vmem_limit_bytes=VMEM_LIMIT),
        cost_estimate=pl.CostEstimate(
            flops=6 * len(matrices) * matrices[0].size * width,
            bytes_accessed=4 * len(matrices) * matrices[0].size,
            transcendentals=0,
        ),
        name="packed_grams",
    )(*matrices)
    return packed


def gram_kernel(width, by_rows, matrix_ref, *gram_refs):
    for block, gram_ref in enumerate(gram_refs):
        place = slice(block * width, (block + 1) * width)
        if by_rows:
            gram_ref[...] = fine_dot(matrix_ref[place, :], matrix_ref[place, :], 1, 1)
        else:
            gram_ref[...] = fine_dot(matrix_ref[:, place], matrix_ref[:, place], 0, 0)


def block_grams(matrix, width, by_rows):
    count = matrix.shape[0 if by_rows else 1] // width
    return pl.pallas_call(
        functools.partial(gram_kernel, width, by_rows),
        out_shape=[jax.ShapeDtypeStruct((width, width), jnp.float32)] * count,
        compiler_params=pltpu.CompilerParams(vmem_limit_bytes=VMEM_LIMIT),
        cost_estimate=pl.CostEstimate(
            flops=12 * matrix.size * width, bytes_accessed=4 * matrix.size, transcendentals=0
        ),
        name="block_grams",
    )(matrix)


def newton_factor(gram):
    _, _, eye = eye_of(gram.shape[0])
    trace = jnp.sum(jnp.sum(gram * eye, axis=1, keepdims=True), axis=0, keepdims=True)
    inverse = 1.0 / (jnp.sqrt(trace) + 1e-07)
    gram = gram * inverse * inverse
    total = None
    for iteration in range(NS_ITERS):
        poly = NS_A * eye + NS_B * gram + NS_C * fine_dot(gram, gram)
        total = poly if total is None else fine_dot(total, poly)
        if iteration < NS_ITERS - 1:
            gram = fine_dot(fine_dot(poly, gram), poly)
    return total * inverse


def factor_kernel(own_ref, *refs):
    part_refs, factor_ref = refs[:-1], refs[-1]
    width = factor_ref.shape[0]

    @pl.when(own_ref[0] != 0)
    def _():
        total = 0.0
        for part_ref in part_refs:
            part = wide(part_ref[...])
            total = total + (part if part.ndim == 2 else jnp.sum(part, axis=0))
        _, _, eye = eye_of(width)
        packed = total[:width]
        gram = packed + packed.T + eye * (total[width : width + 1] - packed)
        factor_ref[...] = newton_factor(gram).astype(LOW)

    @pl.when(own_ref[0] == 0)
    def _():
        factor_ref[...] = jnp.zeros_like(factor_ref)


def block_factor(own, parts):
    width = parts[0].shape[-1]
    vmem = pl.BlockSpec(memory_space=pltpu.VMEM)
    return pl.pallas_call(
        factor_kernel,
        in_specs=[pl.BlockSpec(memory_space=pltpu.SMEM)] + [vmem] * len(parts),
        out_specs=vmem,
        out_shape=jax.ShapeDtypeStruct((width, width), LOW),
        compiler_params=pltpu.CompilerParams(vmem_limit_bytes=VMEM_LIMIT),
        cost_estimate=pl.CostEstimate(
            flops=100 * width**3, bytes_accessed=20 * width * width, transcendentals=0
        ),
        name="block_factor",
    )(own, *parts)


def apply_kernel(width, count, place_ref, matrix_ref, weight_ref, *refs):
    choice_refs, new_ref, factor_ref = refs[:-2], refs[-2], refs[-1]
    for block in range(count):
        for number, choice_ref in enumerate(choice_refs):

            @pl.when(place_ref[block] == number)
            def _(choice_ref=choice_ref):
                factor_ref[...] = choice_ref[...]

        rows = slice(block * width, (block + 1) * width)
        high, low = split(matrix_ref[rows, :])
        product = contract(factor_ref[...], high, 1, 0) + contract(factor_ref[...], low, 1, 0)
        new_ref[rows, :] = weight_ref[rows, :] - MUON_RATE * product


def apply_factors(matrix, weight, places, choices):
    width = choices[0].shape[0]
    count = matrix.shape[0] // width
    vmem = pl.BlockSpec(memory_space=pltpu.VMEM)
    return pl.pallas_call(
        functools.partial(apply_kernel, width, count),
        in_specs=[pl.BlockSpec(memory_space=pltpu.SMEM)] + [vmem] * (2 + len(choices)),
        out_specs=vmem,
        out_shape=jax.ShapeDtypeStruct(matrix.shape, jnp.float32),
        scratch_shapes=[pltpu.VMEM((width, width), LOW)],
        compiler_params=pltpu.CompilerParams(vmem_limit_bytes=VMEM_LIMIT),
        cost_estimate=pl.CostEstimate(
            flops=4 * matrix.size * width, bytes_accessed=12 * matrix.size, transcendentals=0
        ),
        name="apply_factors",
    )(places, matrix, weight, *choices)


def update_kernel(sizes, counts, *refs):
    firsts = [2 * len(sizes) + sum(counts[:n]) for n in range(len(sizes))]
    for number, (width, by_rows) in enumerate(sizes):
        matrix_ref, weight_ref = refs[2 * number], refs[2 * number + 1]
        part_refs = refs[firsts[number] : firsts[number] + counts[number]]
        new_ref = refs[2 * len(sizes) + sum(counts) + number]
        for block in range(part_refs[0].shape[0]):
            gram = part_refs[0][block]
            for part_ref in part_refs[1:]:
                gram = gram + part_ref[block]
            factor = newton_factor(gram)
            place = slice(block * width, (block + 1) * width)
            if by_rows:
                new_ref[place, :] = weight_ref[place, :] - MUON_RATE * fine_dot(
                    factor, matrix_ref[place, :]
                )
            else:
                new_ref[:, place] = weight_ref[:, place] - MUON_RATE * fine_dot(
                    matrix_ref[:, place], factor
                )


def gather_grams(moment, width, by_rows):
    grams = jnp.stack(block_grams(moment, width, by_rows))
    size = lax.axis_size("dp")
    return [grams] + [
        lax.ppermute(grams, "dp", [(i, (i + shift) % size) for i in range(size)])
        for shift in range(1, size)
    ]


def small_updates(items):
    vmem = pl.BlockSpec(memory_space=pltpu.VMEM)
    flat = [array for moment, weight, _, _, _ in items for array in (moment, weight)]
    flat = flat + [part for item in items for part in item[4]]
    counts = [len(item[4]) for item in items]
    return pl.pallas_call(
        functools.partial(update_kernel, [(item[2], item[3]) for item in items], counts),
        in_specs=[vmem] * len(flat),
        out_specs=[vmem] * len(items),
        out_shape=[jax.ShapeDtypeStruct(item[0].shape, jnp.float32) for item in items],
        compiler_params=pltpu.CompilerParams(vmem_limit_bytes=VMEM_LIMIT),
        cost_estimate=pl.CostEstimate(
            flops=sum(100 * item[4][0].size * item[2] for item in items),
            bytes_accessed=sum(12 * item[0].size for item in items),
            transcendentals=0,
        ),
        name="small_update",
    )(*flat)


def small_update(moment, weight, width, by_rows, parts=None):
    if parts is None:
        parts = gather_grams(moment, width, by_rows)
    return small_updates([(moment, weight, width, by_rows, parts)])[0]


def exchange(values, owners):
    size = lax.axis_size("dp")
    me = lax.axis_index("dp")
    parts = []
    for shift in range(size):
        target = (me + shift) % size
        part = values[0]
        for value, owner in zip(values[1:], owners[1:]):
            part = jnp.where(target == owner, value, part)
        if shift:
            pairs = [((o - shift) % size, o) for o in owners]
            part = lax.ppermute(part, "dp", pairs)
        parts.append(part)
    return parts


def share_out(factor, owners):
    size = lax.axis_size("dp")
    return [factor] + [
        lax.ppermute(factor, "dp", [(o, (o + shift) % size) for o in owners])
        for shift in range(1, size)
    ]


def back_factor_kernel(places, parts, *refs):
    own_ref, refs = refs[0], refs[1:]
    count = len(places)
    piece_refs, refs = refs[:count], refs[count:]
    rows_ref, part_refs = refs[0], refs[1 : 1 + parts]
    out_ref, factor_ref, weight_ref, sem_ref = refs[1 + parts :]
    copies = fetch_all(places, piece_refs, weight_ref, sem_ref)
    factor_kernel(own_ref, *part_refs, factor_ref)
    project_back_blocks(places, copies, rows_ref, out_ref, weight_ref)


def back_and_factor(rows, blocks, depth, own, parts):
    places, arrays = flat_pieces(blocks)
    size = len(blocks)
    height = max(first + count for _, first, count in places)
    width = arrays[0].shape[1]
    gram_width = parts[0].shape[-1]
    vmem = pl.BlockSpec(memory_space=pltpu.VMEM)
    return pl.pallas_call(
        functools.partial(back_factor_kernel, places, len(parts)),
        in_specs=[pl.BlockSpec(memory_space=pltpu.SMEM)]
        + [pl.BlockSpec(memory_space=pltpu.HBM)] * len(arrays)
        + [vmem] * (1 + len(parts)),
        out_specs=[vmem, vmem],
        out_shape=[
            jax.ShapeDtypeStruct((rows.shape[0], depth), jnp.float32),
            jax.ShapeDtypeStruct((gram_width, gram_width), LOW),
        ],
        scratch_shapes=[
            pltpu.VMEM((size, height, width), LOW),
            pltpu.SemaphoreType.DMA((len(arrays),)),
        ],
        compiler_params=pltpu.CompilerParams(vmem_limit_bytes=VMEM_MOST),
        cost_estimate=pl.CostEstimate(
            flops=2 * rows.size * depth + 100 * gram_width**3,
            bytes_accessed=2 * (size * height * width + 3 * rows.size),
            transcendentals=0,
        ),
        name="back_and_factor",
    )(own, *arrays, rows, *parts)


def is_owner(owners):
    me = lax.axis_index("dp")
    own = jnp.zeros((1,), jnp.int32)
    for o in owners:
        own = own + (me == o).astype(jnp.int32)
    return own


def owned_factor(parts, owners):
    return block_factor(is_owner(owners), parts)


def owned_update(moment, weight, choices, owners):
    size = lax.axis_size("dp")
    me = lax.axis_index("dp")
    places = jnp.stack([(me - o) % size for o in owners]).astype(jnp.int32)
    return apply_factors(moment, weight, places, choices)


def shards(
    inputs,
    cotangent,
    lengths,
    w_query,
    w_keyval,
    w_out,
    w_gate_up,
    w_down,
    gains,
    m_query,
    m_keyval,
    m_out,
    m_gate_up,
    m_down,
    m_gains,
):
    batches, own_rows, model_width = inputs.shape
    head_dim = w_keyval.shape[1] // 2
    half_dim = head_dim // 2
    units_here = w_down.shape[1]
    query_cols = w_query.shape[1]
    size = lax.axis_size("mp")
    me = lax.axis_index("mp")
    tokens = batches * own_rows
    seq_len = size * own_rows

    groups = lax.axis_size("dp")
    share = w_keyval.shape[0] // size

    def rows_of(value):
        return lax.all_gather(value, "dp", axis=0, tiled=False)

    gate_up_t = jnp.transpose(w_gate_up, (1, 2, 0))
    down_t = jnp.transpose(w_down)
    low_keyval = w_keyval.astype(LOW).reshape(-1, query_cols)
    query_block = rows_of(jnp.concatenate([w_query.astype(LOW), low_keyval], axis=0))
    out_block = rows_of(w_out.astype(LOW))
    full_gate = rows_of(gate_up_t[0].astype(LOW))
    full_up = rows_of(gate_up_t[1].astype(LOW))
    full_down = rows_of(down_t.astype(LOW))
    order = jnp.array(gather_order(size), jnp.int32)
    place = jnp.zeros((size,), jnp.int32).at[order].set(jnp.arange(size, dtype=jnp.int32))
    place = place[me ^ jnp.arange(size)]

    cot_rows = cotangent.reshape(tokens, model_width)
    cot = Gather(cot_rows, size)
    cot.first()
    full_keyval = query_block[:, w_query.shape[0] :].reshape(model_width, 2 * head_dim)
    query_block = query_block[:, : w_query.shape[0]].reshape(model_width, query_cols)
    own_positions = me * own_rows + jnp.arange(own_rows, dtype=jnp.int32)
    key_positions = jnp.concatenate(
        [(me ^ s) * own_rows + jnp.arange(own_rows, dtype=jnp.int32) for s in gather_order(size)]
    )
    qid = []
    kid = []
    offsets = []
    for batch_index in range(batches):
        own_segment, own_offset = doc_layout(lengths[batch_index], own_positions)
        key_segment, unused = doc_layout(lengths[batch_index], key_positions)
        qid.append(jnp.stack([own_segment, own_positions], axis=1))
        kid.append(jnp.stack([key_segment, key_positions], axis=0))
        offsets.append(own_offset)
    qid = jnp.stack(qid)
    kid = jnp.stack(kid)
    cosine, sine = rotary_tables(jnp.stack(offsets), half_dim)
    flat_cos = cosine.reshape(tokens, half_dim)
    flat_sin = sine.reshape(tokens, half_dim)

    x_rows = wide(inputs).reshape(tokens, model_width)
    x_scale = inverse_scale(x_rows)
    normed = (x_rows * x_scale * gains[0]).astype(LOW)
    own_keyval = plain_dot(normed, full_keyval)
    own_keyval = jnp.concatenate(
        [rotate(own_keyval[:, :head_dim], flat_cos, flat_sin), own_keyval[:, head_dim:]], axis=1
    ).astype(LOW)
    cot.parts, query_block = tie(cot.parts, query_block)
    query_gather = Gather(query_block, size)
    query_gather.first()
    own_keyval = query_gather.cut(own_keyval)
    flips = flips_of(size)
    keyval = own_keyval.reshape(1, batches, own_rows, 2 * head_dim)
    for flip in flips:
        keyval = jnp.concatenate([keyval, swap(keyval, flip, size)], axis=0)
        if flip == flips[-2]:
            keyval, cot.parts = tie(keyval, cot.parts)
            cot.relay()
    keyval = jnp.swapaxes(keyval, 0, 1).reshape(batches, seq_len, 2 * head_dim)
    query_gather.second()
    query_gather.relay()
    query_gather.parts, out_block = tie(query_gather.parts, out_block)
    out_gather = Gather(out_block.reshape(model_width, query_cols), size)
    out_gather.first()
    query_gather.third()
    query_pieces = query_gather.pieces()
    queries = project(normed, query_pieces, head_dim, (flat_cos, flat_sin))
    queries = queries.reshape(batches, own_rows, -1)
    done = ()
    for batch in range(batches):
        done = attention_forward(batch, queries, keyval, qid, kid, head_dim, done)
        if batch == 0:
            out_gather.parts, queries, done = tie(out_gather.parts, queries, done)
            out_gather.second()
            out_gather.relay()
    out_gather.parts, done, full_gate, cot.parts = tie(
        out_gather.parts, done, full_gate, cot.parts
    )
    out_gather.third()
    cot.second()
    context, logs = done
    context = context.reshape(tokens, -1)
    out_pieces = out_gather.pieces()
    mid = x_rows + project_back(context, out_pieces, model_width)
    mid_scale = inverse_scale(mid)
    normed_mid_rows = (mid * mid_scale * gains[1]).astype(LOW)
    mid_gather = Gather(normed_mid_rows, size)
    mid_gather.first()
    cot.third()
    full_cot = [in_steps(run, cot.pieces()) for run in range(2)]
    mid_gather.parts, full_cot[1], full_up = tie(mid_gather.parts, full_cot[1], full_up)
    mid_gather.second()
    mid_gather.relay()
    units = [None, None]
    units[1] = hidden_units(1, mid_gather.pieces(), full_gate, full_up)
    mid_gather.parts, units[1] = tie(mid_gather.parts, units[1])
    mid_gather.third()
    units[0] = hidden_units(0, mid_gather.pieces(), full_gate, full_up)
    normed_mid = [unit[0] for unit in units]
    (sum_down,) = units_sum([[unit[4] for unit in units]], full_cot, groups)
    sum_down, units = tie(sum_down, units)
    d_mid_sum = Scatter(size)
    steps = size // 2
    turned = []
    for run in range(2):
        _, gate, upward, _, _ = units[run]
        *grads, evens, odds = hidden_back(
            full_cot[run], gate, upward, full_gate, full_up, full_down, steps
        )
        turned.append(grads)
        if run == 0:
            odds, units = tie(odds, units)
        else:
            d_mid_sum.parts, odds = tie(d_mid_sum.parts, odds)
        d_mid_sum.first(evens, odds)
    turned = d_mid_sum.second(turned)

    def scatter_rows(value):
        return lax.psum_scatter(value, "dp", scatter_dimension=0, tiled=False)

    old_gate_up = jnp.transpose(m_gate_up, (1, 2, 0))
    old_down = jnp.transpose(m_down)
    grad_down = scatter_rows(sum_down)
    sum_gate, sum_up = units_sum(
        [[grads[0] for grads in turned], [grads[1] for grads in turned]], normed_mid, groups
    )
    d_mid_sum.parts, sum_gate, sum_up, grad_down = tie(
        d_mid_sum.parts, sum_gate, sum_up, grad_down
    )
    grad_gate = scatter_rows(sum_gate)
    grad_up = scatter_rows(sum_up)
    hidden = d_mid_sum.third([unit[3] for unit in units])
    mlp_sum = Scatter(size)
    mlp_parts = [hidden_out(part, full_down, steps) for part in hidden]
    d_mid_sum.parts, mlp_parts = tie(d_mid_sum.parts, mlp_parts)
    for evens, odds in mlp_parts:
        mlp_sum.first(evens, odds)
    d_mid_norm = d_mid_sum.total()
    d_mid = wide(cot_rows) + norm_back(d_mid_norm, mid, mid_scale, gains[1])
    gain_mid = jnp.sum(d_mid_norm * mid * mid_scale, axis=0)

    d_mid_low = d_mid.astype(LOW)
    out_sum = Scatter(size)
    out_parts = [blocks_sum(run, d_mid_low, context, size) for run in range(2)]
    mlp_sum.parts, out_parts, d_mid_low = tie(mlp_sum.parts, out_parts, d_mid_low)
    for evens, odds in out_parts:
        out_sum.first(evens, odds)
    d_mid_low = mlp_sum.second(d_mid_low)
    d_context = project(d_mid_low, out_pieces, head_dim).reshape(batches, own_rows, -1)
    out_sum.parts, d_context, grad_gate = tie(out_sum.parts, d_context, grad_gate)
    d_context = out_sum.second(d_context)
    fast = groups == 4 and units_here == 2 * FF_BLOCK
    grad_down = wide(grad_down)
    moment_down = DECAY * old_down + grad_down
    moment_gate = DECAY * old_gate_up[0] + wide(grad_gate)
    first_owners = (0, 1, 2, 3)
    last_owners = (1, 2)
    if fast:
        moment_down, moment_gate, d_context = tie(moment_down, moment_gate, d_context)
        slots = ((0, 0, 1), (0, 1, 2), (1, 0, 0), (1, 1, 3))
        first_parts = owners_parts((moment_down, moment_gate), FF_BLOCK, slots, groups)
        first_parts = lax.all_to_all(first_parts, "dp", 0, 0, tiled=True)
    backs = ()
    for batch in range(batches):
        backs = attention_backward(
            batch, queries, d_context, logs, keyval, qid, kid, cosine, sine, head_dim, backs
        )
        if batch == 0:
            backs, mlp_sum.parts, d_context = tie(backs, mlp_sum.parts, d_context)
            d_context = mlp_sum.third(d_context)
    if fast:
        backs, first_parts = tie(backs, first_parts)
    backs, out_sum.parts, grad_up = tie(backs, out_sum.parts, grad_up)
    d_queries, d_keyval = out_sum.third(backs)
    d_queries = d_queries.reshape(tokens, -1)

    def own_rows_of(total, width):
        return scatter_rows(total.astype(LOW).reshape(groups, -1, width))

    query_sum = Scatter(size)
    query_parts = [blocks_sum(run, normed, d_queries, size) for run in range(2)]
    for evens, odds in query_parts:
        query_sum.first(evens, odds)
    d_keyval = d_keyval.reshape(batches, size, own_rows, 2 * head_dim)
    d_keyval = jnp.swapaxes(d_keyval, 0, 1)[place]
    d_keyval = lax.all_to_all(d_keyval, "mp", 0, 0, tiled=True)
    output = (mid + mlp_sum.total()).astype(LOW).reshape(inputs.shape)
    moment_up = DECAY * old_gate_up[1] + wide(grad_up)
    own = is_owner(first_owners)
    query_parts, own, moment_up = tie(query_parts, own, moment_up)
    if fast:
        up_grams = owners_parts((moment_up,), FF_BLOCK, ((0, 0, 0), (0, 1, 1)), 2)
        query_sum.parts, up_grams, own = tie(query_sum.parts, up_grams, own)
        last_parts = exchange((up_grams[0], up_grams[1]), last_owners)
    out_sum.parts, own = tie(out_sum.parts, own)
    grad_out = own_rows_of(out_sum.total(), query_cols)
    if fast:
        own = query_sum.second(own)
        d_normed, first_factor = back_and_factor(
            d_queries, query_pieces, model_width, own, [first_parts]
        )
    else:
        d_queries = query_sum.second(d_queries)
        d_normed = project_back(d_queries, query_pieces, model_width)
    d_keyval, d_normed, query_sum.parts = tie(d_keyval, d_normed, query_sum.parts)
    d_normed = query_sum.third(d_normed)
    d_keyval = jnp.sum(wide(d_keyval), axis=0).reshape(tokens, 2 * head_dim)
    d_keyval = jnp.concatenate(
        [rotate(d_keyval[:, :head_dim], flat_cos, -flat_sin), d_keyval[:, head_dim:]], axis=1
    ).astype(LOW)
    sum_keyval = outer_sum(normed, d_keyval).astype(LOW)
    sum_keyval = jnp.swapaxes(sum_keyval.reshape(groups, size, share, 2 * head_dim), 0, 1)
    sum_keyval = lax.all_to_all(sum_keyval, "mp", 0, 0, tiled=True)
    if fast:
        last_parts, d_keyval = tie(last_parts, d_keyval)
        last_factor = owned_factor(last_parts, last_owners)
        query_sum.parts, last_factor, d_normed = tie(query_sum.parts, last_factor, d_normed)
        first_choices = share_out(first_factor, first_owners)
        last_choices = share_out(last_factor, last_owners)
    grad_query = own_rows_of(query_sum.total(), query_cols)
    d_normed = d_normed + rows_dot(d_keyval, full_keyval)
    input_grad = (d_mid + norm_back(d_normed, x_rows, x_scale, gains[0])).astype(LOW)
    input_grad = input_grad.reshape(inputs.shape)
    gain_input = jnp.sum(d_normed * x_rows * x_scale, axis=0)
    share_sums = jnp.sum(wide(sum_keyval), axis=0).astype(LOW)
    share_sums, input_grad = tie(share_sums, input_grad)
    share_parts = lax.all_to_all(share_sums, "dp", 0, 0, tiled=True)
    grad_out = wide(grad_out)
    moment_out = DECAY * m_out + grad_out
    out_grams = gather_grams(moment_out, head_dim, False)
    if fast:
        new_down = owned_update(moment_down, down_t, first_choices, (1, 2))
        new_gate = owned_update(moment_gate, gate_up_t[0], first_choices, (0, 3))
    else:
        new_down = small_update(moment_down, down_t, FF_BLOCK, True)
        new_gate = small_update(moment_gate, gate_up_t[0], FF_BLOCK, True)
    share_parts, new_down = tie(share_parts, new_down)
    grad_keyval = jnp.sum(wide(share_parts), axis=0)
    grad_keyval = gather_small(grad_keyval.astype(LOW), size)
    if fast:
        new_up = owned_update(moment_up, gate_up_t[1], last_choices, last_owners)
    else:
        new_up = small_update(moment_up, gate_up_t[1], FF_BLOCK, True)
    new_out = small_update(moment_out, w_out, head_dim, False, out_grams)
    grad_keyval, new_out, new_up = tie(grad_keyval, new_out, new_up)
    grad_keyval = wide(grad_keyval[place]).reshape(w_keyval.shape)
    moment_keyval = DECAY * m_keyval + grad_keyval
    keyval_grams = gather_grams(moment_keyval, 2 * head_dim, False)
    grad_query = wide(grad_query)
    moment_query = DECAY * m_query + grad_query
    query_grams = gather_grams(moment_query, head_dim, False)
    new_keyval, new_query = small_updates(
        [
            (moment_keyval, w_keyval, 2 * head_dim, False, keyval_grams),
            (moment_query, w_query, head_dim, False, query_grams),
        ]
    )
    grad_gains = add_all(add_all(jnp.stack([gain_input, gain_mid], axis=0), "mp"), "dp")
    grad_gate_up = wide(jnp.stack([grad_gate, grad_up]))
    moment_gate_up = DECAY * old_gate_up + grad_gate_up
    new_gate_up = jnp.stack([new_gate, new_up])

    def back(value):
        return jnp.transpose(value, (2, 0, 1))

    moment_gains = DECAY * m_gains + grad_gains
    new_gains = gains - GAIN_RATE * moment_gains
    return (
        output,
        input_grad,
        grad_query,
        grad_keyval,
        grad_out,
        back(grad_gate_up),
        jnp.transpose(grad_down),
        grad_gains,
        moment_query,
        moment_keyval,
        moment_out,
        back(moment_gate_up),
        jnp.transpose(moment_down),
        moment_gains,
        new_query,
        new_keyval,
        new_out,
        back(new_gate_up),
        jnp.transpose(new_down),
        new_gains,
    )


def solution(mesh):
    rows = P("dp", None)
    both = P("dp", "mp")
    tokens = P("dp", "mp", None)
    gate_up = P("dp", None, "mp")
    weights = (both, rows, both, gate_up, both, P())
    return jax.shard_map(
        shards,
        mesh=mesh,
        in_specs=(tokens, tokens, rows) + weights + weights,
        out_specs=(tokens, tokens) + weights + weights + weights,
        check_vma=False,
    )
```

```python
import functools

import jax
import jax.numpy as jnp
from jax import lax
from jax.experimental import pallas as pl
from jax.experimental.pallas import tpu as pltpu
from jax.sharding import PartitionSpec as P

FF_BLOCK = 352
NS_ITERS = 5
FORWARD_HEADS = 8
BACKWARD_HEADS = 4

EPS = 1e-05
THETA = 10000.0
NS_A = 3.4445
NS_B = -4.775
NS_C = 2.0315
MUON_RATE = 0.8
GAIN_RATE = 0.002
DECAY = 0.5
MASKED = -1e30
VMEM_LIMIT = 40 * 1024 * 1024
VMEM_MOST = 58 * 1024 * 1024
LOW = jnp.bfloat16


def doc_layout(doc_lengths, positions):
    ends = jnp.cumsum(doc_lengths)
    starts = ends - doc_lengths
    segment = jnp.sum((positions[:, None] >= ends[None, :]).astype(jnp.int32), axis=1)
    member = (
        segment[:, None] == jnp.arange(doc_lengths.shape[0], dtype=jnp.int32)[None, :]
    ).astype(jnp.int32)
    offset = positions - jnp.sum(member * starts[None, :], axis=1)
    return (segment, offset)


def rotary_tables(offset, half_dim):
    freqs = jnp.power(THETA, -jnp.arange(half_dim, dtype=jnp.float32) / half_dim)
    angle = offset.astype(jnp.float32)[..., None] * freqs
    return (jnp.cos(angle), jnp.sin(angle))


def rotate(vector, cosine, sine):
    half_dim = vector.shape[-1] // 2
    first_half = vector[..., :half_dim]
    second_half = vector[..., half_dim:]
    return jnp.concatenate(
        [first_half * cosine - second_half * sine, second_half * cosine + first_half * sine],
        axis=-1,
    )


def inverse_scale(vector):
    return lax.rsqrt(jnp.mean(vector * vector, axis=-1, keepdims=True) + EPS)


def norm_back(grad_rows, value_rows, scale_rows, gain_row):
    weighted = grad_rows * gain_row
    cubed = scale_rows * scale_rows * scale_rows
    return scale_rows * weighted - value_rows * cubed * jnp.mean(
        weighted * value_rows, axis=-1, keepdims=True
    )


def contract(left, right, left_dim, right_dim):
    return lax.dot_general(
        left,
        right,
        (((left_dim,), (right_dim,)), ((), ())),
        preferred_element_type=jnp.float32,
    )


def plain_dot(left, right):
    return contract(left, right, 1, 0)


def rows_dot(left, right):
    return contract(left, right, 1, 1)


def outer_sum(left, right):
    return contract(left, right, 0, 0)


def swap(value, flip, size):
    return lax.ppermute(value, "mp", [(i, i ^ flip) for i in range(size)])


def tie(*values):
    return lax.optimization_barrier(values)


class Gather:
    def __init__(self, value, size):
        self.size = size
        self.half = value.shape[0] // 2
        self.parts = {"own": value}
        self.cuts = []

    def swap(self, name, flip):
        return swap(self.parts[name], flip, self.size)

    def first(self):
        parts = self.parts
        if self.size != 8:
            for s in range(1, self.size):
                parts[str(s)] = self.swap("own", s)
            return
        parts["one"] = self.swap("own", 1)
        parts["two"] = self.swap("own", 2)
        parts["four"] = self.swap("own", 4)

    def cut(self, value):
        parts = self.parts
        if self.size != 8:
            return value
        top, low = parts["two"][: self.half], parts["four"][self.half :]
        self.cuts = list(tie(top, low, value))
        return self.cuts.pop()

    def second(self):
        parts = self.parts
        if self.size != 8:
            return
        if not self.cuts:
            self.cut(jnp.zeros((), jnp.float32))
        parts["six_top"] = swap(self.cuts[0], 4, self.size)
        parts["six_low"] = swap(self.cuts[1], 2, self.size)

    def relay(self):
        parts = self.parts
        if self.size != 8:
            return
        parts["three"] = self.swap("two", 1)
        parts["five"] = self.swap("four", 1)

    def third(self):
        parts = self.parts
        if self.size != 8:
            return
        parts["seven_top"] = self.swap("six_top", 1)
        parts["seven_low"] = self.swap("six_low", 1)

    def pieces(self):
        parts = self.parts
        if self.size != 8:
            return [[(0, parts["own"])]] + [[(0, parts[str(s)])] for s in range(1, self.size)]
        blocks = []
        for name in ("own", "one", "two", "three", "four", "five", "six", "seven"):
            if name in parts:
                blocks.append([(0, parts[name])])
            elif name + "_top" in parts:
                blocks.append([(0, parts[name + "_top"]), (self.half, parts[name + "_low"])])
            else:
                blocks.append([])
        return blocks


def flips_of(size):
    flips = [1 << bit for bit in range(size.bit_length() - 1)]
    return flips[1:] + flips[:1]


def gather_order(size):
    order = [0]
    for flip in flips_of(size):
        order = order + [s ^ flip for s in order]
    return order


def gather_small(value, size):
    value = value[None]
    for flip in flips_of(size):
        value = jnp.concatenate([value, swap(value, flip, size)], axis=0)
    return value


def scatter_small(parts, size):
    for flip in flips_of(size)[::-1]:
        half = parts.shape[0] // 2
        parts = wide(parts[:half]) + wide(swap(parts[half:].astype(LOW), flip, size))
    return parts[0]


def wide(value):
    return value.astype(jnp.float32)


def step_order(size):
    if size == 8:
        return [(3, 0), (1, 0), (3, 1), (2, 1)], [(1, 1), (2, 0), (0, 0), (0, 1)]
    steps = [(pair, half) for pair in range(size // 2) for half in range(2)]
    return steps[: len(steps) // 2], steps[len(steps) // 2 :]


class Scatter:
    def __init__(self, size):
        self.size = size
        self.runs = []
        self.parts = {}

    def first(self, evens, odds):
        self.runs.append((evens, odds))
        if self.size == 8:
            self.parts["core" + str(len(self.runs))] = swap(odds, 1, self.size)

    def second(self, later=None):
        if self.size != 8:
            steps = step_order(self.size)
            place = {step: (run, n) for run in (0, 1) for n, step in enumerate(steps[run])}
            total = 0.0
            for s in range(self.size):
                halves = []
                for half in (0, 1):
                    run, n = place[(s // 2, half)]
                    halves.append(self.runs[run][s % 2][n])
                part = jnp.concatenate(halves, axis=0)
                total = total + wide(swap(part, s, self.size) if s else part)
            self.parts["total"] = total
            return later
        evens, core = self.runs[0][0], self.parts.pop("core1")
        two = (wide(evens[:2]) + wide(core[:2])).astype(LOW)
        four = (wide(evens[2:]) + wide(core[2:])).astype(LOW)
        two, four, later = tie(two, four, later)
        self.parts["two"] = swap(two, 2, self.size)
        self.parts["four"] = swap(four, 4, self.size)
        return later

    def third(self, later=None):
        if self.size != 8:
            return later
        evens, core = self.runs[1][0], self.parts["core2"]
        low = wide(evens[0]) + wide(core[0]) + wide(self.parts["four"][0])
        top = wide(evens[1]) + wide(core[1]) + wide(self.parts["two"][0])
        low, top, later = tie(low.astype(LOW), top.astype(LOW), later)
        self.parts["low"] = swap(low, 2, self.size)
        self.parts["top"] = swap(top, 4, self.size)
        return later

    def total(self):
        parts = self.parts
        if self.size != 8:
            return parts["total"]
        evens, core = self.runs[1][0], parts["core2"]
        top = wide(evens[2]) + wide(core[2]) + wide(parts["two"][1]) + wide(parts["top"])
        low = wide(evens[3]) + wide(core[3]) + wide(parts["four"][1]) + wide(parts["low"])
        return jnp.concatenate([top, low], axis=0)


def as_rows(value, width):
    value = value.reshape(-1, width)
    high = value.astype(LOW)
    return jnp.concatenate([high, (value - wide(high)).astype(LOW)], axis=0)


def from_rows(rows):
    half = rows.shape[0] // 2
    return wide(rows[:half]) + wide(rows[half:])


def masked_bias(qid_ref, kid_ref):
    rows = qid_ref[0]
    keys = kid_ref[0]
    allowed = (rows[:, 0:1] == keys[0:1, :]) & (rows[:, 1:2] >= keys[1:2, :])
    return jnp.where(allowed, 0.0, MASKED)


def forward_kernel(heads, head_dim, q_ref, kv_ref, qid_ref, kid_ref, *refs):
    ctx_ref, log_ref, bias_ref, probs_ref = refs[-4:]

    @pl.when(pl.program_id(1) == 0)
    def _():
        bias_ref[...] = masked_bias(qid_ref, kid_ref)

    keys = kv_ref[0, :, :head_dim]
    values = kv_ref[0, :, head_dim:]
    rows = q_ref.shape[1]
    for head in range(heads):
        cols = slice(head * head_dim, (head + 1) * head_dim)
        scores = contract(q_ref[0, :, cols], keys, 1, 1) * head_dim ** (-0.5) + bias_ref[...]
        top = jnp.max(scores, axis=-1, keepdims=True)
        powers = jnp.exp(scores - top)
        total = jnp.sum(powers, axis=-1, keepdims=True)
        log_ref[0, :, cols] = jnp.broadcast_to(top + jnp.log(total), (rows, head_dim))
        probs_ref[head * rows : (head + 1) * rows] = (powers * (1.0 / total)).astype(LOW)
    context = contract(probs_ref[...], values, 1, 0).astype(LOW)
    for head in range(heads):
        cols = slice(head * head_dim, (head + 1) * head_dim)
        ctx_ref[0, :, cols] = context[head * rows : (head + 1) * rows]


def attention_forward(batch, queries, keyval, qid, kid, head_dim, earlier=()):
    all_batches, rows, width = queries.shape
    batches = 1
    seq_len = keyval.shape[1]
    heads = min(FORWARD_HEADS, width // head_dim)
    block = pl.BlockSpec((1, rows, heads * head_dim), lambda b, h: (batch, 0, h))
    work = batches * rows * width * seq_len
    return pl.pallas_call(
        functools.partial(forward_kernel, heads, head_dim),
        grid=(batches, width // (heads * head_dim)),
        in_specs=[
            block,
            pl.BlockSpec((1, seq_len, 2 * head_dim), lambda b, h: (batch, 0, 0)),
            pl.BlockSpec((1, rows, 2), lambda b, h: (batch, 0, 0)),
            pl.BlockSpec((1, 2, seq_len), lambda b, h: (batch, 0, 0)),
        ]
        + [pl.BlockSpec(memory_space=pltpu.HBM)] * len(earlier),
        out_specs=[block, block],
        out_shape=[
            jax.ShapeDtypeStruct((all_batches, rows, width), LOW),
            jax.ShapeDtypeStruct((all_batches, rows, width), jnp.float32),
        ],
        input_output_aliases={4 + n: n for n in range(len(earlier))},
        scratch_shapes=[
            pltpu.VMEM((rows, seq_len), jnp.float32),
            pltpu.VMEM((heads * rows, seq_len), LOW),
        ],
        compiler_params=pltpu.CompilerParams(vmem_limit_bytes=VMEM_LIMIT),
        cost_estimate=pl.CostEstimate(
            flops=8 * work, bytes_accessed=8 * batches * rows * width, transcendentals=work // head_dim
        ),
        name="attention_forward",
    )(queries, keyval, qid, kid, *earlier)


def backward_kernel(
    heads,
    head_dim,
    q_ref,
    dctx_ref,
    log_ref,
    kv_ref,
    qid_ref,
    kid_ref,
    cos_ref,
    sin_ref,
    *refs,
):
    dq_ref, out_ref, dkv_ref, bias_ref, probs_ref, ds_ref = refs[-6:]

    @pl.when(pl.program_id(1) == 0)
    def _():
        bias_ref[...] = masked_bias(qid_ref, kid_ref)
        dkv_ref[...] = jnp.zeros_like(dkv_ref)

    scale = head_dim ** (-0.5)
    half = head_dim // 2
    keys = kv_ref[0, :, :head_dim]
    values = kv_ref[0, :, head_dim:]
    cosine = cos_ref[0]
    sine = sin_ref[0]
    rows = q_ref.shape[1]
    for head in range(heads):
        cols = slice(head * head_dim, (head + 1) * head_dim)
        place = slice(head * rows, (head + 1) * rows)
        scores = contract(q_ref[0, :, cols], keys, 1, 1) * scale + bias_ref[...]
        probs = jnp.exp(scores - log_ref[0, :, head * head_dim : head * head_dim + 1])
        d_probs = contract(dctx_ref[0, :, cols], values, 1, 1)
        centre = jnp.sum(d_probs * probs, axis=-1, keepdims=True)
        ds_ref[place] = (probs * (d_probs - centre)).astype(LOW)
        probs_ref[place] = probs.astype(LOW)
    queries = jnp.concatenate(
        [q_ref[0, :, head * head_dim : (head + 1) * head_dim] for head in range(heads)], axis=0
    )
    d_context = jnp.concatenate(
        [dctx_ref[0, :, head * head_dim : (head + 1) * head_dim] for head in range(heads)], axis=0
    )
    dkv_ref[:, :head_dim] += contract(queries, ds_ref[...], 0, 0).T * scale
    dkv_ref[:, head_dim:] += contract(d_context, probs_ref[...], 0, 0).T
    d_query = contract(ds_ref[...], keys, 1, 0) * scale
    for head in range(heads):
        first = d_query[head * rows : (head + 1) * rows, :half]
        second = d_query[head * rows : (head + 1) * rows, half:]
        dq_ref[0, :, head * head_dim : (head + 1) * head_dim] = jnp.concatenate(
            [first * cosine + second * sine, second * cosine - first * sine], axis=1
        ).astype(LOW)

    @pl.when(pl.program_id(1) == pl.num_programs(1) - 1)
    def _():
        out_ref[0] = dkv_ref[...].astype(LOW)


def attention_backward(
    batch, queries, d_context, logs, keyval, qid, kid, cosine, sine, head_dim, earlier=()
):
    all_batches, rows, width = queries.shape
    batches = 1
    seq_len = keyval.shape[1]
    heads = min(BACKWARD_HEADS, width // head_dim)
    block = pl.BlockSpec((1, rows, heads * head_dim), lambda b, h: (batch, 0, h))
    work = batches * rows * width * seq_len

    def whole(*shape):
        return pl.BlockSpec((1,) + shape, lambda b, h: (batch, 0, 0))

    return pl.pallas_call(
        functools.partial(backward_kernel, heads, head_dim),
        grid=(batches, width // (heads * head_dim)),
        in_specs=[
            block,
            block,
            block,
            whole(seq_len, 2 * head_dim),
            whole(rows, 2),
            whole(2, seq_len),
            whole(rows, head_dim // 2),
            whole(rows, head_dim // 2),
        ]
        + [pl.BlockSpec(memory_space=pltpu.HBM)] * len(earlier),
        out_specs=[block, whole(seq_len, 2 * head_dim)],
        out_shape=[
            jax.ShapeDtypeStruct((all_batches, rows, width), LOW),
            jax.ShapeDtypeStruct((all_batches, seq_len, 2 * head_dim), LOW),
        ],
        input_output_aliases={8 + n: n for n in range(len(earlier))},
        scratch_shapes=[
            pltpu.VMEM((seq_len, 2 * head_dim), jnp.float32),
            pltpu.VMEM((rows, seq_len), jnp.float32),
            pltpu.VMEM((heads * rows, seq_len), LOW),
            pltpu.VMEM((heads * rows, seq_len), LOW),
        ],
        compiler_params=pltpu.CompilerParams(vmem_limit_bytes=VMEM_LIMIT),
        cost_estimate=pl.CostEstimate(
            flops=20 * work,
            bytes_accessed=12 * batches * rows * width,
            transcendentals=work // head_dim,
        ),
        name="attention_backward",
    )(queries, d_context, logs, keyval, qid, kid, cosine, sine, *earlier)


def flat_pieces(blocks):
    places = []
    arrays = []
    for number, pieces in enumerate(blocks):
        for first, rows in pieces:
            places.append((number, first, rows.shape[0]))
            arrays.append(rows)
    return places, arrays


def fetch_all(places, piece_refs, weight_ref, sem_ref):
    copies = []
    for number, (block, first, rows) in enumerate(places):
        copies.append(
            pltpu.make_async_copy(
                piece_refs[number],
                weight_ref.at[block, pl.ds(first, rows)],
                sem_ref.at[number],
            )
        )
    for copy in copies:
        copy.start()
    return copies


def project_kernel(places, head_dim, turned, turns, *refs):
    count = len(places)
    piece_refs, refs = refs[:count], refs[count:]
    if turned:
        rows_ref, cos_ref, sin_ref, out_ref, weight_ref, sem_ref = refs
    else:
        rows_ref, out_ref, weight_ref, sem_ref = refs
    copies = fetch_all(places, piece_refs, weight_ref, sem_ref)
    depth = rows_ref.shape[1]
    width = weight_ref.shape[2]
    half = head_dim // 2
    for block in range(weight_ref.shape[0]):
        for number, place in enumerate(places):
            if place[0] == block:
                copies[number].wait()
        product = contract(rows_ref[...], weight_ref[block, :depth], 1, 0)
        if turned:
            for head in range(width // head_dim):
                first = product[:, head * head_dim : head * head_dim + half]
                second = product[:, head * head_dim + half : (head + 1) * head_dim]
                cosine = cos_ref[...]
                sine = sin_ref[...]
                place = block * width + head * head_dim
                if turns is not None and place >= turns * head_dim:
                    out_ref[:, place : place + head_dim] = product[
                        :, head * head_dim : (head + 1) * head_dim
                    ].astype(LOW)
                    continue
                out_ref[:, place : place + head_dim] = jnp.concatenate(
                    [first * cosine - second * sine, second * cosine + first * sine], axis=1
                ).astype(LOW)
        else:
            out_ref[:, block * width : (block + 1) * width] = product.astype(LOW)


def project(rows, blocks, head_dim, tables=None, turns=None):
    places, arrays = flat_pieces(blocks)
    size = len(blocks)
    depth = max(first + count for _, first, count in places)
    width = arrays[0].shape[1]
    vmem = pl.BlockSpec(memory_space=pltpu.VMEM)
    turned = tables is not None
    return pl.pallas_call(
        functools.partial(project_kernel, places, head_dim, turned, turns),
        in_specs=[pl.BlockSpec(memory_space=pltpu.HBM)] * len(arrays) + [vmem] * (3 if turned else 1),
        out_specs=vmem,
        out_shape=jax.ShapeDtypeStruct((rows.shape[0], size * width), LOW),
        scratch_shapes=[
            pltpu.VMEM((size, depth, width), LOW),
            pltpu.SemaphoreType.DMA((len(arrays),)),
        ],
        compiler_params=pltpu.CompilerParams(vmem_limit_bytes=VMEM_LIMIT),
        cost_estimate=pl.CostEstimate(
            flops=2 * rows.size * size * width,
            bytes_accessed=2 * (size * depth * width + 2 * rows.size),
            transcendentals=0,
        ),
        name="project",
    )(*arrays, rows, *(tables if turned else ()))


def project_back_kernel(places, *refs):
    count = len(places)
    piece_refs, (rows_ref, out_ref, weight_ref, sem_ref) = refs[:count], refs[count:]
    copies = fetch_all(places, piece_refs, weight_ref, sem_ref)
    project_back_blocks(places, copies, rows_ref, out_ref, weight_ref)


def project_back_blocks(places, copies, rows_ref, out_ref, weight_ref):
    depth = out_ref.shape[1]
    width = weight_ref.shape[2]
    for block in range(weight_ref.shape[0]):
        for number, place in enumerate(places):
            if place[0] == block:
                copies[number].wait()
        product = contract(
            rows_ref[:, block * width : (block + 1) * width], weight_ref[block, :depth], 1, 1
        )
        if block == 0:
            out_ref[...] = product
        else:
            out_ref[...] += product


def project_back(rows, blocks, depth):
    places, arrays = flat_pieces(blocks)
    size = len(blocks)
    height = max(first + count for _, first, count in places)
    width = arrays[0].shape[1]
    vmem = pl.BlockSpec(memory_space=pltpu.VMEM)
    return pl.pallas_call(
        functools.partial(project_back_kernel, places),
        in_specs=[pl.BlockSpec(memory_space=pltpu.HBM)] * len(arrays) + [vmem],
        out_specs=vmem,
        out_shape=jax.ShapeDtypeStruct((rows.shape[0], depth), jnp.float32),
        scratch_shapes=[
            pltpu.VMEM((size, height, width), LOW),
            pltpu.SemaphoreType.DMA((len(arrays),)),
        ],
        compiler_params=pltpu.CompilerParams(vmem_limit_bytes=VMEM_LIMIT),
        cost_estimate=pl.CostEstimate(
            flops=2 * rows.size * depth,
            bytes_accessed=2 * (size * height * width + 3 * rows.size),
            transcendentals=0,
        ),
        name="project_back",
    )(*arrays, rows)


def beside(source_refs, weight_ref, sem_ref, whole=(), whole_ref=None):
    @pl.when(pl.program_id(0) == 0)
    def _():
        copies = []
        for number, source_ref in enumerate(source_refs):
            groups, _, chunk = source_ref.shape
            for group in range(groups):
                cols = pl.ds(group * chunk, chunk)
                copies.append(
                    pltpu.make_async_copy(
                        source_ref.at[group],
                        weight_ref.at[number, :, cols],
                        sem_ref.at[number, group],
                    )
                )
        for ref, number in whole:
            copies.append(
                pltpu.make_async_copy(
                    ref, whole_ref.at[number], sem_ref.at[len(source_refs) + number, 0]
                )
            )
        for copy in copies:
            copy.start()
        for copy in copies:
            copy.wait()


def hidden_kernel(places, steps_order, turn, *refs):
    count = len(places)
    piece_refs = refs[:count]
    source_refs = refs[count : count + 2]
    all_ref, gate_ref, up_ref, hidden_ref, turned_ref = refs[count + 2 : count + 7]
    slot_ref, weight_ref, sem_ref, weight_sem_ref = refs[count + 7 :]
    step = pl.program_id(0)
    steps = pl.num_programs(0)
    half = slot_ref.shape[1] // 2

    def each(number, act):
        slot = lax.rem(number, 2)
        for static, (pair, side) in enumerate(steps_order):

            @pl.when(number == static)
            def _(pair=pair, side=side):
                for parity in range(2):
                    block, start = 2 * pair + parity, side * half
                    for index, (owner, first, rows) in enumerate(places):
                        if owner == block and first <= start < first + rows:
                            act(
                                pltpu.make_async_copy(
                                    piece_refs[index].at[pl.ds(start - first, half)],
                                    slot_ref.at[slot, pl.ds(parity * half, half)],
                                    sem_ref.at[slot, parity],
                                )
                            )

    @pl.when(step == 0)
    def _():
        each(step, lambda copy: copy.start())

    @pl.when(step + 1 < steps)
    def _():
        each(step + 1, lambda copy: copy.start())

    beside(source_refs, weight_ref, weight_sem_ref)
    each(step, lambda copy: copy.wait())
    rows = slot_ref[lax.rem(step, 2)]
    all_ref[...] = rows
    gate = contract(rows, weight_ref[0], 1, 1)
    upward = contract(rows, weight_ref[1], 1, 1)
    gate_ref[...] = gate
    up_ref[...] = upward
    hidden = gate * jax.nn.sigmoid(gate) * upward
    hidden_ref[...] = hidden.astype(LOW)
    turned_ref[...] = (hidden.T if turn else hidden).astype(LOW)


def in_steps(run, blocks):
    half = sum(piece.shape[0] for _, piece in blocks[0]) // 2
    rows = []
    for pair, side in step_order(len(blocks))[run]:
        start = side * half
        for pieces in blocks[2 * pair : 2 * pair + 2]:
            for first, piece in pieces:
                if first <= start < first + piece.shape[0]:
                    rows.append(piece[start - first : start - first + half])
    return jnp.concatenate(rows, axis=0)


def hidden_units(run, blocks, full_gate, full_up):
    size = len(blocks)
    steps = step_order(size)[run]
    used = {2 * pair + parity for pair, _ in steps for parity in (0, 1)}
    places, arrays = flat_pieces([part if s in used else [] for s, part in enumerate(blocks)])
    rows = max(first + count for _, first, count in places)
    depth = arrays[0].shape[1]
    units = full_gate.shape[1]
    turn = rows % 128 == 0

    def block(width):
        return pl.BlockSpec((rows, width), lambda s: (s, 0))

    turned = pl.BlockSpec((units, rows), lambda s: (0, s)) if turn else block(units)
    turned_shape = (units, len(steps) * rows) if turn else (len(steps) * rows, units)
    return pl.pallas_call(
        functools.partial(hidden_kernel, places, steps, turn),
        grid=(len(steps),),
        in_specs=[pl.BlockSpec(memory_space=pltpu.HBM)] * (len(arrays) + 2),
        out_specs=[block(depth), block(units), block(units), block(units), turned],
        out_shape=[
            jax.ShapeDtypeStruct((len(steps) * rows, depth), LOW),
            jax.ShapeDtypeStruct((len(steps) * rows, units), jnp.float32),
            jax.ShapeDtypeStruct((len(steps) * rows, units), jnp.float32),
            jax.ShapeDtypeStruct((len(steps) * rows, units), LOW),
            jax.ShapeDtypeStruct(turned_shape, LOW),
        ],
        scratch_shapes=[
            pltpu.VMEM((2, rows, depth), LOW),
            pltpu.VMEM((2, units, depth), LOW),
            pltpu.SemaphoreType.DMA((2, 2)),
            pltpu.SemaphoreType.DMA((2, full_gate.shape[0])),
        ],
        compiler_params=pltpu.CompilerParams(vmem_limit_bytes=VMEM_LIMIT),
        cost_estimate=pl.CostEstimate(
            flops=4 * len(steps) * rows * depth * units,
            bytes_accessed=4 * len(steps) * rows * depth,
            transcendentals=len(steps) * rows * units,
        ),
        name="hidden_units",
    )(*arrays, full_gate, full_up)


def hidden_back_kernel(
    turn,
    cot_ref,
    gate_ref,
    up_ref,
    full_gate_ref,
    full_up_ref,
    source_ref,
    dg_ref,
    du_ref,
    even_ref,
    odd_ref,
    down_ref,
    both_ref,
    sem_ref,
):
    groups, _, chunk = full_gate_ref.shape
    beside([source_ref], down_ref, sem_ref, [(full_gate_ref, 0), (full_up_ref, 1)], both_ref)
    gate = gate_ref[...]
    upward = up_ref[...]
    sigma = jax.nn.sigmoid(gate)
    d_hidden = contract(cot_ref[...], down_ref[0], 1, 1)
    d_gate = d_hidden * upward * sigma * (1.0 + gate * (1.0 - sigma))
    d_up = d_hidden * gate * sigma
    dg_ref[...] = (d_gate.T if turn else d_gate).astype(LOW)
    du_ref[...] = (d_up.T if turn else d_up).astype(LOW)
    d_gate = d_gate.astype(LOW)
    d_up = d_up.astype(LOW)
    for group in range(groups):
        part = contract(d_gate, both_ref[0, group], 1, 0)
        part = (part + contract(d_up, both_ref[1, group], 1, 0)).astype(LOW)
        cols = slice(group * chunk, (group + 1) * chunk)
        even_ref[0, :, cols] = part[: part.shape[0] // 2]
        odd_ref[0, :, cols] = part[part.shape[0] // 2 :]


def hidden_back(cotangent, gate, upward, full_gate, full_up, down, steps):
    tokens, depth = cotangent.shape
    rows = tokens // steps
    units = gate.shape[1]
    turn = rows % 128 == 0

    def block(width):
        return pl.BlockSpec((rows, width), lambda s: (s, 0))

    if turn:
        turned = pl.BlockSpec((units, rows), lambda s: (0, s))
        turned_shape = (units, steps * rows)
    else:
        turned = pl.BlockSpec((rows, units), lambda s: (s, 0))
        turned_shape = (steps * rows, units)
    half = pl.BlockSpec((1, rows // 2, depth), lambda s: (s, 0, 0))
    return pl.pallas_call(
        functools.partial(hidden_back_kernel, turn),
        grid=(steps,),
        in_specs=[
            block(depth),
            block(units),
            block(units),
            pl.BlockSpec(memory_space=pltpu.HBM),
            pl.BlockSpec(memory_space=pltpu.HBM),
            pl.BlockSpec(memory_space=pltpu.HBM),
        ],
        out_specs=[turned, turned, half, half],
        out_shape=[
            jax.ShapeDtypeStruct(turned_shape, LOW),
            jax.ShapeDtypeStruct(turned_shape, LOW),
            jax.ShapeDtypeStruct((steps, rows // 2, depth), LOW),
            jax.ShapeDtypeStruct((steps, rows // 2, depth), LOW),
        ],
        scratch_shapes=[
            pltpu.VMEM((1, units, depth), LOW),
            pltpu.VMEM((2,) + full_gate.shape, LOW),
            pltpu.SemaphoreType.DMA((3, down.shape[0])),
        ],
        compiler_params=pltpu.CompilerParams(vmem_limit_bytes=VMEM_MOST),
        cost_estimate=pl.CostEstimate(
            flops=6 * steps * rows * depth * units,
            bytes_accessed=4 * steps * rows * depth,
            transcendentals=steps * rows * units,
        ),
        name="hidden_back",
    )(cotangent, gate, upward, full_gate, full_up, down)


def hidden_out_kernel(hidden_ref, down_ref, even_ref, odd_ref):
    groups, _, chunk = down_ref.shape
    for group in range(groups):
        part = contract(hidden_ref[...], down_ref[group], 1, 0).astype(LOW)
        cols = slice(group * chunk, (group + 1) * chunk)
        even_ref[0, :, cols] = part[: part.shape[0] // 2]
        odd_ref[0, :, cols] = part[part.shape[0] // 2 :]


def hidden_out(hidden, down, steps):
    tokens, units = hidden.shape
    rows = tokens // steps
    depth = down.shape[0] * down.shape[2]
    return pl.pallas_call(
        hidden_out_kernel,
        grid=(steps,),
        in_specs=[
            pl.BlockSpec((rows, units), lambda s: (s, 0)),
            pl.BlockSpec(down.shape, lambda s: (0, 0, 0), pipeline_mode=pl.Buffered(1)),
        ],
        out_specs=[pl.BlockSpec((1, rows // 2, depth), lambda s: (s, 0, 0))] * 2,
        out_shape=[jax.ShapeDtypeStruct((steps, rows // 2, depth), LOW)] * 2,
        compiler_params=pltpu.CompilerParams(vmem_limit_bytes=VMEM_LIMIT),
        cost_estimate=pl.CostEstimate(
            flops=2 * steps * rows * depth * units,
            bytes_accessed=2 * steps * rows * depth,
            transcendentals=0,
        ),
        name="hidden_out",
    )(hidden, down)


def units_sum_kernel(runs, turn, *refs):
    row_refs, refs = refs[:runs], refs[runs:]
    sums = len(refs) // (runs + 1)
    unit_refs, out_refs = refs[: runs * sums], refs[runs * sums :]
    for number, out_ref in enumerate(out_refs):
        total = 0.0
        for run, row_ref in enumerate(row_refs):
            unit_ref = unit_refs[number * runs + run]
            total = total + contract(unit_ref[...], row_ref[...], 1 if turn else 0, 0)
        out_ref[0] = total.astype(LOW)


def units_sum(units, rows, groups):
    tokens, depth = rows[0].shape
    turn = units[0][0].shape[1] == tokens
    width = units[0][0].shape[0 if turn else 1]
    chunk = depth // groups
    cut = 2
    flat = [part for parts in units for part in parts]
    out = pl.BlockSpec((1, width, chunk // cut), lambda s: (s // cut, 0, lax.rem(s, cut)))
    return pl.pallas_call(
        functools.partial(units_sum_kernel, len(rows), turn),
        grid=(groups * cut,),
        in_specs=[pl.BlockSpec((tokens, chunk // cut), lambda s: (0, s))] * len(rows)
        + [
            pl.BlockSpec(part.shape, lambda s: (0, 0), pipeline_mode=pl.Buffered(1))
            for part in flat
        ],
        out_specs=[out] * len(units),
        out_shape=[jax.ShapeDtypeStruct((groups, width, chunk), LOW)] * len(units),
        compiler_params=pltpu.CompilerParams(vmem_limit_bytes=VMEM_LIMIT),
        cost_estimate=pl.CostEstimate(
            flops=2 * len(flat) * tokens * depth * width,
            bytes_accessed=2 * len(flat) * tokens * (depth + width),
            transcendentals=0,
        ),
        name="units_sum",
    )(*rows, *flat)


def pick(values, index):
    value = values[0]
    for number in range(1, len(values)):
        value = jnp.where(index == number, values[number], value)
    return value


def blocks_sum_kernel(row_ref, col_ref, even_ref, odd_ref):
    part = contract(row_ref[...], col_ref[...], 0, 0).astype(LOW)
    even_ref[0] = part[:, : part.shape[1] // 2]
    odd_ref[0] = part[:, part.shape[1] // 2 :]


def blocks_sum(run, rows, cols, size):
    tokens, depth = rows.shape
    width = cols.shape[1] // size
    order = step_order(size)[run]
    pairs = [pair for pair, _ in order]
    sides = [side for _, side in order]
    return pl.pallas_call(
        blocks_sum_kernel,
        grid=(len(order),),
        in_specs=[
            pl.BlockSpec((tokens, depth // 2), lambda s: (0, pick(sides, s))),
            pl.BlockSpec((tokens, 2 * width), lambda s: (0, pick(pairs, s))),
        ],
        out_specs=[pl.BlockSpec((1, depth // 2, width), lambda s: (s, 0, 0))] * 2,
        out_shape=[jax.ShapeDtypeStruct((len(order), depth // 2, width), LOW)] * 2,
        compiler_params=pltpu.CompilerParams(vmem_limit_bytes=VMEM_LIMIT),
        cost_estimate=pl.CostEstimate(
            flops=tokens * depth * len(order) * 2 * width,
            bytes_accessed=2 * depth * len(order) * width,
            transcendentals=0,
        ),
        name="blocks_sum",
    )(rows, cols)


def split(value):
    high = value.astype(LOW)
    return high, (value - wide(high)).astype(LOW)


def fine_dot(left, right, left_dim=1, right_dim=0):
    left_high, left_low = split(left)
    right_high, right_low = split(right)
    small = contract(left_high, right_low, left_dim, right_dim)
    small = small + contract(left_low, right_high, left_dim, right_dim)
    return contract(left_high, right_high, left_dim, right_dim) + small


def eye_of(width):
    row = lax.broadcasted_iota(jnp.int32, (width, width), 0)
    col = lax.broadcasted_iota(jnp.int32, (width, width), 1)
    return row, col, jnp.where(row == col, 1.0, 0.0)


def pack(gram):
    row, col, eye = eye_of(gram.shape[0])
    high = wide(gram.astype(LOW))
    low = gram - high
    packed = jnp.where(col >= row, high, low).astype(LOW)
    return packed, jnp.sum(low * eye, axis=0, keepdims=True)


def unpack(total):
    width = total.shape[1]
    _, _, eye = eye_of(width)
    packed = total[:width]
    return packed + packed.T + eye * (total[width : width + 1] - packed)


def packed_kernel(width, slots, by_rows, *refs):
    matrix_refs, out_ref = refs[:-1], refs[-1]
    for slot in range(out_ref.shape[0]):
        if slot not in [used for _, _, used in slots]:
            out_ref[slot] = jnp.zeros_like(out_ref[slot])
    for number, block, slot in slots:
        place = slice(block * width, (block + 1) * width)
        if by_rows:
            part = matrix_refs[number][place, :]
            packed, last = pack(fine_dot(part, part, 1, 1))
        else:
            part = matrix_refs[number][:, place]
            packed, last = pack(fine_dot(part, part, 0, 0))
        out_ref[slot, :width, :] = packed
        out_ref[slot, width:, :] = jnp.broadcast_to(
            last, (out_ref.shape[1] - width, width)
        ).astype(LOW)


def packed_grams(matrices, width, slots, size, by_rows=True):
    return pl.pallas_call(
        functools.partial(packed_kernel, width, slots, by_rows),
        out_shape=jax.ShapeDtypeStruct((size, width + 16, width), LOW),
        compiler_params=pltpu.CompilerParams(vmem_limit_bytes=VMEM_LIMIT),
        cost_estimate=pl.CostEstimate(
            flops=6 * len(matrices) * matrices[0].size * width,
            bytes_accessed=4 * len(matrices) * matrices[0].size,
            transcendentals=0,
        ),
        name="packed_grams",
    )(*matrices)


def newton_factor(gram):
    _, _, eye = eye_of(gram.shape[0])
    trace = jnp.sum(jnp.sum(gram * eye, axis=1, keepdims=True), axis=0, keepdims=True)
    inverse = 1.0 / (jnp.sqrt(trace) + 1e-07)
    gram = gram * inverse * inverse
    total = None
    for iteration in range(NS_ITERS):
        poly = NS_A * eye + NS_B * gram + NS_C * fine_dot(gram, gram)
        total = poly if total is None else fine_dot(total, poly)
        if iteration < NS_ITERS - 1:
            gram = fine_dot(fine_dot(poly, gram), poly)
    return total * inverse


def factor_kernel(own_ref, *refs):
    part_refs, factor_ref = refs[:-1], refs[-1]
    width = factor_ref.shape[0]

    @pl.when(own_ref[0] != 0)
    def _():
        total = 0.0
        for part_ref in part_refs:
            part = wide(part_ref[...])
            total = total + (part if part.ndim == 2 else jnp.sum(part, axis=0))
        factor_ref[...] = newton_factor(unpack(total)).astype(LOW)

    @pl.when(own_ref[0] == 0)
    def _():
        factor_ref[...] = jnp.zeros_like(factor_ref)


def block_factor(own, parts):
    width = parts[0].shape[-1]
    vmem = pl.BlockSpec(memory_space=pltpu.VMEM)
    return pl.pallas_call(
        factor_kernel,
        in_specs=[pl.BlockSpec(memory_space=pltpu.SMEM)] + [vmem] * len(parts),
        out_specs=vmem,
        out_shape=jax.ShapeDtypeStruct((width, width), LOW),
        compiler_params=pltpu.CompilerParams(vmem_limit_bytes=VMEM_LIMIT),
        cost_estimate=pl.CostEstimate(
            flops=100 * width**3, bytes_accessed=20 * width * width, transcendentals=0
        ),
        name="block_factor",
    )(own, *parts)


def apply_kernel(width, count, place_ref, matrix_ref, weight_ref, *refs):
    choice_refs, new_ref, factor_ref = refs[:-2], refs[-2], refs[-1]
    for block in range(count):
        for number, choice_ref in enumerate(choice_refs):

            @pl.when(place_ref[block] == number)
            def _(choice_ref=choice_ref):
                factor_ref[...] = choice_ref[...]

        rows = slice(block * width, (block + 1) * width)
        high, low = split(matrix_ref[rows, :])
        product = contract(factor_ref[...], high, 1, 0) + contract(factor_ref[...], low, 1, 0)
        new_ref[rows, :] = weight_ref[rows, :] - MUON_RATE * product


def apply_factors(matrix, weight, places, choices):
    width = choices[0].shape[0]
    count = matrix.shape[0] // width
    vmem = pl.BlockSpec(memory_space=pltpu.VMEM)
    return pl.pallas_call(
        functools.partial(apply_kernel, width, count),
        in_specs=[pl.BlockSpec(memory_space=pltpu.SMEM)] + [vmem] * (2 + len(choices)),
        out_specs=vmem,
        out_shape=jax.ShapeDtypeStruct(matrix.shape, jnp.float32),
        scratch_shapes=[pltpu.VMEM((width, width), LOW)],
        compiler_params=pltpu.CompilerParams(vmem_limit_bytes=VMEM_LIMIT),
        cost_estimate=pl.CostEstimate(
            flops=4 * matrix.size * width, bytes_accessed=12 * matrix.size, transcendentals=0
        ),
        name="apply_factors",
    )(places, matrix, weight, *choices)


def update_kernel(sizes, counts, *refs):
    firsts = [2 * len(sizes) + sum(counts[:n]) for n in range(len(sizes))]
    for number, (width, by_rows) in enumerate(sizes):
        matrix_ref, weight_ref = refs[2 * number], refs[2 * number + 1]
        part_refs = refs[firsts[number] : firsts[number] + counts[number]]
        new_ref = refs[2 * len(sizes) + sum(counts) + number]
        for block in range(part_refs[0].shape[0]):
            total = 0.0
            for part_ref in part_refs:
                total = total + wide(part_ref[block])
            factor = newton_factor(unpack(total))
            place = slice(block * width, (block + 1) * width)
            if by_rows:
                new_ref[place, :] = weight_ref[place, :] - MUON_RATE * fine_dot(
                    factor, matrix_ref[place, :]
                )
            else:
                new_ref[:, place] = weight_ref[:, place] - MUON_RATE * fine_dot(
                    matrix_ref[:, place], factor
                )


def gather_grams(moment, width, by_rows):
    count = moment.shape[0 if by_rows else 1] // width
    slots = tuple((0, block, block) for block in range(count))
    grams = packed_grams((moment,), width, slots, count, by_rows)
    size = lax.axis_size("dp")
    return [grams] + [
        lax.ppermute(grams, "dp", [(i, (i + shift) % size) for i in range(size)])
        for shift in range(1, size)
    ]


def small_updates(items):
    vmem = pl.BlockSpec(memory_space=pltpu.VMEM)
    flat = [array for moment, weight, _, _, _ in items for array in (moment, weight)]
    flat = flat + [part for item in items for part in item[4]]
    counts = [len(item[4]) for item in items]
    return pl.pallas_call(
        functools.partial(update_kernel, [(item[2], item[3]) for item in items], counts),
        in_specs=[vmem] * len(flat),
        out_specs=[vmem] * len(items),
        out_shape=[jax.ShapeDtypeStruct(item[0].shape, jnp.float32) for item in items],
        compiler_params=pltpu.CompilerParams(vmem_limit_bytes=VMEM_LIMIT),
        cost_estimate=pl.CostEstimate(
            flops=sum(100 * item[4][0].size * item[2] for item in items),
            bytes_accessed=sum(12 * item[0].size for item in items),
            transcendentals=0,
        ),
        name="small_update",
    )(*flat)


def small_update(moment, weight, width, by_rows, parts=None):
    if parts is None:
        parts = gather_grams(moment, width, by_rows)
    return small_updates([(moment, weight, width, by_rows, parts)])[0]


def exchange(values, owners):
    size = lax.axis_size("dp")
    me = lax.axis_index("dp")
    parts = []
    for shift in range(size):
        target = (me + shift) % size
        part = values[0]
        for value, owner in zip(values[1:], owners[1:]):
            part = jnp.where(target == owner, value, part)
        if shift:
            pairs = [((o - shift) % size, o) for o in owners]
            part = lax.ppermute(part, "dp", pairs)
        parts.append(part)
    return parts


def share_out(factor, owners):
    size = lax.axis_size("dp")
    return [factor] + [
        lax.ppermute(factor, "dp", [(o, (o + shift) % size) for o in owners])
        for shift in range(1, size)
    ]


def back_factor_kernel(places, parts, *refs):
    own_ref, refs = refs[0], refs[1:]
    count = len(places)
    piece_refs, refs = refs[:count], refs[count:]
    rows_ref, part_refs = refs[0], refs[1 : 1 + parts]
    out_ref, factor_ref, weight_ref, sem_ref = refs[1 + parts :]
    copies = fetch_all(places, piece_refs, weight_ref, sem_ref)
    factor_kernel(own_ref, *part_refs, factor_ref)
    project_back_blocks(places, copies, rows_ref, out_ref, weight_ref)


def back_and_factor(rows, blocks, depth, own, parts):
    places, arrays = flat_pieces(blocks)
    size = len(blocks)
    height = max(first + count for _, first, count in places)
    width = arrays[0].shape[1]
    gram_width = parts[0].shape[-1]
    vmem = pl.BlockSpec(memory_space=pltpu.VMEM)
    return pl.pallas_call(
        functools.partial(back_factor_kernel, places, len(parts)),
        in_specs=[pl.BlockSpec(memory_space=pltpu.SMEM)]
        + [pl.BlockSpec(memory_space=pltpu.HBM)] * len(arrays)
        + [vmem] * (1 + len(parts)),
        out_specs=[vmem, vmem],
        out_shape=[
            jax.ShapeDtypeStruct((rows.shape[0], depth), jnp.float32),
            jax.ShapeDtypeStruct((gram_width, gram_width), LOW),
        ],
        scratch_shapes=[
            pltpu.VMEM((size, height, width), LOW),
            pltpu.SemaphoreType.DMA((len(arrays),)),
        ],
        compiler_params=pltpu.CompilerParams(vmem_limit_bytes=VMEM_MOST),
        cost_estimate=pl.CostEstimate(
            flops=2 * rows.size * depth + 100 * gram_width**3,
            bytes_accessed=2 * (size * height * width + 3 * rows.size),
            transcendentals=0,
        ),
        name="back_and_factor",
    )(own, *arrays, rows, *parts)


def is_owner(owners):
    me = lax.axis_index("dp")
    own = jnp.zeros((1,), jnp.int32)
    for o in owners:
        own = own + (me == o).astype(jnp.int32)
    return own


def owned_factor(parts, owners):
    return block_factor(is_owner(owners), parts)


def owned_update(moment, weight, choices, owners):
    size = lax.axis_size("dp")
    me = lax.axis_index("dp")
    places = jnp.stack([(me - o) % size for o in owners]).astype(jnp.int32)
    return apply_factors(moment, weight, places, choices)


def shards(
    inputs,
    cotangent,
    lengths,
    w_query,
    w_keyval,
    w_out,
    w_gate_up,
    w_down,
    gains,
    m_query,
    m_keyval,
    m_out,
    m_gate_up,
    m_down,
    m_gains,
):
    batches, own_rows, model_width = inputs.shape
    head_dim = w_keyval.shape[1] // 2
    half_dim = head_dim // 2
    units_here = w_down.shape[1]
    query_cols = w_query.shape[1]
    size = lax.axis_size("mp")
    me = lax.axis_index("mp")
    tokens = batches * own_rows
    seq_len = size * own_rows

    groups = lax.axis_size("dp")
    share = w_keyval.shape[0] // size

    def rows_of(value):
        return lax.all_gather(value, "dp", axis=0, tiled=False)

    gate_up_t = jnp.transpose(w_gate_up, (1, 2, 0))
    down_t = jnp.transpose(w_down)
    cot_rows = cotangent.reshape(tokens, model_width)
    cot = Gather(cot_rows, size)
    cot.first()
    query_block = rows_of(w_query.astype(LOW))
    own_positions = me * own_rows + jnp.arange(own_rows, dtype=jnp.int32)
    key_positions = jnp.concatenate(
        [(me ^ s) * own_rows + jnp.arange(own_rows, dtype=jnp.int32) for s in gather_order(size)]
    )
    qid = []
    kid = []
    offsets = []
    for batch_index in range(batches):
        own_segment, own_offset = doc_layout(lengths[batch_index], own_positions)
        key_segment, unused = doc_layout(lengths[batch_index], key_positions)
        qid.append(jnp.stack([own_segment, own_positions], axis=1))
        kid.append(jnp.stack([key_segment, key_positions], axis=0))
        offsets.append(own_offset)
    qid = jnp.stack(qid)
    kid = jnp.stack(kid)
    cosine, sine = rotary_tables(jnp.stack(offsets), half_dim)
    flat_cos = cosine.reshape(tokens, half_dim)
    flat_sin = sine.reshape(tokens, half_dim)

    x_rows = wide(inputs).reshape(tokens, model_width)
    x_scale = inverse_scale(x_rows)
    normed = (x_rows * x_scale * gains[0]).astype(LOW)
    cot.parts, query_block, low_keyval, normed, flat_cos, flat_sin, qid, kid = tie(
        cot.parts, query_block, w_keyval.astype(LOW), normed, flat_cos, flat_sin, qid, kid
    )
    full_keyval = rows_of(low_keyval)
    query_gather = Gather(query_block.reshape(model_width, query_cols), size)
    query_gather.first()
    full_keyval, query_gather.parts, low_out = tie(
        full_keyval, query_gather.parts, w_out.astype(LOW)
    )
    query_gather.second()
    out_block = rows_of(low_out)
    full_gate = rows_of(gate_up_t[0].astype(LOW))
    full_up = rows_of(gate_up_t[1].astype(LOW))
    full_down = rows_of(down_t.astype(LOW))
    order = jnp.array(gather_order(size), jnp.int32)
    place = jnp.zeros((size,), jnp.int32).at[order].set(jnp.arange(size, dtype=jnp.int32))
    place = place[me ^ jnp.arange(size)]

    full_keyval = full_keyval.reshape(model_width, 2 * head_dim)
    own_keyval = project(normed, [[(0, full_keyval)]], head_dim, (flat_cos, flat_sin), 1)
    query_gather.parts, own_keyval = tie(query_gather.parts, own_keyval)
    flips = flips_of(size)
    keyval = own_keyval.reshape(1, batches, own_rows, 2 * head_dim)
    for flip in flips:
        keyval = jnp.concatenate([keyval, swap(keyval, flip, size)], axis=0)
        if flip == flips[-2]:
            keyval, cot.parts = tie(keyval, cot.parts)
            cot.relay()
    keyval = jnp.swapaxes(keyval, 0, 1).reshape(batches, seq_len, 2 * head_dim)
    query_gather.relay()
    query_gather.parts, out_block = tie(query_gather.parts, out_block)
    out_gather = Gather(out_block.reshape(model_width, query_cols), size)
    out_gather.first()
    query_gather.third()
    query_pieces = query_gather.pieces()
    queries = project(normed, query_pieces, head_dim, (flat_cos, flat_sin))
    queries = queries.reshape(batches, own_rows, -1)
    done = ()
    for batch in range(batches):
        done = attention_forward(batch, queries, keyval, qid, kid, head_dim, done)
        if batch == 0:
            out_gather.parts, queries, done = tie(out_gather.parts, queries, done)
            out_gather.second()
            out_gather.relay()
    out_gather.parts, done, full_gate, cot.parts = tie(
        out_gather.parts, done, full_gate, cot.parts
    )
    out_gather.third()
    cot.second()
    context, logs = done
    context = context.reshape(tokens, -1)
    out_pieces = out_gather.pieces()
    mid = x_rows + project_back(context, out_pieces, model_width)
    mid_scale = inverse_scale(mid)
    normed_mid_rows = (mid * mid_scale * gains[1]).astype(LOW)
    mid_gather = Gather(normed_mid_rows, size)
    mid_gather.first()
    cot.third()
    full_cot = [in_steps(run, cot.pieces()) for run in range(2)]
    mid_gather.parts, full_cot[1], full_up = tie(mid_gather.parts, full_cot[1], full_up)
    mid_gather.second()
    mid_gather.relay()
    units = [None, None]
    units[1] = hidden_units(1, mid_gather.pieces(), full_gate, full_up)
    mid_gather.parts, units[1] = tie(mid_gather.parts, units[1])
    mid_gather.third()
    units[0] = hidden_units(0, mid_gather.pieces(), full_gate, full_up)
    normed_mid = [unit[0] for unit in units]
    (sum_down,) = units_sum([[unit[4] for unit in units]], full_cot, groups)
    sum_down, units = tie(sum_down, units)
    d_mid_sum = Scatter(size)
    steps = size // 2
    turned = []
    for run in range(2):
        _, gate, upward, _, _ = units[run]
        *grads, evens, odds = hidden_back(
            full_cot[run], gate, upward, full_gate, full_up, full_down, steps
        )
        turned.append(grads)
        if run == 0:
            odds, units = tie(odds, units)
        else:
            d_mid_sum.parts, odds = tie(d_mid_sum.parts, odds)
        d_mid_sum.first(evens, odds)
    turned = d_mid_sum.second(turned)

    def scatter_rows(value):
        return lax.psum_scatter(value, "dp", scatter_dimension=0, tiled=False)

    old_gate_up = jnp.transpose(m_gate_up, (1, 2, 0))
    old_down = jnp.transpose(m_down)
    grad_down = scatter_rows(sum_down)
    sum_gate, sum_up = units_sum(
        [[grads[0] for grads in turned], [grads[1] for grads in turned]], normed_mid, groups
    )
    d_mid_sum.parts, sum_gate, sum_up, grad_down = tie(
        d_mid_sum.parts, sum_gate, sum_up, grad_down
    )
    grad_gate = scatter_rows(sum_gate)
    grad_up = scatter_rows(sum_up)
    hidden = d_mid_sum.third([unit[3] for unit in units])
    mlp_sum = Scatter(size)
    mlp_parts = [hidden_out(part, full_down, steps) for part in hidden]
    d_mid_sum.parts, mlp_parts = tie(d_mid_sum.parts, mlp_parts)
    for evens, odds in mlp_parts:
        mlp_sum.first(evens, odds)
    d_mid_norm = d_mid_sum.total()
    d_mid = wide(cot_rows) + norm_back(d_mid_norm, mid, mid_scale, gains[1])
    gain_mid = jnp.sum(d_mid_norm * mid * mid_scale, axis=0)

    d_mid_low = d_mid.astype(LOW)
    out_sum = Scatter(size)
    out_parts = [blocks_sum(run, d_mid_low, context, size) for run in range(2)]
    mlp_sum.parts, out_parts, d_mid_low = tie(mlp_sum.parts, out_parts, d_mid_low)
    for evens, odds in out_parts:
        out_sum.first(evens, odds)
    d_mid_low = mlp_sum.second(d_mid_low)
    d_context = project(d_mid_low, out_pieces, head_dim).reshape(batches, own_rows, -1)
    out_sum.parts, d_context, grad_gate = tie(out_sum.parts, d_context, grad_gate)
    d_context = out_sum.second(d_context)
    fast = groups == 4 and units_here == 2 * FF_BLOCK
    grad_down = wide(grad_down)
    moment_down = DECAY * old_down + grad_down
    moment_gate = DECAY * old_gate_up[0] + wide(grad_gate)
    first_owners = (0, 1, 2, 3)
    last_owners = (1, 2)
    if fast:
        moment_down, moment_gate, d_context = tie(moment_down, moment_gate, d_context)
        slots = ((0, 0, 1), (0, 1, 2), (1, 0, 0), (1, 1, 3))
        first_parts = packed_grams((moment_down, moment_gate), FF_BLOCK, slots, groups)
        first_parts = lax.all_to_all(first_parts, "dp", 0, 0, tiled=True)
    backs = ()
    for batch in range(batches):
        backs = attention_backward(
            batch, queries, d_context, logs, keyval, qid, kid, cosine, sine, head_dim, backs
        )
        if batch == 0:
            backs, mlp_sum.parts, d_context = tie(backs, mlp_sum.parts, d_context)
            d_context = mlp_sum.third(d_context)
    if fast:
        backs, first_parts = tie(backs, first_parts)
    backs, out_sum.parts, grad_up = tie(backs, out_sum.parts, grad_up)
    d_queries, d_keyval = out_sum.third(backs)
    d_queries = d_queries.reshape(tokens, -1)

    def own_rows_of(total, width):
        return scatter_rows(total.astype(LOW).reshape(groups, -1, width))

    query_sum = Scatter(size)
    query_parts = [blocks_sum(run, normed, d_queries, size) for run in range(2)]
    for evens, odds in query_parts:
        query_sum.first(evens, odds)
    d_keyval = d_keyval.reshape(batches, size, own_rows, 2 * head_dim)
    d_keyval = jnp.swapaxes(d_keyval, 0, 1)[place]
    d_keyval = lax.all_to_all(d_keyval, "mp", 0, 0, tiled=True)
    output = (mid + mlp_sum.total()).astype(LOW).reshape(inputs.shape)
    moment_up = DECAY * old_gate_up[1] + wide(grad_up)
    own = is_owner(first_owners)
    query_parts, own, moment_up = tie(query_parts, own, moment_up)
    if fast:
        up_grams = packed_grams((moment_up,), FF_BLOCK, ((0, 0, 0), (0, 1, 1)), 2)
        query_sum.parts, up_grams, own = tie(query_sum.parts, up_grams, own)
        last_parts = exchange((up_grams[0], up_grams[1]), last_owners)
    out_sum.parts, own = tie(out_sum.parts, own)
    grad_out = own_rows_of(out_sum.total(), query_cols)
    if fast:
        own = query_sum.second(own)
        d_normed, first_factor = back_and_factor(
            d_queries, query_pieces, model_width, own, [first_parts]
        )
    else:
        d_queries = query_sum.second(d_queries)
        d_normed = project_back(d_queries, query_pieces, model_width)
    d_keyval, d_normed, query_sum.parts = tie(d_keyval, d_normed, query_sum.parts)
    d_normed = query_sum.third(d_normed)
    if fast:
        first_choices = share_out(first_factor, first_owners)
    d_keyval = jnp.sum(wide(d_keyval), axis=0).reshape(tokens, 2 * head_dim)
    d_keyval = jnp.concatenate(
        [rotate(d_keyval[:, :head_dim], flat_cos, -flat_sin), d_keyval[:, head_dim:]], axis=1
    ).astype(LOW)
    sum_keyval = outer_sum(normed, d_keyval).astype(LOW)
    sum_keyval = jnp.swapaxes(sum_keyval.reshape(groups, size, share, 2 * head_dim), 0, 1)
    sum_keyval = lax.all_to_all(sum_keyval, "mp", 0, 0, tiled=True)
    if fast:
        last_parts, d_keyval = tie(last_parts, d_keyval)
        last_factor = owned_factor(last_parts, last_owners)
        query_sum.parts, last_factor, d_normed, first_choices[1] = tie(
            query_sum.parts, last_factor, d_normed, first_choices[1]
        )
        last_choices = share_out(last_factor, last_owners)
    grad_query = own_rows_of(query_sum.total(), query_cols)
    d_normed = d_normed + rows_dot(d_keyval, full_keyval)
    input_grad = (d_mid + norm_back(d_normed, x_rows, x_scale, gains[0])).astype(LOW)
    input_grad = input_grad.reshape(inputs.shape)
    gain_input = jnp.sum(d_normed * x_rows * x_scale, axis=0)
    share_sums = jnp.sum(wide(sum_keyval), axis=0).astype(LOW)
    share_sums, input_grad = tie(share_sums, input_grad)
    gain_rows = as_rows(jnp.stack([gain_input, gain_mid], axis=0), 2 * head_dim)
    gain_rows = jnp.broadcast_to(gain_rows[None], (groups,) + gain_rows.shape)
    share_parts = jnp.concatenate([share_sums, gain_rows], axis=1)
    share_parts = lax.all_to_all(share_parts, "dp", 0, 0, tiled=True)
    grad_out = wide(grad_out)
    moment_out = DECAY * m_out + grad_out
    out_grams = gather_grams(moment_out, head_dim, False)
    if fast:
        new_down = owned_update(moment_down, down_t, first_choices, (1, 2))
        new_gate = owned_update(moment_gate, gate_up_t[0], first_choices, (0, 3))
    else:
        new_down = small_update(moment_down, down_t, FF_BLOCK, True)
        new_gate = small_update(moment_gate, gate_up_t[0], FF_BLOCK, True)
    share_parts, new_down = tie(share_parts, new_down)
    grad_keyval = jnp.sum(wide(share_parts), axis=0)
    gain_rows = as_rows(from_rows(grad_keyval[share:]), 2 * head_dim)
    grad_keyval = jnp.concatenate([grad_keyval[:share].astype(LOW), gain_rows], axis=0)
    grad_keyval = lax.all_gather(grad_keyval, "mp", axis=0, tiled=False)
    if fast:
        new_up = owned_update(moment_up, gate_up_t[1], last_choices, last_owners)
    else:
        new_up = small_update(moment_up, gate_up_t[1], FF_BLOCK, True)
    new_out = small_update(moment_out, w_out, head_dim, False, out_grams)
    grad_keyval, new_out, new_up = tie(grad_keyval, new_out, new_up)
    grad_keyval = wide(grad_keyval)
    grad_gains = from_rows(jnp.sum(grad_keyval[:, share:], axis=0)).reshape(gains.shape)
    grad_keyval = grad_keyval[:, :share].reshape(w_keyval.shape)
    moment_keyval = DECAY * m_keyval + grad_keyval
    keyval_grams = gather_grams(moment_keyval, 2 * head_dim, False)
    grad_query = wide(grad_query)
    moment_query = DECAY * m_query + grad_query
    query_grams = gather_grams(moment_query, head_dim, False)
    new_keyval, new_query = small_updates(
        [
            (moment_keyval, w_keyval, 2 * head_dim, False, keyval_grams),
            (moment_query, w_query, head_dim, False, query_grams),
        ]
    )
    grad_gate_up = wide(jnp.stack([grad_gate, grad_up]))
    moment_gate_up = DECAY * old_gate_up + grad_gate_up
    new_gate_up = jnp.stack([new_gate, new_up])

    def back(value):
        return jnp.transpose(value, (2, 0, 1))

    moment_gains = DECAY * m_gains + grad_gains
    new_gains = gains - GAIN_RATE * moment_gains
    return (
        output,
        input_grad,
        grad_query,
        grad_keyval,
        grad_out,
        back(grad_gate_up),
        jnp.transpose(grad_down),
        grad_gains,
        moment_query,
        moment_keyval,
        moment_out,
        back(moment_gate_up),
        jnp.transpose(moment_down),
        moment_gains,
        new_query,
        new_keyval,
        new_out,
        back(new_gate_up),
        jnp.transpose(new_down),
        new_gains,
    )


def solution(mesh):
    rows = P("dp", None)
    both = P("dp", "mp")
    tokens = P("dp", "mp", None)
    gate_up = P("dp", None, "mp")
    weights = (both, rows, both, gate_up, both, P())
    return jax.shard_map(
        shards,
        mesh=mesh,
        in_specs=(tokens, tokens, rows) + weights + weights,
        out_specs=(tokens, tokens) + weights + weights + weights,
        check_vma=False,
    )
```

```python
import functools

import jax
import jax.numpy as jnp
from jax import lax
from jax.experimental import pallas as pl
from jax.experimental.pallas import tpu as pltpu
from jax.sharding import PartitionSpec as P

FF_BLOCK = 352
NS_ITERS = 5
FORWARD_HEADS = 8
BACKWARD_HEADS = 4

EPS = 1e-05
THETA = 10000.0
NS_A = 3.4445
NS_B = -4.775
NS_C = 2.0315
MUON_RATE = 0.8
GAIN_RATE = 0.002
DECAY = 0.5
MASKED = -1e30
VMEM_LIMIT = 40 * 1024 * 1024
VMEM_MOST = 58 * 1024 * 1024
LOW = jnp.bfloat16


def doc_layout(doc_lengths, positions):
    ends = jnp.cumsum(doc_lengths)
    starts = ends - doc_lengths
    segment = jnp.sum((positions[:, None] >= ends[None, :]).astype(jnp.int32), axis=1)
    member = (
        segment[:, None] == jnp.arange(doc_lengths.shape[0], dtype=jnp.int32)[None, :]
    ).astype(jnp.int32)
    offset = positions - jnp.sum(member * starts[None, :], axis=1)
    return (segment, offset)


def rotary_tables(offset, half_dim):
    freqs = jnp.power(THETA, -jnp.arange(half_dim, dtype=jnp.float32) / half_dim)
    angle = offset.astype(jnp.float32)[..., None] * freqs
    return (jnp.cos(angle), jnp.sin(angle))


def rotate(vector, cosine, sine):
    half_dim = vector.shape[-1] // 2
    first_half = vector[..., :half_dim]
    second_half = vector[..., half_dim:]
    return jnp.concatenate(
        [first_half * cosine - second_half * sine, second_half * cosine + first_half * sine],
        axis=-1,
    )


def inverse_scale(vector):
    return lax.rsqrt(jnp.mean(vector * vector, axis=-1, keepdims=True) + EPS)


def norm_back(grad_rows, value_rows, scale_rows, gain_row):
    weighted = grad_rows * gain_row
    cubed = scale_rows * scale_rows * scale_rows
    return scale_rows * weighted - value_rows * cubed * jnp.mean(
        weighted * value_rows, axis=-1, keepdims=True
    )


def contract(left, right, left_dim, right_dim):
    return lax.dot_general(
        left,
        right,
        (((left_dim,), (right_dim,)), ((), ())),
        preferred_element_type=jnp.float32,
    )


def plain_dot(left, right):
    return contract(left, right, 1, 0)


def rows_dot(left, right):
    return contract(left, right, 1, 1)


def outer_sum(left, right):
    return contract(left, right, 0, 0)


def swap(value, flip, size):
    return lax.ppermute(value, "mp", [(i, i ^ flip) for i in range(size)])


def tie(*values):
    return lax.optimization_barrier(values)


class Gather:
    def __init__(self, value, size):
        self.size = size
        self.half = value.shape[0] // 2
        self.parts = {"own": value}
        self.cuts = []

    def swap(self, name, flip):
        return swap(self.parts[name], flip, self.size)

    def first(self):
        parts = self.parts
        if self.size != 8:
            for s in range(1, self.size):
                parts[str(s)] = self.swap("own", s)
            return
        parts["one"] = self.swap("own", 1)
        parts["two"] = self.swap("own", 2)
        parts["four"] = self.swap("own", 4)

    def cut(self, value):
        parts = self.parts
        if self.size != 8:
            return value
        top, low = parts["two"][: self.half], parts["four"][self.half :]
        self.cuts = list(tie(top, low, value))
        return self.cuts.pop()

    def second(self):
        parts = self.parts
        if self.size != 8:
            return
        if not self.cuts:
            self.cut(jnp.zeros((), jnp.float32))
        parts["six_top"] = swap(self.cuts[0], 4, self.size)
        parts["six_low"] = swap(self.cuts[1], 2, self.size)

    def relay(self):
        parts = self.parts
        if self.size != 8:
            return
        parts["three"] = self.swap("two", 1)
        parts["five"] = self.swap("four", 1)

    def third(self):
        parts = self.parts
        if self.size != 8:
            return
        parts["seven_top"] = self.swap("six_top", 1)
        parts["seven_low"] = self.swap("six_low", 1)

    def pieces(self):
        parts = self.parts
        if self.size != 8:
            return [[(0, parts["own"])]] + [[(0, parts[str(s)])] for s in range(1, self.size)]
        blocks = []
        for name in ("own", "one", "two", "three", "four", "five", "six", "seven"):
            if name in parts:
                blocks.append([(0, parts[name])])
            elif name + "_top" in parts:
                blocks.append([(0, parts[name + "_top"]), (self.half, parts[name + "_low"])])
            else:
                blocks.append([])
        return blocks


def flips_of(size):
    flips = [1 << bit for bit in range(size.bit_length() - 1)]
    return flips[1:] + flips[:1]


def gather_order(size):
    order = [0]
    for flip in flips_of(size):
        order = order + [s ^ flip for s in order]
    return order


def gather_small(value, size):
    value = value[None]
    for flip in flips_of(size):
        value = jnp.concatenate([value, swap(value, flip, size)], axis=0)
    return value


def scatter_small(parts, size):
    for flip in flips_of(size)[::-1]:
        half = parts.shape[0] // 2
        parts = wide(parts[:half]) + wide(swap(parts[half:].astype(LOW), flip, size))
    return parts[0]


def wide(value):
    return value.astype(jnp.float32)


def step_order(size):
    if size == 8:
        return [(3, 0), (1, 0), (3, 1), (2, 1)], [(1, 1), (2, 0), (0, 0), (0, 1)]
    steps = [(pair, half) for pair in range(size // 2) for half in range(2)]
    return steps[: len(steps) // 2], steps[len(steps) // 2 :]


class Scatter:
    def __init__(self, size):
        self.size = size
        self.runs = []
        self.parts = {}

    def first(self, evens, odds):
        self.runs.append((evens, odds))
        if self.size == 8:
            self.parts["core" + str(len(self.runs))] = swap(odds, 1, self.size)

    def second(self, later=None):
        if self.size != 8:
            steps = step_order(self.size)
            place = {step: (run, n) for run in (0, 1) for n, step in enumerate(steps[run])}
            total = 0.0
            for s in range(self.size):
                halves = []
                for half in (0, 1):
                    run, n = place[(s // 2, half)]
                    halves.append(self.runs[run][s % 2][n])
                part = jnp.concatenate(halves, axis=0)
                total = total + wide(swap(part, s, self.size) if s else part)
            self.parts["total"] = total
            return later
        evens, core = self.runs[0][0], self.parts.pop("core1")
        two = (wide(evens[:2]) + wide(core[:2])).astype(LOW)
        four = (wide(evens[2:]) + wide(core[2:])).astype(LOW)
        two, four, later = tie(two, four, later)
        self.parts["two"] = swap(two, 2, self.size)
        self.parts["four"] = swap(four, 4, self.size)
        return later

    def third(self, later=None):
        if self.size != 8:
            return later
        evens, core = self.runs[1][0], self.parts["core2"]
        low = wide(evens[0]) + wide(core[0]) + wide(self.parts["four"][0])
        top = wide(evens[1]) + wide(core[1]) + wide(self.parts["two"][0])
        low, top, later = tie(low.astype(LOW), top.astype(LOW), later)
        self.parts["low"] = swap(low, 2, self.size)
        self.parts["top"] = swap(top, 4, self.size)
        return later

    def total(self):
        parts = self.parts
        if self.size != 8:
            return parts["total"]
        evens, core = self.runs[1][0], parts["core2"]
        top = wide(evens[2]) + wide(core[2]) + wide(parts["two"][1]) + wide(parts["top"])
        low = wide(evens[3]) + wide(core[3]) + wide(parts["four"][1]) + wide(parts["low"])
        return jnp.concatenate([top, low], axis=0)


def as_rows(value, width):
    value = value.reshape(-1, width)
    high = value.astype(LOW)
    return jnp.concatenate([high, (value - wide(high)).astype(LOW)], axis=0)


def from_rows(rows):
    half = rows.shape[0] // 2
    return wide(rows[:half]) + wide(rows[half:])


def masked_bias(qid_ref, kid_ref):
    rows = qid_ref[0]
    keys = kid_ref[0]
    allowed = (rows[:, 0:1] == keys[0:1, :]) & (rows[:, 1:2] >= keys[1:2, :])
    return jnp.where(allowed, 0.0, MASKED)


def forward_kernel(heads, head_dim, q_ref, kv_ref, qid_ref, kid_ref, *refs):
    ctx_ref, log_ref, bias_ref, probs_ref = refs[-4:]

    @pl.when(pl.program_id(1) == 0)
    def _():
        bias_ref[...] = masked_bias(qid_ref, kid_ref)

    keys = kv_ref[0, :, :head_dim]
    values = kv_ref[0, :, head_dim:]
    rows = q_ref.shape[1]
    for head in range(heads):
        cols = slice(head * head_dim, (head + 1) * head_dim)
        scores = contract(q_ref[0, :, cols], keys, 1, 1) * head_dim ** (-0.5) + bias_ref[...]
        top = jnp.max(scores, axis=-1, keepdims=True)
        powers = jnp.exp(scores - top)
        total = jnp.sum(powers, axis=-1, keepdims=True)
        log_ref[0, :, cols] = jnp.broadcast_to(top + jnp.log(total), (rows, head_dim))
        probs_ref[head * rows : (head + 1) * rows] = (powers * (1.0 / total)).astype(LOW)
    context = contract(probs_ref[...], values, 1, 0).astype(LOW)
    for head in range(heads):
        cols = slice(head * head_dim, (head + 1) * head_dim)
        ctx_ref[0, :, cols] = context[head * rows : (head + 1) * rows]


def attention_forward(batch, queries, keyval, qid, kid, head_dim, earlier=()):
    all_batches, rows, width = queries.shape
    batches = 1
    seq_len = keyval.shape[1]
    heads = min(FORWARD_HEADS, width // head_dim)
    block = pl.BlockSpec((1, rows, heads * head_dim), lambda b, h: (batch, 0, h))
    work = batches * rows * width * seq_len
    return pl.pallas_call(
        functools.partial(forward_kernel, heads, head_dim),
        grid=(batches, width // (heads * head_dim)),
        in_specs=[
            block,
            pl.BlockSpec((1, seq_len, 2 * head_dim), lambda b, h: (batch, 0, 0)),
            pl.BlockSpec((1, rows, 2), lambda b, h: (batch, 0, 0)),
            pl.BlockSpec((1, 2, seq_len), lambda b, h: (batch, 0, 0)),
        ]
        + [pl.BlockSpec(memory_space=pltpu.HBM)] * len(earlier),
        out_specs=[block, block],
        out_shape=[
            jax.ShapeDtypeStruct((all_batches, rows, width), LOW),
            jax.ShapeDtypeStruct((all_batches, rows, width), jnp.float32),
        ],
        input_output_aliases={4 + n: n for n in range(len(earlier))},
        scratch_shapes=[
            pltpu.VMEM((rows, seq_len), jnp.float32),
            pltpu.VMEM((heads * rows, seq_len), LOW),
        ],
        compiler_params=pltpu.CompilerParams(vmem_limit_bytes=VMEM_LIMIT),
        cost_estimate=pl.CostEstimate(
            flops=8 * work, bytes_accessed=8 * batches * rows * width, transcendentals=work // head_dim
        ),
        name="attention_forward",
    )(queries, keyval, qid, kid, *earlier)


def backward_kernel(
    heads,
    head_dim,
    q_ref,
    dctx_ref,
    log_ref,
    kv_ref,
    qid_ref,
    kid_ref,
    cos_ref,
    sin_ref,
    *refs,
):
    dq_ref, out_ref, dkv_ref, bias_ref, probs_ref, ds_ref = refs[-6:]

    @pl.when(pl.program_id(1) == 0)
    def _():
        bias_ref[...] = masked_bias(qid_ref, kid_ref)
        dkv_ref[...] = jnp.zeros_like(dkv_ref)

    scale = head_dim ** (-0.5)
    half = head_dim // 2
    keys = kv_ref[0, :, :head_dim]
    values = kv_ref[0, :, head_dim:]
    cosine = cos_ref[0]
    sine = sin_ref[0]
    rows = q_ref.shape[1]
    for head in range(heads):
        cols = slice(head * head_dim, (head + 1) * head_dim)
        place = slice(head * rows, (head + 1) * rows)
        scores = contract(q_ref[0, :, cols], keys, 1, 1) * scale + bias_ref[...]
        probs = jnp.exp(scores - log_ref[0, :, head * head_dim : head * head_dim + 1])
        d_probs = contract(dctx_ref[0, :, cols], values, 1, 1)
        centre = jnp.sum(d_probs * probs, axis=-1, keepdims=True)
        ds_ref[place] = (probs * (d_probs - centre)).astype(LOW)
        probs_ref[place] = probs.astype(LOW)
    queries = jnp.concatenate(
        [q_ref[0, :, head * head_dim : (head + 1) * head_dim] for head in range(heads)], axis=0
    )
    d_context = jnp.concatenate(
        [dctx_ref[0, :, head * head_dim : (head + 1) * head_dim] for head in range(heads)], axis=0
    )
    dkv_ref[:, :head_dim] += contract(queries, ds_ref[...], 0, 0).T * scale
    dkv_ref[:, head_dim:] += contract(d_context, probs_ref[...], 0, 0).T
    d_query = contract(ds_ref[...], keys, 1, 0) * scale
    for head in range(heads):
        first = d_query[head * rows : (head + 1) * rows, :half]
        second = d_query[head * rows : (head + 1) * rows, half:]
        dq_ref[0, :, head * head_dim : (head + 1) * head_dim] = jnp.concatenate(
            [first * cosine + second * sine, second * cosine - first * sine], axis=1
        ).astype(LOW)

    @pl.when(pl.program_id(1) == pl.num_programs(1) - 1)
    def _():
        out_ref[0] = dkv_ref[...].astype(LOW)


def attention_backward(
    batch, queries, d_context, logs, keyval, qid, kid, cosine, sine, head_dim, earlier=()
):
    all_batches, rows, width = queries.shape
    batches = 1
    seq_len = keyval.shape[1]
    heads = min(BACKWARD_HEADS, width // head_dim)
    block = pl.BlockSpec((1, rows, heads * head_dim), lambda b, h: (batch, 0, h))
    work = batches * rows * width * seq_len

    def whole(*shape):
        return pl.BlockSpec((1,) + shape, lambda b, h: (batch, 0, 0))

    return pl.pallas_call(
        functools.partial(backward_kernel, heads, head_dim),
        grid=(batches, width // (heads * head_dim)),
        in_specs=[
            block,
            block,
            block,
            whole(seq_len, 2 * head_dim),
            whole(rows, 2),
            whole(2, seq_len),
            whole(rows, head_dim // 2),
            whole(rows, head_dim // 2),
        ]
        + [pl.BlockSpec(memory_space=pltpu.HBM)] * len(earlier),
        out_specs=[block, whole(seq_len, 2 * head_dim)],
        out_shape=[
            jax.ShapeDtypeStruct((all_batches, rows, width), LOW),
            jax.ShapeDtypeStruct((all_batches, seq_len, 2 * head_dim), LOW),
        ],
        input_output_aliases={8 + n: n for n in range(len(earlier))},
        scratch_shapes=[
            pltpu.VMEM((seq_len, 2 * head_dim), jnp.float32),
            pltpu.VMEM((rows, seq_len), jnp.float32),
            pltpu.VMEM((heads * rows, seq_len), LOW),
            pltpu.VMEM((heads * rows, seq_len), LOW),
        ],
        compiler_params=pltpu.CompilerParams(vmem_limit_bytes=VMEM_LIMIT),
        cost_estimate=pl.CostEstimate(
            flops=20 * work,
            bytes_accessed=12 * batches * rows * width,
            transcendentals=work // head_dim,
        ),
        name="attention_backward",
    )(queries, d_context, logs, keyval, qid, kid, cosine, sine, *earlier)


def flat_pieces(blocks):
    places = []
    arrays = []
    for number, pieces in enumerate(blocks):
        for first, rows in pieces:
            places.append((number, first, rows.shape[0]))
            arrays.append(rows)
    return places, arrays


def fetch_all(places, piece_refs, weight_ref, sem_ref):
    copies = []
    for number, (block, first, rows) in enumerate(places):
        copies.append(
            pltpu.make_async_copy(
                piece_refs[number],
                weight_ref.at[block, pl.ds(first, rows)],
                sem_ref.at[number],
            )
        )
    for copy in copies:
        copy.start()
    return copies


def project_kernel(places, head_dim, turned, turns, *refs):
    count = len(places)
    piece_refs, refs = refs[:count], refs[count:]
    if turned:
        rows_ref, cos_ref, sin_ref, out_ref, weight_ref, sem_ref = refs
    else:
        rows_ref, out_ref, weight_ref, sem_ref = refs
    copies = fetch_all(places, piece_refs, weight_ref, sem_ref)
    depth = rows_ref.shape[1]
    width = weight_ref.shape[2]
    half = head_dim // 2
    for block in range(weight_ref.shape[0]):
        for number, place in enumerate(places):
            if place[0] == block:
                copies[number].wait()
        product = contract(rows_ref[...], weight_ref[block, :depth], 1, 0)
        if turned:
            for head in range(width // head_dim):
                first = product[:, head * head_dim : head * head_dim + half]
                second = product[:, head * head_dim + half : (head + 1) * head_dim]
                cosine = cos_ref[...]
                sine = sin_ref[...]
                place = block * width + head * head_dim
                if turns is not None and place >= turns * head_dim:
                    out_ref[:, place : place + head_dim] = product[
                        :, head * head_dim : (head + 1) * head_dim
                    ].astype(LOW)
                    continue
                out_ref[:, place : place + head_dim] = jnp.concatenate(
                    [first * cosine - second * sine, second * cosine + first * sine], axis=1
                ).astype(LOW)
        else:
            out_ref[:, block * width : (block + 1) * width] = product.astype(LOW)


def project(rows, blocks, head_dim, tables=None, turns=None):
    places, arrays = flat_pieces(blocks)
    size = len(blocks)
    depth = max(first + count for _, first, count in places)
    width = arrays[0].shape[1]
    vmem = pl.BlockSpec(memory_space=pltpu.VMEM)
    turned = tables is not None
    return pl.pallas_call(
        functools.partial(project_kernel, places, head_dim, turned, turns),
        in_specs=[pl.BlockSpec(memory_space=pltpu.HBM)] * len(arrays) + [vmem] * (3 if turned else 1),
        out_specs=vmem,
        out_shape=jax.ShapeDtypeStruct((rows.shape[0], size * width), LOW),
        scratch_shapes=[
            pltpu.VMEM((size, depth, width), LOW),
            pltpu.SemaphoreType.DMA((len(arrays),)),
        ],
        compiler_params=pltpu.CompilerParams(vmem_limit_bytes=VMEM_LIMIT),
        cost_estimate=pl.CostEstimate(
            flops=2 * rows.size * size * width,
            bytes_accessed=2 * (size * depth * width + 2 * rows.size),
            transcendentals=0,
        ),
        name="project",
    )(*arrays, rows, *(tables if turned else ()))


def project_back_kernel(places, *refs):
    count = len(places)
    piece_refs, (rows_ref, out_ref, weight_ref, sem_ref) = refs[:count], refs[count:]
    copies = fetch_all(places, piece_refs, weight_ref, sem_ref)
    project_back_blocks(places, copies, rows_ref, out_ref, weight_ref)


def project_back_blocks(places, copies, rows_ref, out_ref, weight_ref):
    depth = out_ref.shape[1]
    width = weight_ref.shape[2]
    for block in range(weight_ref.shape[0]):
        for number, place in enumerate(places):
            if place[0] == block:
                copies[number].wait()
        product = contract(
            rows_ref[:, block * width : (block + 1) * width], weight_ref[block, :depth], 1, 1
        )
        if block == 0:
            out_ref[...] = product
        else:
            out_ref[...] += product


def project_back(rows, blocks, depth):
    places, arrays = flat_pieces(blocks)
    size = len(blocks)
    height = max(first + count for _, first, count in places)
    width = arrays[0].shape[1]
    vmem = pl.BlockSpec(memory_space=pltpu.VMEM)
    return pl.pallas_call(
        functools.partial(project_back_kernel, places),
        in_specs=[pl.BlockSpec(memory_space=pltpu.HBM)] * len(arrays) + [vmem],
        out_specs=vmem,
        out_shape=jax.ShapeDtypeStruct((rows.shape[0], depth), jnp.float32),
        scratch_shapes=[
            pltpu.VMEM((size, height, width), LOW),
            pltpu.SemaphoreType.DMA((len(arrays),)),
        ],
        compiler_params=pltpu.CompilerParams(vmem_limit_bytes=VMEM_LIMIT),
        cost_estimate=pl.CostEstimate(
            flops=2 * rows.size * depth,
            bytes_accessed=2 * (size * height * width + 3 * rows.size),
            transcendentals=0,
        ),
        name="project_back",
    )(*arrays, rows)


def beside(source_refs, weight_ref, sem_ref, whole=(), whole_ref=None):
    @pl.when(pl.program_id(0) == 0)
    def _():
        copies = []
        for number, source_ref in enumerate(source_refs):
            groups, _, chunk = source_ref.shape
            for group in range(groups):
                cols = pl.ds(group * chunk, chunk)
                copies.append(
                    pltpu.make_async_copy(
                        source_ref.at[group],
                        weight_ref.at[number, :, cols],
                        sem_ref.at[number, group],
                    )
                )
        for ref, number in whole:
            copies.append(
                pltpu.make_async_copy(
                    ref, whole_ref.at[number], sem_ref.at[len(source_refs) + number, 0]
                )
            )
        for copy in copies:
            copy.start()
        for copy in copies:
            copy.wait()


def hidden_kernel(places, steps_order, turn, *refs):
    count = len(places)
    piece_refs = refs[:count]
    source_refs = refs[count : count + 2]
    all_ref, gate_ref, up_ref, hidden_ref, turned_ref = refs[count + 2 : count + 7]
    slot_ref, weight_ref, sem_ref, weight_sem_ref = refs[count + 7 :]
    step = pl.program_id(0)
    steps = pl.num_programs(0)
    half = slot_ref.shape[1] // 2

    def each(number, act):
        slot = lax.rem(number, 2)
        for static, (pair, side) in enumerate(steps_order):

            @pl.when(number == static)
            def _(pair=pair, side=side):
                for parity in range(2):
                    block, start = 2 * pair + parity, side * half
                    for index, (owner, first, rows) in enumerate(places):
                        if owner == block and first <= start < first + rows:
                            act(
                                pltpu.make_async_copy(
                                    piece_refs[index].at[pl.ds(start - first, half)],
                                    slot_ref.at[slot, pl.ds(parity * half, half)],
                                    sem_ref.at[slot, parity],
                                )
                            )

    @pl.when(step == 0)
    def _():
        each(step, lambda copy: copy.start())

    @pl.when(step + 1 < steps)
    def _():
        each(step + 1, lambda copy: copy.start())

    beside(source_refs, weight_ref, weight_sem_ref)
    each(step, lambda copy: copy.wait())
    rows = slot_ref[lax.rem(step, 2)]
    all_ref[...] = rows
    gate = contract(rows, weight_ref[0], 1, 1)
    upward = contract(rows, weight_ref[1], 1, 1)
    gate_ref[...] = gate
    up_ref[...] = upward
    hidden = gate * jax.nn.sigmoid(gate) * upward
    hidden_ref[...] = hidden.astype(LOW)
    turned_ref[...] = (hidden.T if turn else hidden).astype(LOW)


def in_steps(run, blocks):
    half = sum(piece.shape[0] for _, piece in blocks[0]) // 2
    rows = []
    for pair, side in step_order(len(blocks))[run]:
        start = side * half
        for pieces in blocks[2 * pair : 2 * pair + 2]:
            for first, piece in pieces:
                if first <= start < first + piece.shape[0]:
                    rows.append(piece[start - first : start - first + half])
    return jnp.concatenate(rows, axis=0)


def hidden_units(run, blocks, full_gate, full_up):
    size = len(blocks)
    steps = step_order(size)[run]
    used = {2 * pair + parity for pair, _ in steps for parity in (0, 1)}
    places, arrays = flat_pieces([part if s in used else [] for s, part in enumerate(blocks)])
    rows = max(first + count for _, first, count in places)
    depth = arrays[0].shape[1]
    units = full_gate.shape[1]
    turn = rows % 128 == 0

    def block(width):
        return pl.BlockSpec((rows, width), lambda s: (s, 0))

    turned = pl.BlockSpec((units, rows), lambda s: (0, s)) if turn else block(units)
    turned_shape = (units, len(steps) * rows) if turn else (len(steps) * rows, units)
    return pl.pallas_call(
        functools.partial(hidden_kernel, places, steps, turn),
        grid=(len(steps),),
        in_specs=[pl.BlockSpec(memory_space=pltpu.HBM)] * (len(arrays) + 2),
        out_specs=[block(depth), block(units), block(units), block(units), turned],
        out_shape=[
            jax.ShapeDtypeStruct((len(steps) * rows, depth), LOW),
            jax.ShapeDtypeStruct((len(steps) * rows, units), jnp.float32),
            jax.ShapeDtypeStruct((len(steps) * rows, units), jnp.float32),
            jax.ShapeDtypeStruct((len(steps) * rows, units), LOW),
            jax.ShapeDtypeStruct(turned_shape, LOW),
        ],
        scratch_shapes=[
            pltpu.VMEM((2, rows, depth), LOW),
            pltpu.VMEM((2, units, depth), LOW),
            pltpu.SemaphoreType.DMA((2, 2)),
            pltpu.SemaphoreType.DMA((2, full_gate.shape[0])),
        ],
        compiler_params=pltpu.CompilerParams(vmem_limit_bytes=VMEM_LIMIT),
        cost_estimate=pl.CostEstimate(
            flops=4 * len(steps) * rows * depth * units,
            bytes_accessed=4 * len(steps) * rows * depth,
            transcendentals=len(steps) * rows * units,
        ),
        name="hidden_units",
    )(*arrays, full_gate, full_up)


def hidden_back_kernel(
    turn,
    cot_ref,
    gate_ref,
    up_ref,
    full_gate_ref,
    full_up_ref,
    source_ref,
    dg_ref,
    du_ref,
    even_ref,
    odd_ref,
    down_ref,
    both_ref,
    sem_ref,
):
    groups, _, chunk = full_gate_ref.shape
    beside([source_ref], down_ref, sem_ref, [(full_gate_ref, 0), (full_up_ref, 1)], both_ref)
    gate = gate_ref[...]
    upward = up_ref[...]
    sigma = jax.nn.sigmoid(gate)
    d_hidden = contract(cot_ref[...], down_ref[0], 1, 1)
    d_gate = d_hidden * upward * sigma * (1.0 + gate * (1.0 - sigma))
    d_up = d_hidden * gate * sigma
    dg_ref[...] = (d_gate.T if turn else d_gate).astype(LOW)
    du_ref[...] = (d_up.T if turn else d_up).astype(LOW)
    d_gate = d_gate.astype(LOW)
    d_up = d_up.astype(LOW)
    for group in range(groups):
        part = contract(d_gate, both_ref[0, group], 1, 0)
        part = (part + contract(d_up, both_ref[1, group], 1, 0)).astype(LOW)
        cols = slice(group * chunk, (group + 1) * chunk)
        even_ref[0, :, cols] = part[: part.shape[0] // 2]
        odd_ref[0, :, cols] = part[part.shape[0] // 2 :]


def hidden_back(cotangent, gate, upward, full_gate, full_up, down, steps):
    tokens, depth = cotangent.shape
    rows = tokens // steps
    units = gate.shape[1]
    turn = rows % 128 == 0

    def block(width):
        return pl.BlockSpec((rows, width), lambda s: (s, 0))

    if turn:
        turned = pl.BlockSpec((units, rows), lambda s: (0, s))
        turned_shape = (units, steps * rows)
    else:
        turned = pl.BlockSpec((rows, units), lambda s: (s, 0))
        turned_shape = (steps * rows, units)
    half = pl.BlockSpec((1, rows // 2, depth), lambda s: (s, 0, 0))
    return pl.pallas_call(
        functools.partial(hidden_back_kernel, turn),
        grid=(steps,),
        in_specs=[
            block(depth),
            block(units),
            block(units),
            pl.BlockSpec(memory_space=pltpu.HBM),
            pl.BlockSpec(memory_space=pltpu.HBM),
            pl.BlockSpec(memory_space=pltpu.HBM),
        ],
        out_specs=[turned, turned, half, half],
        out_shape=[
            jax.ShapeDtypeStruct(turned_shape, LOW),
            jax.ShapeDtypeStruct(turned_shape, LOW),
            jax.ShapeDtypeStruct((steps, rows // 2, depth), LOW),
            jax.ShapeDtypeStruct((steps, rows // 2, depth), LOW),
        ],
        scratch_shapes=[
            pltpu.VMEM((1, units, depth), LOW),
            pltpu.VMEM((2,) + full_gate.shape, LOW),
            pltpu.SemaphoreType.DMA((3, down.shape[0])),
        ],
        compiler_params=pltpu.CompilerParams(vmem_limit_bytes=VMEM_MOST),
        cost_estimate=pl.CostEstimate(
            flops=6 * steps * rows * depth * units,
            bytes_accessed=4 * steps * rows * depth,
            transcendentals=steps * rows * units,
        ),
        name="hidden_back",
    )(cotangent, gate, upward, full_gate, full_up, down)


def hidden_out_kernel(hidden_ref, down_ref, even_ref, odd_ref):
    groups, _, chunk = down_ref.shape
    for group in range(groups):
        part = contract(hidden_ref[...], down_ref[group], 1, 0).astype(LOW)
        cols = slice(group * chunk, (group + 1) * chunk)
        even_ref[0, :, cols] = part[: part.shape[0] // 2]
        odd_ref[0, :, cols] = part[part.shape[0] // 2 :]


def hidden_out(hidden, down, steps):
    tokens, units = hidden.shape
    rows = tokens // steps
    depth = down.shape[0] * down.shape[2]
    return pl.pallas_call(
        hidden_out_kernel,
        grid=(steps,),
        in_specs=[
            pl.BlockSpec((rows, units), lambda s: (s, 0)),
            pl.BlockSpec(down.shape, lambda s: (0, 0, 0), pipeline_mode=pl.Buffered(1)),
        ],
        out_specs=[pl.BlockSpec((1, rows // 2, depth), lambda s: (s, 0, 0))] * 2,
        out_shape=[jax.ShapeDtypeStruct((steps, rows // 2, depth), LOW)] * 2,
        compiler_params=pltpu.CompilerParams(vmem_limit_bytes=VMEM_LIMIT),
        cost_estimate=pl.CostEstimate(
            flops=2 * steps * rows * depth * units,
            bytes_accessed=2 * steps * rows * depth,
            transcendentals=0,
        ),
        name="hidden_out",
    )(hidden, down)


def units_sum_kernel(runs, turn, *refs):
    row_refs, refs = refs[:runs], refs[runs:]
    sums = len(refs) // (runs + 1)
    unit_refs, out_refs = refs[: runs * sums], refs[runs * sums :]
    for number, out_ref in enumerate(out_refs):
        total = 0.0
        for run, row_ref in enumerate(row_refs):
            unit_ref = unit_refs[number * runs + run]
            total = total + contract(unit_ref[...], row_ref[...], 1 if turn else 0, 0)
        out_ref[0] = total.astype(LOW)


def units_sum(units, rows, groups):
    tokens, depth = rows[0].shape
    turn = units[0][0].shape[1] == tokens
    width = units[0][0].shape[0 if turn else 1]
    chunk = depth // groups
    cut = 2
    flat = [part for parts in units for part in parts]
    out = pl.BlockSpec((1, width, chunk // cut), lambda s: (s // cut, 0, lax.rem(s, cut)))
    return pl.pallas_call(
        functools.partial(units_sum_kernel, len(rows), turn),
        grid=(groups * cut,),
        in_specs=[pl.BlockSpec((tokens, chunk // cut), lambda s: (0, s))] * len(rows)
        + [
            pl.BlockSpec(part.shape, lambda s: (0, 0), pipeline_mode=pl.Buffered(1))
            for part in flat
        ],
        out_specs=[out] * len(units),
        out_shape=[jax.ShapeDtypeStruct((groups, width, chunk), LOW)] * len(units),
        compiler_params=pltpu.CompilerParams(vmem_limit_bytes=VMEM_LIMIT),
        cost_estimate=pl.CostEstimate(
            flops=2 * len(flat) * tokens * depth * width,
            bytes_accessed=2 * len(flat) * tokens * (depth + width),
            transcendentals=0,
        ),
        name="units_sum",
    )(*rows, *flat)


def pick(values, index):
    value = values[0]
    for number in range(1, len(values)):
        value = jnp.where(index == number, values[number], value)
    return value


def blocks_sum_kernel(row_ref, col_ref, even_ref, odd_ref):
    part = contract(row_ref[...], col_ref[...], 0, 0).astype(LOW)
    even_ref[0] = part[:, : part.shape[1] // 2]
    odd_ref[0] = part[:, part.shape[1] // 2 :]


def blocks_sum(run, rows, cols, size):
    tokens, depth = rows.shape
    width = cols.shape[1] // size
    order = step_order(size)[run]
    pairs = [pair for pair, _ in order]
    sides = [side for _, side in order]
    return pl.pallas_call(
        blocks_sum_kernel,
        grid=(len(order),),
        in_specs=[
            pl.BlockSpec((tokens, depth // 2), lambda s: (0, pick(sides, s))),
            pl.BlockSpec((tokens, 2 * width), lambda s: (0, pick(pairs, s))),
        ],
        out_specs=[pl.BlockSpec((1, depth // 2, width), lambda s: (s, 0, 0))] * 2,
        out_shape=[jax.ShapeDtypeStruct((len(order), depth // 2, width), LOW)] * 2,
        compiler_params=pltpu.CompilerParams(vmem_limit_bytes=VMEM_LIMIT),
        cost_estimate=pl.CostEstimate(
            flops=tokens * depth * len(order) * 2 * width,
            bytes_accessed=2 * depth * len(order) * width,
            transcendentals=0,
        ),
        name="blocks_sum",
    )(rows, cols)


def split(value):
    high = value.astype(LOW)
    return high, (value - wide(high)).astype(LOW)


def fine_dot(left, right, left_dim=1, right_dim=0):
    left_high, left_low = split(left)
    right_high, right_low = split(right)
    small = contract(left_high, right_low, left_dim, right_dim)
    small = small + contract(left_low, right_high, left_dim, right_dim)
    return contract(left_high, right_high, left_dim, right_dim) + small


def eye_of(width):
    row = lax.broadcasted_iota(jnp.int32, (width, width), 0)
    col = lax.broadcasted_iota(jnp.int32, (width, width), 1)
    return row, col, jnp.where(row == col, 1.0, 0.0)


def pack(gram):
    row, col, eye = eye_of(gram.shape[0])
    high = wide(gram.astype(LOW))
    low = gram - high
    packed = jnp.where(col >= row, high, low).astype(LOW)
    return packed, jnp.sum(low * eye, axis=0, keepdims=True)


def unpack(total):
    width = total.shape[1]
    _, _, eye = eye_of(width)
    packed = total[:width]
    return packed + packed.T + eye * (total[width : width + 1] - packed)


def packed_kernel(width, slots, by_rows, *refs):
    matrix_refs, out_ref = refs[:-1], refs[-1]
    for slot in range(out_ref.shape[0]):
        if slot not in [used for _, _, used in slots]:
            out_ref[slot] = jnp.zeros_like(out_ref[slot])
    for number, block, slot in slots:
        place = slice(block * width, (block + 1) * width)
        if by_rows:
            part = matrix_refs[number][place, :]
            packed, last = pack(fine_dot(part, part, 1, 1))
        else:
            part = matrix_refs[number][:, place]
            packed, last = pack(fine_dot(part, part, 0, 0))
        out_ref[slot, :width, :] = packed
        out_ref[slot, width:, :] = jnp.broadcast_to(
            last, (out_ref.shape[1] - width, width)
        ).astype(LOW)


def packed_grams(matrices, width, slots, size, by_rows=True):
    return pl.pallas_call(
        functools.partial(packed_kernel, width, slots, by_rows),
        out_shape=jax.ShapeDtypeStruct((size, width + 16, width), LOW),
        compiler_params=pltpu.CompilerParams(vmem_limit_bytes=VMEM_LIMIT),
        cost_estimate=pl.CostEstimate(
            flops=6 * len(matrices) * matrices[0].size * width,
            bytes_accessed=4 * len(matrices) * matrices[0].size,
            transcendentals=0,
        ),
        name="packed_grams",
    )(*matrices)


def newton_factor(gram):
    _, _, eye = eye_of(gram.shape[0])
    trace = jnp.sum(jnp.sum(gram * eye, axis=1, keepdims=True), axis=0, keepdims=True)
    inverse = 1.0 / (jnp.sqrt(trace) + 1e-07)
    gram = gram * inverse * inverse
    total = None
    for iteration in range(NS_ITERS):
        poly = NS_A * eye + NS_B * gram + NS_C * fine_dot(gram, gram)
        total = poly if total is None else fine_dot(total, poly)
        if iteration < NS_ITERS - 1:
            gram = fine_dot(fine_dot(poly, gram), poly)
    return total * inverse


def factor_kernel(own_ref, *refs):
    part_refs, factor_ref = refs[:-1], refs[-1]
    width = factor_ref.shape[0]

    @pl.when(own_ref[0] != 0)
    def _():
        total = 0.0
        for part_ref in part_refs:
            part = wide(part_ref[...])
            total = total + (part if part.ndim == 2 else jnp.sum(part, axis=0))
        factor_ref[...] = newton_factor(unpack(total)).astype(LOW)

    @pl.when(own_ref[0] == 0)
    def _():
        factor_ref[...] = jnp.zeros_like(factor_ref)


def block_factor(own, parts):
    width = parts[0].shape[-1]
    vmem = pl.BlockSpec(memory_space=pltpu.VMEM)
    return pl.pallas_call(
        factor_kernel,
        in_specs=[pl.BlockSpec(memory_space=pltpu.SMEM)] + [vmem] * len(parts),
        out_specs=vmem,
        out_shape=jax.ShapeDtypeStruct((width, width), LOW),
        compiler_params=pltpu.CompilerParams(vmem_limit_bytes=VMEM_LIMIT),
        cost_estimate=pl.CostEstimate(
            flops=100 * width**3, bytes_accessed=20 * width * width, transcendentals=0
        ),
        name="block_factor",
    )(own, *parts)


def apply_kernel(width, count, place_ref, matrix_ref, weight_ref, *refs):
    choice_refs, new_ref, factor_ref = refs[:-2], refs[-2], refs[-1]
    for block in range(count):
        for number, choice_ref in enumerate(choice_refs):

            @pl.when(place_ref[block] == number)
            def _(choice_ref=choice_ref):
                factor_ref[...] = choice_ref[...]

        rows = slice(block * width, (block + 1) * width)
        high, low = split(matrix_ref[rows, :])
        product = contract(factor_ref[...], high, 1, 0) + contract(factor_ref[...], low, 1, 0)
        new_ref[rows, :] = weight_ref[rows, :] - MUON_RATE * product


def apply_factors(matrix, weight, places, choices):
    width = choices[0].shape[0]
    count = matrix.shape[0] // width
    vmem = pl.BlockSpec(memory_space=pltpu.VMEM)
    return pl.pallas_call(
        functools.partial(apply_kernel, width, count),
        in_specs=[pl.BlockSpec(memory_space=pltpu.SMEM)] + [vmem] * (2 + len(choices)),
        out_specs=vmem,
        out_shape=jax.ShapeDtypeStruct(matrix.shape, jnp.float32),
        scratch_shapes=[pltpu.VMEM((width, width), LOW)],
        compiler_params=pltpu.CompilerParams(vmem_limit_bytes=VMEM_LIMIT),
        cost_estimate=pl.CostEstimate(
            flops=4 * matrix.size * width, bytes_accessed=12 * matrix.size, transcendentals=0
        ),
        name="apply_factors",
    )(places, matrix, weight, *choices)


def update_kernel(sizes, counts, *refs):
    firsts = [2 * len(sizes) + sum(counts[:n]) for n in range(len(sizes))]
    for number, (width, by_rows) in enumerate(sizes):
        matrix_ref, weight_ref = refs[2 * number], refs[2 * number + 1]
        part_refs = refs[firsts[number] : firsts[number] + counts[number]]
        new_ref = refs[2 * len(sizes) + sum(counts) + number]
        for block in range(part_refs[0].shape[0]):
            total = 0.0
            for part_ref in part_refs:
                total = total + wide(part_ref[block])
            factor = newton_factor(unpack(total))
            place = slice(block * width, (block + 1) * width)
            if by_rows:
                new_ref[place, :] = weight_ref[place, :] - MUON_RATE * fine_dot(
                    factor, matrix_ref[place, :]
                )
            else:
                new_ref[:, place] = weight_ref[:, place] - MUON_RATE * fine_dot(
                    matrix_ref[:, place], factor
                )


def gather_grams(moment, width, by_rows):
    count = moment.shape[0 if by_rows else 1] // width
    slots = tuple((0, block, block) for block in range(count))
    grams = packed_grams((moment,), width, slots, count, by_rows)
    size = lax.axis_size("dp")
    return [grams] + [
        lax.ppermute(grams, "dp", [(i, (i + shift) % size) for i in range(size)])
        for shift in range(1, size)
    ]


def small_updates(items):
    vmem = pl.BlockSpec(memory_space=pltpu.VMEM)
    flat = [array for moment, weight, _, _, _ in items for array in (moment, weight)]
    flat = flat + [part for item in items for part in item[4]]
    counts = [len(item[4]) for item in items]
    return pl.pallas_call(
        functools.partial(update_kernel, [(item[2], item[3]) for item in items], counts),
        in_specs=[vmem] * len(flat),
        out_specs=[vmem] * len(items),
        out_shape=[jax.ShapeDtypeStruct(item[0].shape, jnp.float32) for item in items],
        compiler_params=pltpu.CompilerParams(vmem_limit_bytes=VMEM_LIMIT),
        cost_estimate=pl.CostEstimate(
            flops=sum(100 * item[4][0].size * item[2] for item in items),
            bytes_accessed=sum(12 * item[0].size for item in items),
            transcendentals=0,
        ),
        name="small_update",
    )(*flat)


def small_update(moment, weight, width, by_rows, parts=None):
    if parts is None:
        parts = gather_grams(moment, width, by_rows)
    return small_updates([(moment, weight, width, by_rows, parts)])[0]


def exchange(values, owners):
    size = lax.axis_size("dp")
    me = lax.axis_index("dp")
    parts = []
    for shift in range(size):
        target = (me + shift) % size
        part = values[0]
        for value, owner in zip(values[1:], owners[1:]):
            part = jnp.where(target == owner, value, part)
        if shift:
            pairs = [((o - shift) % size, o) for o in owners]
            part = lax.ppermute(part, "dp", pairs)
        parts.append(part)
    return parts


def share_out(factor, owners):
    size = lax.axis_size("dp")
    return [factor] + [
        lax.ppermute(factor, "dp", [(o, (o + shift) % size) for o in owners])
        for shift in range(1, size)
    ]


def back_factor_kernel(places, parts, *refs):
    own_ref, refs = refs[0], refs[1:]
    count = len(places)
    piece_refs, refs = refs[:count], refs[count:]
    rows_ref, part_refs = refs[0], refs[1 : 1 + parts]
    out_ref, factor_ref, weight_ref, sem_ref = refs[1 + parts :]
    copies = fetch_all(places, piece_refs, weight_ref, sem_ref)
    factor_kernel(own_ref, *part_refs, factor_ref)
    project_back_blocks(places, copies, rows_ref, out_ref, weight_ref)


def back_and_factor(rows, blocks, depth, own, parts):
    places, arrays = flat_pieces(blocks)
    size = len(blocks)
    height = max(first + count for _, first, count in places)
    width = arrays[0].shape[1]
    gram_width = parts[0].shape[-1]
    vmem = pl.BlockSpec(memory_space=pltpu.VMEM)
    return pl.pallas_call(
        functools.partial(back_factor_kernel, places, len(parts)),
        in_specs=[pl.BlockSpec(memory_space=pltpu.SMEM)]
        + [pl.BlockSpec(memory_space=pltpu.HBM)] * len(arrays)
        + [vmem] * (1 + len(parts)),
        out_specs=[vmem, vmem],
        out_shape=[
            jax.ShapeDtypeStruct((rows.shape[0], depth), jnp.float32),
            jax.ShapeDtypeStruct((gram_width, gram_width), LOW),
        ],
        scratch_shapes=[
            pltpu.VMEM((size, height, width), LOW),
            pltpu.SemaphoreType.DMA((len(arrays),)),
        ],
        compiler_params=pltpu.CompilerParams(vmem_limit_bytes=VMEM_MOST),
        cost_estimate=pl.CostEstimate(
            flops=2 * rows.size * depth + 100 * gram_width**3,
            bytes_accessed=2 * (size * height * width + 3 * rows.size),
            transcendentals=0,
        ),
        name="back_and_factor",
    )(own, *arrays, rows, *parts)


def is_owner(owners):
    me = lax.axis_index("dp")
    own = jnp.zeros((1,), jnp.int32)
    for o in owners:
        own = own + (me == o).astype(jnp.int32)
    return own


def owned_factor(parts, owners):
    return block_factor(is_owner(owners), parts)


def owned_update(moment, weight, choices, owners):
    size = lax.axis_size("dp")
    me = lax.axis_index("dp")
    places = jnp.stack([(me - o) % size for o in owners]).astype(jnp.int32)
    return apply_factors(moment, weight, places, choices)


def shards(
    inputs,
    cotangent,
    lengths,
    w_query,
    w_keyval,
    w_out,
    w_gate_up,
    w_down,
    gains,
    m_query,
    m_keyval,
    m_out,
    m_gate_up,
    m_down,
    m_gains,
):
    batches, own_rows, model_width = inputs.shape
    head_dim = w_keyval.shape[1] // 2
    half_dim = head_dim // 2
    units_here = w_down.shape[1]
    query_cols = w_query.shape[1]
    size = lax.axis_size("mp")
    me = lax.axis_index("mp")
    tokens = batches * own_rows
    seq_len = size * own_rows

    groups = lax.axis_size("dp")
    share = w_keyval.shape[0] // size

    def rows_of(value):
        return lax.all_gather(value, "dp", axis=0, tiled=False)

    gate_up_t = jnp.transpose(w_gate_up, (1, 2, 0))
    down_t = jnp.transpose(w_down)
    cot_rows = cotangent.reshape(tokens, model_width)
    cot = Gather(cot_rows, size)
    cot.first()
    query_block = rows_of(w_query.astype(LOW))
    own_positions = me * own_rows + jnp.arange(own_rows, dtype=jnp.int32)
    key_positions = jnp.concatenate(
        [(me ^ s) * own_rows + jnp.arange(own_rows, dtype=jnp.int32) for s in gather_order(size)]
    )
    qid = []
    kid = []
    offsets = []
    for batch_index in range(batches):
        own_segment, own_offset = doc_layout(lengths[batch_index], own_positions)
        key_segment, unused = doc_layout(lengths[batch_index], key_positions)
        qid.append(jnp.stack([own_segment, own_positions], axis=1))
        kid.append(jnp.stack([key_segment, key_positions], axis=0))
        offsets.append(own_offset)
    qid = jnp.stack(qid)
    kid = jnp.stack(kid)
    cosine, sine = rotary_tables(jnp.stack(offsets), half_dim)
    flat_cos = cosine.reshape(tokens, half_dim)
    flat_sin = sine.reshape(tokens, half_dim)

    x_rows = wide(inputs).reshape(tokens, model_width)
    x_scale = inverse_scale(x_rows)
    normed = (x_rows * x_scale * gains[0]).astype(LOW)
    first_one = "one" if size == 8 else "1"
    cot.parts[first_one], query_block, low_keyval, normed, flat_cos, flat_sin, qid, kid = tie(
        cot.parts[first_one],
        query_block,
        w_keyval.astype(LOW),
        normed,
        flat_cos,
        flat_sin,
        qid,
        kid,
    )
    cot.parts, query_block = tie(cot.parts, query_block)
    full_keyval = rows_of(low_keyval)
    query_gather = Gather(query_block.reshape(model_width, query_cols), size)
    query_gather.first()
    full_keyval, query_gather.parts, low_out = tie(
        full_keyval, query_gather.parts, w_out.astype(LOW)
    )
    query_gather.second()
    out_block = rows_of(low_out)
    full_gate = rows_of(gate_up_t[0].astype(LOW))
    full_up = rows_of(gate_up_t[1].astype(LOW))
    full_down = rows_of(down_t.astype(LOW))
    order = jnp.array(gather_order(size), jnp.int32)
    place = jnp.zeros((size,), jnp.int32).at[order].set(jnp.arange(size, dtype=jnp.int32))
    place = place[me ^ jnp.arange(size)]

    full_keyval = full_keyval.reshape(model_width, 2 * head_dim)
    own_keyval = project(normed, [[(0, full_keyval)]], head_dim, (flat_cos, flat_sin), 1)
    query_gather.parts, own_keyval = tie(query_gather.parts, own_keyval)
    flips = flips_of(size)
    keyval = own_keyval.reshape(1, batches, own_rows, 2 * head_dim)
    for flip in flips:
        keyval = jnp.concatenate([keyval, swap(keyval, flip, size)], axis=0)
        if flip == flips[-2]:
            keyval, cot.parts = tie(keyval, cot.parts)
            cot.relay()
    keyval = jnp.swapaxes(keyval, 0, 1).reshape(batches, seq_len, 2 * head_dim)
    query_gather.relay()
    query_gather.parts, out_block = tie(query_gather.parts, out_block)
    out_gather = Gather(out_block.reshape(model_width, query_cols), size)
    out_gather.first()
    query_gather.third()
    query_pieces = query_gather.pieces()
    queries = project(normed, query_pieces, head_dim, (flat_cos, flat_sin))
    queries = queries.reshape(batches, own_rows, -1)
    done = ()
    for batch in range(batches):
        done = attention_forward(batch, queries, keyval, qid, kid, head_dim, done)
        if batch == 0:
            out_gather.parts, queries, done = tie(out_gather.parts, queries, done)
            out_gather.second()
            out_gather.relay()
    out_gather.parts, done, full_gate, cot.parts = tie(
        out_gather.parts, done, full_gate, cot.parts
    )
    out_gather.third()
    cot.second()
    context, logs = done
    context = context.reshape(tokens, -1)
    out_pieces = out_gather.pieces()
    mid = x_rows + project_back(context, out_pieces, model_width)
    mid_scale = inverse_scale(mid)
    normed_mid_rows = (mid * mid_scale * gains[1]).astype(LOW)
    mid_gather = Gather(normed_mid_rows, size)
    mid_gather.first()
    cot.third()
    full_cot = [in_steps(run, cot.pieces()) for run in range(2)]
    mid_gather.parts, full_cot[1], full_up = tie(mid_gather.parts, full_cot[1], full_up)
    mid_gather.second()
    mid_gather.relay()
    units = [None, None]
    units[1] = hidden_units(1, mid_gather.pieces(), full_gate, full_up)
    mid_gather.parts, units[1] = tie(mid_gather.parts, units[1])
    mid_gather.third()
    units[0] = hidden_units(0, mid_gather.pieces(), full_gate, full_up)
    normed_mid = [unit[0] for unit in units]
    (sum_down,) = units_sum([[unit[4] for unit in units]], full_cot, groups)
    sum_down, units = tie(sum_down, units)
    d_mid_sum = Scatter(size)
    steps = size // 2
    turned = []
    for run in range(2):
        _, gate, upward, _, _ = units[run]
        *grads, evens, odds = hidden_back(
            full_cot[run], gate, upward, full_gate, full_up, full_down, steps
        )
        turned.append(grads)
        if run == 0:
            odds, units = tie(odds, units)
        else:
            d_mid_sum.parts, odds = tie(d_mid_sum.parts, odds)
        d_mid_sum.first(evens, odds)
    turned = d_mid_sum.second(turned)

    def scatter_rows(value):
        return lax.psum_scatter(value, "dp", scatter_dimension=0, tiled=False)

    old_gate_up = jnp.transpose(m_gate_up, (1, 2, 0))
    old_down = jnp.transpose(m_down)
    grad_down = scatter_rows(sum_down)
    sum_gate, sum_up = units_sum(
        [[grads[0] for grads in turned], [grads[1] for grads in turned]], normed_mid, groups
    )
    d_mid_sum.parts, sum_gate, sum_up, grad_down = tie(
        d_mid_sum.parts, sum_gate, sum_up, grad_down
    )
    grad_gate = scatter_rows(sum_gate)
    grad_up = scatter_rows(sum_up)
    hidden = d_mid_sum.third([unit[3] for unit in units])
    mlp_sum = Scatter(size)
    mlp_parts = [hidden_out(part, full_down, steps) for part in hidden]
    d_mid_sum.parts, mlp_parts = tie(d_mid_sum.parts, mlp_parts)
    for evens, odds in mlp_parts:
        mlp_sum.first(evens, odds)
    d_mid_norm = d_mid_sum.total()
    d_mid = wide(cot_rows) + norm_back(d_mid_norm, mid, mid_scale, gains[1])
    gain_mid = jnp.sum(d_mid_norm * mid * mid_scale, axis=0)

    d_mid_low = d_mid.astype(LOW)
    out_sum = Scatter(size)
    out_parts = [blocks_sum(run, d_mid_low, context, size) for run in range(2)]
    mlp_sum.parts, out_parts, d_mid_low = tie(mlp_sum.parts, out_parts, d_mid_low)
    for evens, odds in out_parts:
        out_sum.first(evens, odds)
    d_mid_low = mlp_sum.second(d_mid_low)
    d_context = project(d_mid_low, out_pieces, head_dim).reshape(batches, own_rows, -1)
    out_sum.parts, d_context, grad_gate = tie(out_sum.parts, d_context, grad_gate)
    d_context = out_sum.second(d_context)
    fast = groups == 4 and units_here == 2 * FF_BLOCK
    grad_down = wide(grad_down)
    moment_down = DECAY * old_down + grad_down
    moment_gate = DECAY * old_gate_up[0] + wide(grad_gate)
    first_owners = (0, 1, 2, 3)
    last_owners = (1, 2)
    if fast:
        moment_down, moment_gate, d_context = tie(moment_down, moment_gate, d_context)
        slots = ((0, 0, 1), (0, 1, 2), (1, 0, 0), (1, 1, 3))
        first_parts = packed_grams((moment_down, moment_gate), FF_BLOCK, slots, groups)
        first_parts = lax.all_to_all(first_parts, "dp", 0, 0, tiled=True)
    backs = ()
    for batch in range(batches):
        backs = attention_backward(
            batch, queries, d_context, logs, keyval, qid, kid, cosine, sine, head_dim, backs
        )
        if batch == 0:
            backs, mlp_sum.parts, d_context = tie(backs, mlp_sum.parts, d_context)
            d_context = mlp_sum.third(d_context)
    if fast:
        backs, first_parts = tie(backs, first_parts)
    backs, out_sum.parts, grad_up = tie(backs, out_sum.parts, grad_up)
    d_queries, d_keyval = out_sum.third(backs)
    d_queries = d_queries.reshape(tokens, -1)

    def own_rows_of(total, width):
        return scatter_rows(total.astype(LOW).reshape(groups, -1, width))

    query_sum = Scatter(size)
    query_parts = [blocks_sum(run, normed, d_queries, size) for run in range(2)]
    for evens, odds in query_parts:
        query_sum.first(evens, odds)
    d_keyval = d_keyval.reshape(batches, size, own_rows, 2 * head_dim)
    d_keyval = jnp.swapaxes(d_keyval, 0, 1)[place]
    d_keyval = lax.all_to_all(d_keyval, "mp", 0, 0, tiled=True)
    output = (mid + mlp_sum.total()).astype(LOW).reshape(inputs.shape)
    moment_up = DECAY * old_gate_up[1] + wide(grad_up)
    own = is_owner(first_owners)
    query_parts, own, moment_up = tie(query_parts, own, moment_up)
    if fast:
        up_grams = packed_grams((moment_up,), FF_BLOCK, ((0, 0, 0), (0, 1, 1)), 2)
        query_sum.parts, up_grams, own = tie(query_sum.parts, up_grams, own)
        last_parts = exchange((up_grams[0], up_grams[1]), last_owners)
    out_sum.parts, own = tie(out_sum.parts, own)
    grad_out = own_rows_of(out_sum.total(), query_cols)
    if fast:
        own = query_sum.second(own)
        d_normed, first_factor = back_and_factor(
            d_queries, query_pieces, model_width, own, [first_parts]
        )
    else:
        d_queries = query_sum.second(d_queries)
        d_normed = project_back(d_queries, query_pieces, model_width)
    d_keyval, d_normed, query_sum.parts = tie(d_keyval, d_normed, query_sum.parts)
    d_normed = query_sum.third(d_normed)
    if fast:
        first_choices = share_out(first_factor, first_owners)
    d_keyval = jnp.sum(wide(d_keyval), axis=0).reshape(tokens, 2 * head_dim)
    d_keyval = jnp.concatenate(
        [rotate(d_keyval[:, :head_dim], flat_cos, -flat_sin), d_keyval[:, head_dim:]], axis=1
    ).astype(LOW)
    sum_keyval = outer_sum(normed, d_keyval).astype(LOW)
    sum_keyval = jnp.swapaxes(sum_keyval.reshape(groups, size, share, 2 * head_dim), 0, 1)
    sum_keyval = lax.all_to_all(sum_keyval, "mp", 0, 0, tiled=True)
    if fast:
        last_parts, d_keyval = tie(last_parts, d_keyval)
        last_factor = owned_factor(last_parts, last_owners)
        query_sum.parts, last_factor, d_normed, first_choices[1] = tie(
            query_sum.parts, last_factor, d_normed, first_choices[1]
        )
        last_choices = share_out(last_factor, last_owners)
    grad_query = own_rows_of(query_sum.total(), query_cols)
    d_normed = d_normed + rows_dot(d_keyval, full_keyval)
    input_grad = (d_mid + norm_back(d_normed, x_rows, x_scale, gains[0])).astype(LOW)
    input_grad = input_grad.reshape(inputs.shape)
    gain_input = jnp.sum(d_normed * x_rows * x_scale, axis=0)
    share_sums = jnp.sum(wide(sum_keyval), axis=0).astype(LOW)
    share_sums, input_grad = tie(share_sums, input_grad)
    gain_rows = as_rows(jnp.stack([gain_input, gain_mid], axis=0), 2 * head_dim)
    gain_rows = jnp.broadcast_to(gain_rows[None], (groups,) + gain_rows.shape)
    share_parts = jnp.concatenate([share_sums, gain_rows], axis=1)
    share_parts = lax.all_to_all(share_parts, "dp", 0, 0, tiled=True)
    grad_out = wide(grad_out)
    moment_out = DECAY * m_out + grad_out
    out_grams = gather_grams(moment_out, head_dim, False)
    if fast:
        new_down = owned_update(moment_down, down_t, first_choices, (1, 2))
        new_gate = owned_update(moment_gate, gate_up_t[0], first_choices, (0, 3))
    else:
        new_down = small_update(moment_down, down_t, FF_BLOCK, True)
        new_gate = small_update(moment_gate, gate_up_t[0], FF_BLOCK, True)
    share_parts, new_down = tie(share_parts, new_down)
    grad_keyval = jnp.sum(wide(share_parts), axis=0)
    gain_rows = as_rows(from_rows(grad_keyval[share:]), 2 * head_dim)
    grad_keyval = jnp.concatenate([grad_keyval[:share].astype(LOW), gain_rows], axis=0)
    grad_keyval = lax.all_gather(grad_keyval, "mp", axis=0, tiled=False)
    if fast:
        new_up = owned_update(moment_up, gate_up_t[1], last_choices, last_owners)
    else:
        new_up = small_update(moment_up, gate_up_t[1], FF_BLOCK, True)
    new_out = small_update(moment_out, w_out, head_dim, False, out_grams)
    grad_keyval, new_out, new_up = tie(grad_keyval, new_out, new_up)
    grad_keyval = wide(grad_keyval)
    grad_gains = from_rows(jnp.sum(grad_keyval[:, share:], axis=0)).reshape(gains.shape)
    grad_keyval = grad_keyval[:, :share].reshape(w_keyval.shape)
    moment_keyval = DECAY * m_keyval + grad_keyval
    keyval_grams = gather_grams(moment_keyval, 2 * head_dim, False)
    grad_query = wide(grad_query)
    moment_query = DECAY * m_query + grad_query
    query_grams = gather_grams(moment_query, head_dim, False)
    new_keyval, new_query = small_updates(
        [
            (moment_keyval, w_keyval, 2 * head_dim, False, keyval_grams),
            (moment_query, w_query, head_dim, False, query_grams),
        ]
    )
    grad_gate_up = wide(jnp.stack([grad_gate, grad_up]))
    moment_gate_up = DECAY * old_gate_up + grad_gate_up
    new_gate_up = jnp.stack([new_gate, new_up])

    def back(value):
        return jnp.transpose(value, (2, 0, 1))

    moment_gains = DECAY * m_gains + grad_gains
    new_gains = gains - GAIN_RATE * moment_gains
    return (
        output,
        input_grad,
        grad_query,
        grad_keyval,
        grad_out,
        back(grad_gate_up),
        jnp.transpose(grad_down),
        grad_gains,
        moment_query,
        moment_keyval,
        moment_out,
        back(moment_gate_up),
        jnp.transpose(moment_down),
        moment_gains,
        new_query,
        new_keyval,
        new_out,
        back(new_gate_up),
        jnp.transpose(new_down),
        new_gains,
    )


def solution(mesh):
    rows = P("dp", None)
    both = P("dp", "mp")
    tokens = P("dp", "mp", None)
    gate_up = P("dp", None, "mp")
    weights = (both, rows, both, gate_up, both, P())
    return jax.shard_map(
        shards,
        mesh=mesh,
        in_specs=(tokens, tokens, rows) + weights + weights,
        out_specs=(tokens, tokens) + weights + weights + weights,
        check_vma=False,
    )
```
